128 devices in a mesh: prow: 16 (over y_hi, z, core), pcol: 8 (over x, y_lo).
Axes of the slice: x: 4, y: 4 (y_hi: 2, y_lo: 2; y = y_hi * 2 + y_lo), z: 4, core: 2. Of those that a mesh axis runs over, the one named last changes fastest.
Arguments:
- prior: float32 [32, 256, 32, 256], P('prow', None, 'pcol'), may hold values from -1 to 6, as said below
- lfac: float32 [32, 256, 32, 256], P('prow', None, 'pcol'), may hold values from -0.03125 to 0.03125
- tile_mask: int32 [32, 32], replicated, may hold values 0 or 1
- dinv: float32 [4, 256, 256], replicated, may hold values from -1 to 4, as said below
Outputs:
- inverse: float32 [32, 256, 32, 256], P('prow', None, 'pcol')
The draws below stay inside these ranges and needn't reach their ends.
Inputs may be any that keep to these rules, and one draw needn't show every extreme that they name: `prior`: symmetric as a 8192 x 8192 matrix in global order. `dinv`: each block is symmetric.
All inputs are finite; a program needn't handle non-finite values.
Results may differ from the reference program's by a relative error of at most 0.0001.
Values sent between devices are 32-bit elements; how exact they have to be, the bound alone decides.
A program may use at most 64 MiB of HBM per device.

```python
import jax
import jax.numpy as jnp
from jax import lax

B = 256
NT = 32
S = 4
TR = 2
TC = 4
N_PROW = 16
N_PCOL = 8


def symmetric_tiles(key, count, width, off_scale, diag_lo, diag_hi, row_lo, row_hi):
    first, second, third = jax.random.split(key, 3)
    base = jnp.clip(jax.random.normal(first, (count, width, width), jnp.float32), -6.0, 6.0) * off_scale
    mixed = base + jnp.swapaxes(base, 1, 2)
    diag_vals = jnp.exp(jax.random.uniform(second, (count, width), jnp.float32, jnp.log(diag_lo), jnp.log(diag_hi)))
    eye = jnp.eye(width, dtype=jnp.float32)
    whole = mixed + eye[None] * diag_vals[:, :, None]
    scales = jnp.exp(jax.random.uniform(third, (count, width), jnp.float32, jnp.log(row_lo), jnp.log(row_hi)))
    return whole * scales[:, :, None] * scales[:, None, :]


def draw_prior(key, part):
    key = jax.random.fold_in(key, 11)
    order = NT * B
    whole = symmetric_tiles(key, 1, order, 0.35 / order ** 0.5, 1.0, 3.0, 1.0, 1.0)[0]
    tiles = whole.reshape(NT, B, NT, B)
    index = jnp.arange(NT, dtype=jnp.int32)
    back_row = index % TR * (NT // TR) + index // TR
    back_col = index % TC * (NT // TC) + index // TC
    return tiles[back_row][:, :, back_col]


def draw_dinv(key, part):
    key = jax.random.fold_in(key, 23)
    return symmetric_tiles(key, S, B, 0.3 / B ** 0.5, 0.5, 2.0, 1.0, 1.0)


def with_ends(array, rng, least, high):
    dims = array.shape
    index_at = [jax.random.randint(jax.random.fold_in(rng, axis), (), 0, dims[axis]) for axis in range(len(dims))]
    array = array.at[tuple(index_at)].set(least)
    longest = dims.index(max(dims))
    index_at[longest] = (index_at[longest] + 1) % dims[longest]
    return array.at[tuple(index_at)].set(high)


def level_of(own_key, shape, cuts, smallest, top_value):
    loudness, own = 1.0, jax.random.fold_in(own_key, 6)
    for dim, blocks in cuts:
        steps = jnp.exp(jax.random.uniform(jax.random.fold_in(own, dim), (blocks,), jnp.float32, smallest / len(cuts), top_value / len(cuts)))
        loudness = loudness * jnp.repeat(steps, shape[dim] // blocks).reshape([-1 if axis == dim else 1 for axis in range(len(shape))])
    return loudness


def normal_values(key, dims, scale, limit, shards=(), kind=jnp.bfloat16):
    drawn = scale * jax.random.normal(key, dims, jnp.float32)
    if shards:
        drawn = drawn * level_of(key, dims, shards, -0.22, 0.18)
    return jnp.clip(drawn, -limit, limit).astype(kind)


def setup_inputs(seed: int = 0) -> dict:
    key_of = jax.random.split(jax.random.key(seed), 5)
    prior = draw_prior(jax.random.fold_in(key_of[4], 71), 0)
    lfac = normal_values(key_of[1], (NT, B, NT, B), (4 * NT * B) ** -0.5, 0.03125, ((0, 16), (2, 8)), jnp.float32)
    tile_mask = with_ends((jax.random.randint(key_of[2], (NT, NT), 0, 4) < 3).astype(jnp.int32), jax.random.fold_in(key_of[2], 1), 0, 1)
    dinv = draw_dinv(jax.random.fold_in(key_of[4], 71), 0)
    return dict(prior=prior, lfac=lfac, tile_mask=tile_mask, dinv=dinv)


def reference(prior, lfac, tile_mask, dinv):
    rows_n = N_PROW
    cols_n = N_PCOL
    tile_rows = NT // rows_n
    tile_cols = NT // cols_n
    index = jnp.arange(NT, dtype=jnp.int32)
    to_row = ((index % rows_n) * tile_rows + index // rows_n).astype(jnp.int32)
    to_col = ((index % cols_n) * tile_cols + index // cols_n).astype(jnp.int32)
    back_row = ((index % tile_rows) * rows_n + index // tile_rows).astype(jnp.int32)
    back_col = ((index % tile_cols) * cols_n + index // tile_cols).astype(jnp.int32)
    order = NT * B
    full = prior[to_row][:, :, to_col].reshape(order, order)
    lower = lfac[to_row][:, :, to_col]
    keep = (tile_mask * (index[:, None] > index[None, :]).astype(jnp.int32)).astype(jnp.float32)
    lower = (lower * keep[:, None, :, None]).reshape(order, order)
    for k in range(S - 1, -1, -1):
        first = k * B
        after = (k + 1) * B
        panel = lower[after:, first:after]
        block = -jnp.dot(full[after:, after:], panel, precision=lax.Precision.HIGHEST,
                         preferred_element_type=jnp.float32)
        diag = dinv[k] - jnp.dot(panel.T, block, precision=lax.Precision.HIGHEST,
                                 preferred_element_type=jnp.float32)
        full = full.at[after:, first:after].set(block)
        full = full.at[first:after, after:].set(block.T)
        full = full.at[first:after, first:after].set(diag)
    return full.reshape(NT, B, NT, B)[back_row][:, :, back_col]
```

```python
import jax
import jax.numpy as jnp
from jax import lax
from jax.experimental import pallas as pl
from jax.experimental.pallas import tpu as pltpu
from jax.sharding import PartitionSpec as P

B = 256
S = 4
F32 = jnp.float32
BF16 = jnp.bfloat16
MESH = pl.DeviceIdType.MESH
LOW = [(1, 0), (2, 0), (2, 1), (3, 0), (3, 1), (3, 2)]
CORE_OF = {1: 1, 2: 0, 3: 1}


def split(value):
    hi = value.astype(BF16)
    lo = (value - hi.astype(F32)).astype(BF16)
    return hi, lo


def dot3(a, b, dims=((1,), (0,))):
    def one(left, right):
        return lax.dot_general(left, right, (dims, ((), ())), preferred_element_type=F32)

    return one(a[0], b[0]) + (one(a[0], b[1]) + one(a[1], b[0]))


def kernel(prior, lfac, mask, dinv, out,
           g32, gh, gl, lt32, pt, ph, plo, lt, ut, cr, op, om, rm, rp, yr, xt, xa, xb, xo, xh, xl,
           zp, zc, zr, zs, zf, mt, dv, zo,
           g_sem, l_sem, d_sem, o_sem, w_sem,
           s_out, r_out, s_x, r_x, s_y, r_y,
           s_l, r_l, s_c, r_c, s_zo, r_zo, s_zr, r_zr, s_yh, r_yh,
           s_xa, r_xa, s_xb, r_xb, s_zc, r_zc, s_zd, r_zd, s_zf, r_zf):
    row = lax.axis_index("prow")
    col = lax.axis_index("pcol")
    yh, z, core = row // 8, (row // 2) % 4, row % 2
    x, yl = col // 2, col % 2
    quad = row // 2

    def at(r=None, c=None):
        return {"prow": row if r is None else r, "pcol": col if c is None else c}

    def remote(src, dst, ssem, rsem, where):
        return pltpu.make_async_remote_copy(
            src_ref=src, dst_ref=dst, send_sem=ssem, recv_sem=rsem, device_id=where, device_id_type=MESH)

    c_x = (x + 1 - 2 * (x % 2)) * 2 + yl
    c_y = x * 2 + 1 - yl
    c_o = (3 - x) * 2 + yl
    r_core = row + 1 - 2 * core
    r_zp = yh * 8 + ((z + 1) % 4) * 2 + core
    r_zm = yh * 8 + ((z + 3) % 4) * 2 + core
    r_y2 = (row + 8) % 16
    b_row, b_col = col + 8 * yh, z
    b_self = (b_row == row) & (b_col == col)
    a_self = z == row

    loads = []
    for a in range(2):
        for b in range(4):
            loads.append(pltpu.make_async_copy(prior.at[a, :, b, :], g32.at[b, pl.ds(a * B, B), :], g_sem.at[a, b]))
    keep = pltpu.make_async_copy(prior, out, o_sem)
    ltile = [pltpu.make_async_copy(lfac.at[a, :, 0, :], lt32.at[a], l_sem.at[a]) for a in range(2)]
    dload = pltpu.make_async_copy(dinv, dv, d_sem)

    @pl.when(col < S)
    def _():
        for copy in ltile:
            copy.start()
    for copy in loads:
        copy.start()
    dload.start()
    keep.start()

    barrier = pltpu.get_barrier_semaphore()

    def greet(where):
        pl.semaphore_signal(barrier, inc=1, device_id=where, device_id_type=MESH)

    for step in range(1, 16):
        greet(at(r=(row + step) % 16))
    for c in (c_x, c_y, c_o):
        greet(at(c=c))
    greet(at(r=r_y2, c=c_y))

    def b_source(a):
        return (row // 8) * 8 + col * 2 + a, row % 8

    for a in range(2):
        sr, sc = b_source(a)

        @pl.when((col < S) & jnp.logical_not((sr == row) & (sc == col)))
        def _():
            greet(at(r=sr, c=sc))

    @pl.when(col < S)
    def _():
        for a in range(2):
            ltile[a].wait()
            live = mask[row + 16 * a, col] * (row + 16 * a > col).astype(jnp.int32)
            pt[col, a] = lt32[a].T * live.astype(F32)

    pl.semaphore_wait(barrier, 19 + jnp.where(b_self, 0, 1))

    near = jnp.where((x == 0) | (x == 3), 0, 1)
    k_p, k_s = 2 * near + yl, 2 * (1 - near) + yl
    k_pd, k_sd = 2 * near + 1 - yl, 2 * (1 - near) + 1 - yl

    c_out = [remote(pt.at[k_p, a], pt.at[k_p, a], s_out.at[a], r_out.at[a], at(c=c_o)) for a in range(2)]
    c_xs = [remote(pt.at[k_p, a], pt.at[k_p, a], s_x.at[a], r_x.at[a], at(c=c_x)) for a in range(2)]
    c_ys = [remote(pt.at[k_p, a], pt.at[k_p, a], s_y.at[a], r_y.at[a], at(c=c_y)) for a in range(2)]
    c_xd = remote(pt.at[k_pd, 0], pt.at[k_pd, 0], s_x.at[2], r_x.at[2], at(c=c_x))
    c_yd = remote(pt.at[k_s, 1], pt.at[k_s, 1], s_y.at[2], r_y.at[2], at(c=c_y))
    w_xs = [remote(pt.at[k_s, a], pt.at[k_s, a], s_x.at[a], r_x.at[a], at(c=c_x)) for a in range(2)]
    w_ys = [remote(pt.at[k_pd, a], pt.at[k_pd, a], s_y.at[a], r_y.at[a], at(c=c_y)) for a in range(2)]
    w_xd = remote(pt.at[k_sd, 0], pt.at[k_sd, 0], s_x.at[2], r_x.at[2], at(c=c_x))
    w_yd = remote(pt.at[k_sd, 1], pt.at[k_sd, 1], s_y.at[2], r_y.at[2], at(c=c_y))

    for a in range(2):
        @pl.when(x < 2)
        def _():
            c_out[a].start()

        @pl.when(x >= 2)
        def _():
            c_out[a].wait_recv()
        c_xs[a].start()
        c_ys[a].start()

    for a in range(2):
        for b in range(4):
            loads[a * 4 + b].wait()
    for b in range(4):
        hi, lo = split(g32[b])
        gh[b] = hi
        gl[b] = lo

    w_ys[0].wait_recv()
    c_xd.start()
    w_xs[0].wait_recv()
    w_xs[1].wait_recv()
    c_yd.start()
    w_ys[1].wait_recv()
    w_xd.wait_recv()
    w_yd.wait_recv()

    def l_copy(u, slot, where):
        return remote(lt.at[u], lt.at[u], s_l.at[u, slot], r_l.at[u], where)

    def l_wait(u):
        l_copy(u, 0, at(r=r_core)).wait_recv()

    def l_routes(u, j):
        routes = [(row >= 0, l_copy(u, 0, at(r=r_core))), (yh == 0, l_copy(u, 1, at(r=r_y2, c=c_y)))]
        if j == 1:
            routes.append((row == 1, l_copy(u, 2, at(r=r_zp))))
            routes.append(((row == 1) | (row == 7), l_copy(u, 3, at(r=r_zm))))
        else:
            routes.append(((row == j) | (row == j + 2), l_copy(u, 2, at(r=r_zp))))
            routes.append((row == j, l_copy(u, 3, at(r=r_zm))))
        return routes

    order = {0: [(2, 1), (2, 0)], 1: [(3, 2), (3, 1), (1, 0), (3, 0)]}
    for own in range(2):
        @pl.when(core == own)
        def _():
            for j, k in order[own]:
                u = LOW.index((j, k))

                @pl.when(row == j)
                def _():
                    lt[u] = pt[k, 0]

                @pl.when(row != j)
                def _():
                    l_wait(u)
                for cond, copy in l_routes(u, j):
                    @pl.when(cond)
                    def _():
                        copy.start()

    zero = jnp.where(row < S, 0.0, 1.0).astype(F32)
    c_core = []
    for k in (3, 2, 1, 0):
        acc = jnp.concatenate([pt[k, 0] * zero, pt[k, 1]], axis=1)
        for j in range(k + 1, S):
            u = LOW.index((j, k))

            @pl.when(core != CORE_OF[j])
            def _():
                l_wait(u)
            acc = acc - dot3(split(lt[u]), (ph[j], plo[j]))
        hi, lo = split(acc)
        ph[k] = hi
        plo[k] = lo

        @pl.loop(0, 4)
        def _(t):
            ut[k, t] = dot3((ph[k], plo[k]), (gh[t], gl[t]))
        copy = remote(ut.at[k, pl.ds(2 - 2 * core, 2)], cr.at[k], s_c.at[k], r_c.at[k], at(r=r_core))
        copy.start()
        c_core.append(copy)

    c_opp = [remote(ut.at[(z + 2) % 4, 2 * core], op, s_zo.at[0], r_zo.at[0], at(r=r_zp)),
             remote(ut.at[(z + 2) % 4, 2 * core + 1], om, s_zo.at[1], r_zo.at[1], at(r=r_zm))]
    c_rm = [remote(ut.at[(z + 1) % 4, 2 * core + u], rm.at[u], s_zr.at[u], r_zr.at[u], at(r=r_zp)) for u in range(2)]
    c_rp = [remote(ut.at[(z + 3) % 4, 2 * core + u], rp.at[u], s_zr.at[2 + u], r_zr.at[2 + u], at(r=r_zm))
            for u in range(2)]
    for n, k in enumerate((3, 2, 1, 0)):
        c_core[n].wait_recv()
        for u in range(2):
            ut[k, 2 * core + u] = ut[k, 2 * core + u] + cr[k, u]
        rel = (k - z + 4) % 4

        @pl.when(rel == 2)
        def _():
            c_opp[0].start()
            c_opp[1].start()

        @pl.when(rel == 1)
        def _():
            c_rm[1].start()

        @pl.when(rel == 3)
        def _():
            c_rp[0].start()
    c_opp[0].wait_recv()
    ut[(z + 1) % 4, 2 * core] = ut[(z + 1) % 4, 2 * core] + op[...]
    c_rm[0].start()
    c_opp[1].wait_recv()
    ut[(z + 3) % 4, 2 * core + 1] = ut[(z + 3) % 4, 2 * core + 1] + om[...]
    c_rp[1].start()
    for u in (1, 0):
        c_rm[u].wait_recv()
    for u in (0, 1):
        c_rp[u].wait_recv()
    away = 1 - yh
    ut[z, 2 * core + away] = ut[z, 2 * core + away] + (rm[away] + rp[away])
    c_yh = remote(ut.at[z, 2 * core + away], yr, s_yh, r_yh, at(r=r_y2))
    c_yh.start()
    mine = ut[z, 2 * core + yh] + (rm[yh] + rp[yh])
    c_yh.wait_recv()
    xt[...] = -(mine + yr[...])

    t_own = 2 * core + yh
    c_xa = remote(xt, xa.at[t_own], s_xa, r_xa.at[t_own], at(r=z))
    c_xb = remote(xt, xb.at[core], s_xb, r_xb.at[core], at(r=b_row, c=b_col))

    @pl.when(jnp.logical_not(b_self))
    def _():
        c_xb.start()

    @pl.when(b_self)
    def _():
        xb[core] = xt[...]

    @pl.when(jnp.logical_not(a_self))
    def _():
        c_xa.start()

    @pl.when(a_self)
    def _():
        xa[t_own] = xt[...]

    dload.wait()

    @pl.when((row < S) & (col < S))
    def _():
        ones = (lax.broadcasted_iota(jnp.int32, (B, B), 0) == lax.broadcasted_iota(jnp.int32, (B, B), 1))
        for k in range(S):
            for m in range(S):
                if m < k:
                    mt[k, m] = jnp.zeros((B, B), F32)
                elif m == k:
                    mt[k, m] = ones.astype(F32)
                else:
                    acc = lt[LOW.index((m, k))]
                    for j in range(k + 1, m):
                        acc = acc + dot3(split(mt[k, j]), split(lt[LOW.index((m, j))]))
                    mt[k, m] = -acc
        zo[...] = jnp.zeros((B, B), F32)
        for m in range(S):
            half = dot3(split(mt[row, m]), split(dv[m]))
            zo[...] = zo[...] + dot3(split(half), split(mt[col, m]), ((1,), (1,)))

    c_zc = remote(zp.at[1 - core], zc, s_zc, r_zc, at(r=r_core))
    c_zd = [remote(zp.at[core, :, pl.ds(((quad + d) % 8) * 32, 32), :], zr.at[d - 1], s_zd.at[d - 1], r_zd.at[d - 1],
                   at(r=((quad + d) % 8) * 2 + core)) for d in range(1, 8)]
    c_zf = [remote(zs.at[m], zf.at[pl.ds(quad * 32, 32), :], s_zf.at[m], r_zf.at[quad], at(r=2 * m + core))
            for m in range(2)]

    @pl.when(col < S)
    def _():
        for a in range(2):
            sr, sc = b_source(a)

            @pl.when(jnp.logical_not((sr == row) & (sc == col)))
            def _():
                remote(xt, xb.at[a], s_xb, r_xb.at[a], at(r=b_row, c=b_col)).wait_recv()
            xo[a] = xb[a].T
            hi, lo = split(xo[a])
            xh[pl.ds(a * B, B), :] = hi
            xl[pl.ds(a * B, B), :] = lo
        for l in range(S):
            zp[l % 2, l // 2] = dot3((ph[l], plo[l]), (xh[...], xl[...]))
        c_zc.start()
        c_zc.wait_recv()
        zp[core] = zp[core] + zc[...]
        for copy in c_zd:
            copy.start()
        acc = zp[core, :, pl.ds(quad * 32, 32), :]
        for d in range(7):
            c_zd[d].wait_recv()
            acc = acc + zr[d]
        zs[...] = acc
        for m in range(2):
            @pl.when(quad != m)
            def _():
                c_zf[m].start()

            @pl.when(quad == m)
            def _():
                zf[pl.ds(quad * 32, 32), :] = zs[m]

        @pl.when(row < S)
        def _():
            for q in range(8):
                @pl.when(quad != q)
                def _():
                    remote(zs.at[0], zf.at[pl.ds(q * 32, 32), :], s_zf.at[0], r_zf.at[q], at(r=r_core)).wait_recv()
            zo[...] = zo[...] - zf[...]

    keep.wait()
    w_row = [pltpu.make_async_copy(xa.at[t], out.at[0, :, t, :], w_sem.at[t]) for t in range(4)]
    w_col = [pltpu.make_async_copy(xo.at[a], out.at[a, :, 0, :], w_sem.at[4 + a]) for a in range(2)]
    w_dia = pltpu.make_async_copy(zo, out.at[0, :, 0, :], w_sem.at[6])
    writes = [((row < S) & (col >= S), w_row[0])] + [(row < S, w_row[t]) for t in range(1, 4)]
    writes += [((col < S) & (row >= S), w_col[0]), (col < S, w_col[1]), ((row < S) & (col < S), w_dia)]

    @pl.when(row < S)
    def _():
        for t in range(4):
            @pl.when(jnp.logical_not(a_self & (t_own == t)))
            def _():
                remote(xt, xa.at[t], s_xa, r_xa.at[t], at(r=r_core)).wait_recv()
    for cond, copy in writes:
        @pl.when(cond)
        def _():
            copy.start()

    @pl.when(x < 2)
    def _():
        for copy in c_out:
            copy.wait_send()
    for copy in c_xs + c_ys + [c_xd, c_yd] + c_core + c_opp + c_rm + c_rp + [c_yh]:
        copy.wait_send()
    for own in range(2):
        @pl.when(core == own)
        def _():
            for j, k in order[own]:
                for cond, copy in l_routes(LOW.index((j, k)), j):
                    @pl.when(cond)
                    def _():
                        copy.wait_send()

    @pl.when(jnp.logical_not(b_self))
    def _():
        c_xb.wait_send()

    @pl.when(jnp.logical_not(a_self))
    def _():
        c_xa.wait_send()

    @pl.when(col < S)
    def _():
        c_zc.wait_send()
        for copy in c_zd:
            copy.wait_send()
        for m in range(2):
            @pl.when(quad != m)
            def _():
                c_zf[m].wait_send()
    for cond, copy in writes:
        @pl.when(cond)
        def _():
            copy.wait()


def body(prior, lfac, tile_mask, dinv):
    def vmem(*shape, kind=F32):
        return pltpu.VMEM(shape, kind)

    dma = pltpu.SemaphoreType.DMA
    scratch = [
        vmem(4, 2 * B, B), vmem(4, 2 * B, B, kind=BF16), vmem(4, 2 * B, B, kind=BF16),
        vmem(2, B, B), vmem(4, 2, B, B), vmem(4, B, 2 * B, kind=BF16), vmem(4, B, 2 * B, kind=BF16),
        vmem(6, B, B), vmem(4, 4, B, B), vmem(4, 2, B, B),
        vmem(B, B), vmem(B, B), vmem(2, B, B), vmem(2, B, B), vmem(B, B),
        vmem(B, B), vmem(4, B, B), vmem(2, B, B), vmem(2, B, B),
        vmem(2 * B, B, kind=BF16), vmem(2 * B, B, kind=BF16),
        vmem(2, 2, B, B), vmem(2, B, B), vmem(7, 2, 32, B), vmem(2, 32, B), vmem(B, B),
        vmem(4, 4, B, B), vmem(4, B, B), vmem(B, B),
        dma((2, 4)), dma((2,)), dma, dma, dma((7,)),
        dma((2,)), dma((2,)), dma((3,)), dma((3,)), dma((3,)), dma((3,)),
        dma((6, 4)), dma((6,)), dma((4,)), dma((4,)), dma((2,)), dma((2,)), dma((4,)), dma((4,)), dma, dma,
        dma, dma((4,)), dma, dma((2,)), dma, dma, dma((7,)), dma((7,)), dma((2,)), dma((8,)),
    ]
    return pl.pallas_call(
        kernel,
        out_shape=jax.ShapeDtypeStruct(prior.shape, F32),
        in_specs=[pl.BlockSpec(memory_space=pl.ANY), pl.BlockSpec(memory_space=pl.ANY),
                  pl.BlockSpec(memory_space=pltpu.SMEM), pl.BlockSpec(memory_space=pl.ANY)],
        out_specs=pl.BlockSpec(memory_space=pl.ANY),
        scratch_shapes=scratch,
        compiler_params=pltpu.CompilerParams(
            collective_id=0, has_side_effects=True, vmem_limit_bytes=56 * 1024 * 1024),
    )(prior, lfac, tile_mask, dinv)


def solution(mesh):
    placed = (P("prow", None, "pcol", None), P("prow", None, "pcol", None), P(), P())
    return jax.shard_map(
        body, mesh=mesh, in_specs=placed, out_specs=P("prow", None, "pcol", None), check_vma=False
    )
```

```python
import jax
import jax.numpy as jnp
from jax import lax
from jax.experimental import pallas as pl
from jax.experimental.pallas import tpu as pltpu
from jax.sharding import PartitionSpec as P

B = 256
S = 4
F32 = jnp.float32
BF16 = jnp.bfloat16
MESH = pl.DeviceIdType.MESH
LOW = [(1, 0), (2, 0), (2, 1), (3, 0), (3, 1), (3, 2)]
CORE_OF = {1: 1, 2: 0, 3: 1}


def split(value):
    hi = value.astype(BF16)
    lo = (value - hi.astype(F32)).astype(BF16)
    return hi, lo


def dot3(a, b, dims=((1,), (0,))):
    def one(left, right):
        return lax.dot_general(left, right, (dims, ((), ())), preferred_element_type=F32)

    return one(a[0], b[0]) + (one(a[0], b[1]) + one(a[1], b[0]))


def kernel(prior, lfac, mask, dinv, out,
           g32, gh, gl, lt32, pt, ph, plo, lt, ut, cr, op, om, rm, rp, yr, xt, xa, xb, xo, xh, xl,
           zp, zc, zr, zs, zf, mt, dv, zo,
           g_sem, l_sem, d_sem, o_sem, w_sem,
           s_out, r_out, s_x, r_x, s_y, r_y,
           s_l, r_l, s_c, r_c, s_zo, r_zo, s_zr, r_zr, s_yh, r_yh,
           s_xa, r_xa, s_xb, r_xb, s_zc, r_zc, s_zd, r_zd, s_zf, r_zf):
    row = lax.axis_index("prow")
    col = lax.axis_index("pcol")
    yh, z, core = row // 8, (row // 2) % 4, row % 2
    x, yl = col // 2, col % 2
    quad = row // 2

    def at(r=None, c=None):
        return {"prow": row if r is None else r, "pcol": col if c is None else c}

    def remote(src, dst, ssem, rsem, where):
        return pltpu.make_async_remote_copy(
            src_ref=src, dst_ref=dst, send_sem=ssem, recv_sem=rsem, device_id=where, device_id_type=MESH)

    c_x = (x + 1 - 2 * (x % 2)) * 2 + yl
    c_y = x * 2 + 1 - yl
    c_o = (3 - x) * 2 + yl
    r_core = row + 1 - 2 * core
    r_zp = yh * 8 + ((z + 1) % 4) * 2 + core
    r_zm = yh * 8 + ((z + 3) % 4) * 2 + core
    r_y2 = (row + 8) % 16
    b_row, b_col = col + 8 * yh, (z - x + 4) % 4
    b_self = (b_row == row) & (b_col == col)
    a_self = row == b_col

    loads = []
    for a in range(2):
        for b in range(4):
            loads.append(pltpu.make_async_copy(prior.at[a, :, b, :], g32.at[b, pl.ds(a * B, B), :], g_sem.at[a, b]))
    keeps = []
    for a in range(2):
        for b in range(4):
            stays = row >= 0
            if a == 0:
                stays = stays & (row >= S)
            if b == 0:
                stays = stays & (col >= S)
            keeps.append((stays, pltpu.make_async_copy(
                g32.at[b, pl.ds(a * B, B), :], out.at[a, :, b, :], o_sem.at[a, b])))
    ltile = [pltpu.make_async_copy(lfac.at[a, :, 0, :], lt32.at[a], l_sem.at[a]) for a in range(2)]
    dload = pltpu.make_async_copy(dinv, dv, d_sem)

    @pl.when(col < S)
    def _():
        for copy in ltile:
            copy.start()
    for copy in loads:
        copy.start()
    dload.start()

    barrier = pltpu.get_barrier_semaphore()

    def greet(where):
        pl.semaphore_signal(barrier, inc=1, device_id=where, device_id_type=MESH)

    for step in range(1, 16):
        greet(at(r=(row + step) % 16))
    for c in (c_x, c_y, c_o):
        greet(at(c=c))
    greet(at(r=r_y2, c=c_y))

    def b_source(a):
        return yh * 8 + (z + col) % 4 * 2 + a, row % 8

    for a in range(2):
        sr, sc = b_source(a)

        @pl.when((col < S) & jnp.logical_not((sr == row) & (sc == col)))
        def _():
            greet(at(r=sr, c=sc))

    @pl.when(col < S)
    def _():
        for a in range(2):
            ltile[a].wait()
            live = mask[row + 16 * a, col] * (row + 16 * a > col).astype(jnp.int32)
            turned = lt32[a].T * live.astype(F32)
            pt[col, 2 * a] = turned[:B // 2]
            pt[col, 2 * a + 1] = turned[B // 2:]

    pl.semaphore_wait(barrier, 19 + jnp.where(b_self, 0, 1))

    near = jnp.where((x == 0) | (x == 3), 0, 1)
    k_p, k_s = 2 * near + yl, 2 * (1 - near) + yl
    k_pd, k_sd = 2 * near + 1 - yl, 2 * (1 - near) + 1 - yl

    def quarter(k, ch, ssem, rsem, where):
        return remote(pt.at[k, ch], pt.at[k, ch], ssem, rsem, where)

    source, inner = x < 2, x >= 2
    always = row >= 0
    to_x, to_y, to_o = at(c=c_x), at(c=c_y), at(c=c_o)

    def out_recv(ch):
        quarter(k_p, ch, s_out.at[ch], r_out.at[ch], to_o).wait_recv()

    def x_recv(ch):
        quarter(k_s, ch, s_x.at[ch], r_x.at[ch], to_x).wait_recv()

    def y_recv(ch):
        quarter(k_pd, ch, s_y.at[ch], r_y.at[ch], to_y).wait_recv()

    def xd_recv(ch):
        quarter(k_sd, ch, s_x.at[4 + ch], r_x.at[4 + ch], to_x).wait_recv()

    def yd_recv(ch):
        quarter(k_sd, ch, s_y.at[4 + ch], r_y.at[4 + ch], to_y).wait_recv()

    def l_copy(u, slot, where):
        return remote(lt.at[u], lt.at[u], s_l.at[u, slot], r_l.at[u], where)

    def l_wait(u):
        l_copy(u, 0, at(r=r_core)).wait_recv()

    def l_routes(u, j):
        routes = [(always, l_copy(u, 0, at(r=r_core))), (yh == 0, l_copy(u, 1, at(r=r_y2, c=c_y)))]
        if j == 1:
            routes.append((row == 1, l_copy(u, 2, at(r=r_zp))))
            routes.append(((row == 1) | (row == 7), l_copy(u, 3, at(r=r_zm))))
        else:
            routes.append(((row == j) | (row == j + 2), l_copy(u, 2, at(r=r_zp))))
            routes.append((row == j, l_copy(u, 3, at(r=r_zm))))
        return routes

    def l_step(k, first, half_y=0):
        for j in (2, 3, 1):
            u = (j * (j - 1)) // 2 + k
            here = (core == CORE_OF[j]) & (k < j)

            @pl.when(here & (row == j) if first else here & (row != j) & (yh == half_y))
            def _():
                if first:
                    lt[u, pl.ds(0, B // 2), :] = pt[k, 0]
                    lt[u, pl.ds(B // 2, B // 2), :] = pt[k, 1]
                else:
                    l_wait(u)
                for cond, copy in l_routes(u, j):
                    @pl.when(cond)
                    def _():
                        copy.start()

    @pl.when(source)
    def _():
        for ch in range(4):
            quarter(k_p, ch, s_out.at[ch], r_out.at[ch], to_o).start()
            quarter(k_p, ch, s_x.at[ch], r_x.at[ch], to_x).start()
            quarter(k_p, ch, s_y.at[ch], r_y.at[ch], to_y).start()
        l_step(k_p, True)

    for a in range(2):
        for b in range(4):
            loads[a * 4 + b].wait()
            cond, copy = keeps[a * 4 + b]

            @pl.when(cond)
            def _():
                copy.start()
    for b in range(4):
        hi, lo = split(g32[b])
        gh[b] = hi
        gl[b] = lo

    @pl.when(source)
    def _():
        y_recv(0)
        quarter(k_pd, 0, s_x.at[4], r_x.at[4], to_x).start()
        y_recv(1)
        quarter(k_pd, 1, s_x.at[5], r_x.at[5], to_x).start()
        l_step(k_pd, True)
        x_recv(0)
        x_recv(1)
        l_step(k_s, True)

    @pl.when(inner)
    def _():
        for ch in range(2):
            out_recv(ch)
            quarter(k_p, ch, s_x.at[ch], r_x.at[ch], to_x).start()
            quarter(k_p, ch, s_y.at[ch], r_y.at[ch], to_y).start()
        l_step(k_p, True)
        y_recv(0)
        quarter(k_pd, 0, s_x.at[4], r_x.at[4], to_x).start()
        out_recv(2)
        quarter(k_p, 2, s_x.at[2], r_x.at[2], to_x).start()
        y_recv(1)
        l_step(k_pd, True)

    @pl.when(source)
    def _():
        y_recv(2)
        quarter(k_pd, 2, s_out.at[4], r_out.at[4], to_o).start()
        x_recv(2)
        quarter(k_s, 2, s_y.at[6], r_y.at[6], to_y).start()
        y_recv(3)
        quarter(k_pd, 3, s_out.at[5], r_out.at[5], to_o).start()
        x_recv(3)
        quarter(k_s, 3, s_y.at[7], r_y.at[7], to_y).start()

    @pl.when(inner)
    def _():
        x_recv(0)
        x_recv(1)
        quarter(k_s, 1, s_y.at[5], r_y.at[5], to_y).start()
        l_step(k_s, True)
        out_recv(3)
        quarter(k_p, 3, s_x.at[3], r_x.at[3], to_x).start()
        x_recv(2)
        quarter(k_s, 2, s_y.at[6], r_y.at[6], to_y).start()
        x_recv(3)
        quarter(k_s, 3, s_y.at[7], r_y.at[7], to_y).start()
    l_step(k_p, False)
    xd_recv(0)

    @pl.when(source)
    def _():
        xd_recv(1)

    @pl.when(inner)
    def _():
        yd_recv(1)
    l_step(k_sd, True)
    l_step(k_pd, False)
    yd_recv(2)
    yd_recv(3)

    @pl.when(inner)
    def _():
        for ch in (2, 3):
            quarter(k_pd, ch, s_out.at[2 + ch], r_out.at[2 + ch], to_o).wait_recv()
    l_step(k_s, False)
    l_step(k_sd, False)
    for k in (k_pd, k_p, k_sd, k_s):
        l_step(k, False, 1)

    zero = jnp.where(row < S, 0.0, 1.0).astype(F32)
    half = B // 2
    c_core = {k: remote(ut.at[k, pl.ds(2 - 2 * core, 2)], cr.at[k], s_c.at[k], r_c.at[k], at(r=r_core))
              for k in range(S)}

    def products(k):
        acc = jnp.concatenate(
            [jnp.concatenate([pt[k, h] * zero, pt[k, 2 + h]], axis=1) for h in range(2)], axis=0)
        for j in range(k + 1, S):
            u = LOW.index((j, k))

            @pl.when(core != CORE_OF[j])
            def _():
                l_wait(u)
            acc = acc - dot3(split(lt[u]), (ph[j], plo[j]))
        hi, lo = split(acc)
        ph[k] = hi
        plo[k] = lo

        @pl.loop(0, 4)
        def _(t):
            ut[k, t] = dot3((ph[k], plo[k]), (gh[t], gl[t]))
        c_core[k].start()

    k_own = (z - x + 4) % 4
    k_op, k_rm, k_rp = (k_own + 2) % 4, (k_own + 1) % 4, (k_own + 3) % 4
    halves = [pl.ds(0, half), pl.ds(half, half)]

    def unit(k, u, h):
        return ut.at[k, 2 * core + u, halves[h], :]

    c_op = [remote(unit(k_op, 0, h), op.at[h], s_zo.at[0, h], r_zo.at[0, h], at(r=r_zp)) for h in range(2)]
    c_om = [remote(unit(k_op, 1, h), om.at[h], s_zo.at[1, h], r_zo.at[1, h], at(r=r_zm)) for h in range(2)]
    c_rm = [[remote(unit(k_rm, u, h), rm.at[u, h], s_zr.at[0, u, h], r_zr.at[0, u, h], at(r=r_zp)) for h in range(2)]
            for u in range(2)]
    c_rp = [[remote(unit(k_rp, u, h), rp.at[u, h], s_zr.at[1, u, h], r_zr.at[1, u, h], at(r=r_zm)) for h in range(2)]
            for u in range(2)]

    def core_sum(k):
        c_core[k].wait_recv()
        for u in range(2):
            ut[k, 2 * core + u] = ut[k, 2 * core + u] + cr[k, u]

        @pl.when(k == k_op)
        def _():
            for h in range(2):
                c_op[h].start()
                c_om[h].start()

        @pl.when(k == k_rm)
        def _():
            for h in range(2):
                c_rm[1][h].start()

        @pl.when(k == k_rp)
        def _():
            for h in range(2):
                c_rp[0][h].start()

    products(3)
    products(2)
    core_sum(3)
    products(1)
    core_sum(2)
    products(0)
    core_sum(1)
    core_sum(0)
    for h in range(2):
        c_op[h].wait_recv()
        ut[k_rm, 2 * core, halves[h], :] = ut[k_rm, 2 * core, halves[h], :] + op[h]
        c_rm[0][h].start()
        c_om[h].wait_recv()
        ut[k_rp, 2 * core + 1, halves[h], :] = ut[k_rp, 2 * core + 1, halves[h], :] + om[h]
        c_rp[1][h].start()
    away = 1 - yh
    c_yh = [remote(unit(k_own, away, h), yr.at[h], s_yh.at[h], r_yh.at[h], at(r=r_y2)) for h in range(2)]
    for h in range(2):
        for u in range(2):
            c_rm[u][h].wait_recv()
            c_rp[u][h].wait_recv()
        ut[k_own, 2 * core + away, halves[h], :] = (
            ut[k_own, 2 * core + away, halves[h], :] + (rm[away, h] + rp[away, h]))
        c_yh[h].start()

    t_own = 2 * core + yh
    c_xa = [remote(xt.at[h], xa.at[t_own, halves[h], :], s_xa.at[h], r_xa.at[t_own, h], at(r=k_own)) for h in range(2)]
    c_xb = [remote(xt.at[h], xb.at[core, halves[h], :], s_xb.at[h], r_xb.at[core, h], at(r=b_row, c=b_col))
            for h in range(2)]
    for h in range(2):
        mine = ut[k_own, 2 * core + yh, halves[h], :] + (rm[yh, h] + rp[yh, h])
        c_yh[h].wait_recv()
        xt[h] = -(mine + yr[h])

        @pl.when(jnp.logical_not(b_self))
        def _():
            c_xb[h].start()

        @pl.when(b_self)
        def _():
            xb[core, halves[h], :] = xt[h]
    for h in range(2):
        @pl.when(jnp.logical_not(a_self))
        def _():
            c_xa[h].start()

        @pl.when(a_self)
        def _():
            xa[t_own, halves[h], :] = xt[h]

    dload.wait()

    @pl.when((row < S) & (col < S))
    def _():
        ones = (lax.broadcasted_iota(jnp.int32, (B, B), 0) == lax.broadcasted_iota(jnp.int32, (B, B), 1))
        for k in range(S):
            for m in range(S):
                if m < k:
                    mt[k, m] = jnp.zeros((B, B), F32)
                elif m == k:
                    mt[k, m] = ones.astype(F32)
                else:
                    acc = lt[LOW.index((m, k))]
                    for j in range(k + 1, m):
                        acc = acc + dot3(split(mt[k, j]), split(lt[LOW.index((m, j))]))
                    mt[k, m] = -acc
        zo[...] = jnp.zeros((B, B), F32)
        for m in range(S):
            part = dot3(split(mt[row, m]), split(dv[m]))
            zo[...] = zo[...] + dot3(split(part), split(mt[col, m]), ((1,), (1,)))

    c_zc = remote(zp.at[1 - core], zc, s_zc, r_zc, at(r=r_core))
    c_zd = [remote(zp.at[core, :, pl.ds(((quad + d) % 8) * 32, 32), :], zr.at[d - 1], s_zd.at[d - 1], r_zd.at[d - 1],
                   at(r=((quad + d) % 8) * 2 + core)) for d in range(1, 8)]
    c_zf = [remote(zs.at[m], zf.at[pl.ds(quad * 32, 32), :], s_zf.at[m], r_zf.at[quad], at(r=2 * m + core))
            for m in range(2)]

    @pl.when(col < S)
    def _():
        for a in range(2):
            sr, sc = b_source(a)

            @pl.when(jnp.logical_not((sr == row) & (sc == col)))
            def _():
                for h in range(2):
                    remote(xt.at[h], xb.at[a, halves[h], :], s_xb.at[h], r_xb.at[a, h], at(r=b_row, c=b_col)).wait_recv()
            xo[a] = xb[a].T
            hi, lo = split(xo[a])
            xh[pl.ds(a * B, B), :] = hi
            xl[pl.ds(a * B, B), :] = lo
        for l in range(S):
            zp[l % 2, l // 2] = dot3((ph[l], plo[l]), (xh[...], xl[...]))
        c_zc.start()
        c_zc.wait_recv()
        zp[core] = zp[core] + zc[...]
        for copy in c_zd:
            copy.start()
        acc = zp[core, :, pl.ds(quad * 32, 32), :]
        for d in range(7):
            c_zd[d].wait_recv()
            acc = acc + zr[d]
        zs[...] = acc
        for m in range(2):
            @pl.when(quad != m)
            def _():
                c_zf[m].start()

            @pl.when(quad == m)
            def _():
                zf[pl.ds(quad * 32, 32), :] = zs[m]

        @pl.when(row < S)
        def _():
            for q in range(8):
                @pl.when(quad != q)
                def _():
                    remote(zs.at[0], zf.at[pl.ds(q * 32, 32), :], s_zf.at[0], r_zf.at[q], at(r=r_core)).wait_recv()
            zo[...] = zo[...] - zf[...]

    w_row = [pltpu.make_async_copy(xa.at[t], out.at[0, :, t, :], w_sem.at[t]) for t in range(4)]
    w_col = [pltpu.make_async_copy(xo.at[a], out.at[a, :, 0, :], w_sem.at[4 + a]) for a in range(2)]
    w_dia = pltpu.make_async_copy(zo, out.at[0, :, 0, :], w_sem.at[6])
    writes = [((row < S) & (col >= S), w_row[0])] + [(row < S, w_row[t]) for t in range(1, 4)]
    writes += [((col < S) & (row >= S), w_col[0]), (col < S, w_col[1]), ((row < S) & (col < S), w_dia)]

    @pl.when(row < S)
    def _():
        for t in range(4):
            @pl.when(jnp.logical_not(a_self & (t_own == t)))
            def _():
                for h in range(2):
                    remote(xt.at[h], xa.at[t, halves[h], :], s_xa.at[h], r_xa.at[t, h], at(r=r_core)).wait_recv()
    for cond, copy in writes:
        @pl.when(cond)
        def _():
            copy.start()

    @pl.when(source)
    def _():
        for ch in range(4):
            quarter(k_p, ch, s_out.at[ch], r_out.at[ch], to_o).wait_send()
        for ch in (2, 3):
            quarter(k_pd, ch, s_out.at[2 + ch], r_out.at[2 + ch], to_o).wait_send()
            quarter(k_p, ch, s_y.at[ch], r_y.at[ch], to_y).wait_send()
        quarter(k_pd, 1, s_x.at[5], r_x.at[5], to_x).wait_send()

    @pl.when(inner)
    def _():
        quarter(k_s, 1, s_y.at[5], r_y.at[5], to_y).wait_send()
    for ch in range(4):
        quarter(k_p, ch, s_x.at[ch], r_x.at[ch], to_x).wait_send()
    for ch in range(2):
        quarter(k_p, ch, s_y.at[ch], r_y.at[ch], to_y).wait_send()
    quarter(k_pd, 0, s_x.at[4], r_x.at[4], to_x).wait_send()
    for ch in (2, 3):
        quarter(k_s, ch, s_y.at[4 + ch], r_y.at[4 + ch], to_y).wait_send()
    for j, k in LOW:
        @pl.when(core == CORE_OF[j])
        def _():
            for cond, copy in l_routes(LOW.index((j, k)), j):
                @pl.when(cond)
                def _():
                    copy.wait_send()
    for copy in list(c_core.values()) + c_op + c_om + c_rm[0] + c_rm[1] + c_rp[0] + c_rp[1] + c_yh:
        copy.wait_send()

    @pl.when(jnp.logical_not(b_self))
    def _():
        for copy in c_xb:
            copy.wait_send()

    @pl.when(jnp.logical_not(a_self))
    def _():
        for copy in c_xa:
            copy.wait_send()

    @pl.when(col < S)
    def _():
        c_zc.wait_send()
        for copy in c_zd:
            copy.wait_send()
        for m in range(2):
            @pl.when(quad != m)
            def _():
                c_zf[m].wait_send()
    for cond, copy in writes + keeps:
        @pl.when(cond)
        def _():
            copy.wait()


def body(prior, lfac, tile_mask, dinv):
    def vmem(*shape, kind=F32):
        return pltpu.VMEM(shape, kind)

    dma = pltpu.SemaphoreType.DMA
    hb = B // 2
    scratch = [
        vmem(4, 2 * B, B), vmem(4, 2 * B, B, kind=BF16), vmem(4, 2 * B, B, kind=BF16),
        vmem(2, B, B), vmem(4, 4, hb, B), vmem(4, B, 2 * B, kind=BF16), vmem(4, B, 2 * B, kind=BF16),
        vmem(6, B, B), vmem(4, 4, B, B), vmem(4, 2, B, B),
        vmem(2, hb, B), vmem(2, hb, B), vmem(2, 2, hb, B), vmem(2, 2, hb, B), vmem(2, hb, B),
        vmem(2, hb, B), vmem(4, B, B), vmem(2, B, B), vmem(2, B, B),
        vmem(2 * B, B, kind=BF16), vmem(2 * B, B, kind=BF16),
        vmem(2, 2, B, B), vmem(2, B, B), vmem(7, 2, 32, B), vmem(2, 32, B), vmem(B, B),
        vmem(4, 4, B, B), vmem(4, B, B), vmem(B, B),
        dma((2, 4)), dma((2,)), dma, dma((2, 4)), dma((7,)),
        dma((6,)), dma((6,)), dma((6,)), dma((6,)), dma((8,)), dma((8,)),
        dma((6, 4)), dma((6,)), dma((4,)), dma((4,)),
        dma((2, 2)), dma((2, 2)), dma((2, 2, 2)), dma((2, 2, 2)), dma((2,)), dma((2,)),
        dma((2,)), dma((4, 2)), dma((2,)), dma((2, 2)),
        dma, dma, dma((7,)), dma((7,)), dma((2,)), dma((8,)),
    ]
    return pl.pallas_call(
        kernel,
        out_shape=jax.ShapeDtypeStruct(prior.shape, F32),
        in_specs=[pl.BlockSpec(memory_space=pl.ANY), pl.BlockSpec(memory_space=pl.ANY),
                  pl.BlockSpec(memory_space=pltpu.SMEM), pl.BlockSpec(memory_space=pl.ANY)],
        out_specs=pl.BlockSpec(memory_space=pl.ANY),
        scratch_shapes=scratch,
        compiler_params=pltpu.CompilerParams(
            collective_id=0, has_side_effects=True, vmem_limit_bytes=56 * 1024 * 1024),
    )(prior, lfac, tile_mask, dinv)


def solution(mesh):
    placed = (P("prow", None, "pcol", None), P("prow", None, "pcol", None), P(), P())
    return jax.shard_map(
        body, mesh=mesh, in_specs=placed, out_specs=P("prow", None, "pcol", None), check_vma=False
    )
```

```python
import jax
import jax.numpy as jnp
from jax import lax
from jax.experimental import pallas as pl
from jax.experimental.pallas import tpu as pltpu
from jax.sharding import PartitionSpec as P

B = 256
S = 4
F32 = jnp.float32
BF16 = jnp.bfloat16
MESH = pl.DeviceIdType.MESH
LOW = [(1, 0), (2, 0), (2, 1), (3, 0), (3, 1), (3, 2)]
CORE_OF = {1: 1, 2: 0, 3: 1}


def split(value):
    hi = value.astype(BF16)
    lo = (value - hi.astype(F32)).astype(BF16)
    return hi, lo


def dot3(a, b, dims=((1,), (0,))):
    def one(left, right):
        return lax.dot_general(left, right, (dims, ((), ())), preferred_element_type=F32)

    return one(a[0], b[0]) + (one(a[0], b[1]) + one(a[1], b[0]))


def kernel(prior, lfac, mask, dinv, out,
           g32, gth, gtl, lt32, pn, pbh, pbl, ph, plo, lt, lbh, lbl, ut, cr, op, om, rm, rp, yr, xt, xa, xb, xat, xh, xl,
           zp, zc, zr, zs, zf, mt, dv, zo,
           g_sem, l_sem, d_sem, o_sem, w_sem,
           s_out, r_out, s_x, r_x, s_y, r_y,
           s_l, r_l, s_c, r_c, s_zo, r_zo, s_zr, r_zr, s_yh, r_yh,
           s_xa, r_xa, s_xb, r_xb, s_zc, r_zc, s_zd, r_zd, s_zf, r_zf):
    row = lax.axis_index("prow")
    col = lax.axis_index("pcol")
    yh, z, core = row // 8, (row // 2) % 4, row % 2
    x, yl = col // 2, col % 2
    quad = row // 2

    def at(r=None, c=None):
        return {"prow": row if r is None else r, "pcol": col if c is None else c}

    def remote(src, dst, ssem, rsem, where):
        return pltpu.make_async_remote_copy(
            src_ref=src, dst_ref=dst, send_sem=ssem, recv_sem=rsem, device_id=where, device_id_type=MESH)

    c_x = (x + 1 - 2 * (x % 2)) * 2 + yl
    c_y = x * 2 + 1 - yl
    c_o = (3 - x) * 2 + yl
    r_core = row + 1 - 2 * core
    r_zp = yh * 8 + ((z + 1) % 4) * 2 + core
    r_zm = yh * 8 + ((z + 3) % 4) * 2 + core
    r_y2 = (row + 8) % 16
    t_own = 2 * core + yh
    b_row = col + 8 * yh
    q_own = pl.ds(64 * z, 64)

    loads = []
    for a in range(2):
        for b in range(4):
            loads.append(pltpu.make_async_copy(prior.at[a, :, b, :], g32.at[b, pl.ds(a * B, B), :], g_sem.at[a, b]))
    keeps = []
    for a in range(2):
        for b in range(4):
            stays = row >= 0
            if a == 0:
                stays = stays & (row >= S)
            if b == 0:
                stays = stays & (col >= S)
            keeps.append((stays, pltpu.make_async_copy(
                g32.at[b, pl.ds(a * B, B), :], out.at[a, :, b, :], o_sem.at[a, b])))
    ltile = [pltpu.make_async_copy(lfac.at[a, :, 0, :], lt32.at[a], l_sem.at[a]) for a in range(2)]
    dload = pltpu.make_async_copy(dinv, dv, d_sem)

    @pl.when(col < S)
    def _():
        for copy in ltile:
            copy.start()
    for copy in loads:
        copy.start()
    dload.start()

    barrier = pltpu.get_barrier_semaphore()

    def greet(where):
        pl.semaphore_signal(barrier, inc=1, device_id=where, device_id_type=MESH)

    for step in range(1, 16):
        greet(at(r=(row + step) % 16))
    for c in (c_x, c_y, c_o):
        greet(at(c=c))
    greet(at(r=r_y2, c=c_y))

    def b_source(a, q):
        return yh * 8 + q * 2 + a, row % 8

    def b_other(a, q):
        sr, sc = b_source(a, q)
        return jnp.logical_not((sr == row) & (sc == col))

    for a in range(2):
        for q in range(4):
            sr, sc = b_source(a, q)

            @pl.when((col < S) & b_other(a, q))
            def _():
                greet(at(r=sr, c=sc))

    @pl.when(col < S)
    def _():
        for a in range(2):
            ltile[a].wait()
            live = mask[row + 16 * a, col] * (row + 16 * a > col).astype(jnp.int32)
            pn[col, pl.ds(a * B, B), :] = lt32[a] * live.astype(F32)

    pl.semaphore_wait(barrier, 19 + 4 - jnp.where((row == b_row) & (col < S), 1, 0))

    near = jnp.where((x == 0) | (x == 3), 0, 1)
    k_p, k_s = 2 * near + yl, 2 * (1 - near) + yl
    k_pd, k_sd = 2 * near + 1 - yl, 2 * (1 - near) + 1 - yl

    def quarter(k, ch, ssem, rsem, where):
        part = pn.at[k, pl.ds(128 * ch, 128), :]
        return remote(part, part, ssem, rsem, where)

    source, inner = x < 2, x >= 2
    always = row >= 0
    to_x, to_y, to_o = at(c=c_x), at(c=c_y), at(c=c_o)

    def out_recv(ch):
        quarter(k_p, ch, s_out.at[ch], r_out.at[ch], to_o).wait_recv()

    def x_recv(ch):
        quarter(k_s, ch, s_x.at[ch], r_x.at[ch], to_x).wait_recv()

    def y_recv(ch):
        quarter(k_pd, ch, s_y.at[ch], r_y.at[ch], to_y).wait_recv()

    def xd_recv(ch):
        quarter(k_sd, ch, s_x.at[4 + ch // 2], r_x.at[4 + ch // 2], to_x).wait_recv()

    def yd_recv(ch):
        quarter(k_sd, ch, s_y.at[4 + ch], r_y.at[4 + ch], to_y).wait_recv()

    def l_copy(u, slot, where):
        return remote(lt.at[u], lt.at[u], s_l.at[u, slot], r_l.at[u], where)

    def l_wait(u):
        l_copy(u, 0, at(r=r_core)).wait_recv()

    def l_routes(u, j):
        routes = [(always, l_copy(u, 0, at(r=r_core))), (yh == 0, l_copy(u, 1, at(r=r_y2, c=c_y)))]
        if j == 1:
            routes.append(((row == 1) | (row == 3), l_copy(u, 2, at(r=r_zp))))
            routes.append((row == 1, l_copy(u, 3, at(r=r_zm))))
        else:
            routes.append(((row == j) | (row == j + 2), l_copy(u, 2, at(r=r_zp))))
            routes.append((row == j, l_copy(u, 3, at(r=r_zm))))
        return routes

    groups = [(yh == 0) & (z < 3), (yh == 0) & (z == 3), yh == 1]

    def l_step(k, first, group=0):
        for j in (2, 3, 1):
            u = (j * (j - 1)) // 2 + k
            here = (core == CORE_OF[j]) & (k < j)

            @pl.when(here & (row == j) if first else here & (row != j) & groups[group])
            def _():
                if first:
                    lt[u] = pn[k, pl.ds(0, B), :]
                else:
                    l_wait(u)
                for cond, copy in l_routes(u, j):
                    @pl.when(cond)
                    def _():
                        copy.start()

    def p_out(ch):
        quarter(k_p, ch, s_out.at[ch], r_out.at[ch], to_o).start()

    def p_x(ch):
        quarter(k_p, ch, s_x.at[ch], r_x.at[ch], to_x).start()

    def p_y(ch):
        quarter(k_p, ch, s_y.at[ch], r_y.at[ch], to_y).start()

    def e_out(ch):
        quarter(k_pd, ch, s_out.at[3 + ch], r_out.at[3 + ch], to_o).start()

    def d_x(ch):
        quarter(k_pd, ch, s_x.at[4 + ch // 2], r_x.at[4 + ch // 2], to_x).start()

    def d_y(ch):
        quarter(k_s, ch, s_y.at[4 + ch], r_y.at[4 + ch], to_y).start()

    @pl.when(source)
    def _():
        for ch in range(3):
            p_out(ch)
            p_y(ch)
        p_x(0)
        p_x(1)
        l_step(k_p, True)

    for a in range(2):
        for b in range(4):
            loads[a * 4 + b].wait()
            cond, copy = keeps[a * 4 + b]

            @pl.when(cond)
            def _():
                copy.start()
    for b in range(4):
        for a in range(2):
            hi, lo = split(g32[b, pl.ds(a * B, B), :].T)
            gth[b, :, pl.ds(a * B, B)] = hi
            gtl[b, :, pl.ds(a * B, B)] = lo

    @pl.when(source)
    def _():
        y_recv(0)
        d_x(0)
        p_x(2)
        p_out(3)
        y_recv(1)
        e_out(1)
        p_x(3)
        x_recv(0)
        x_recv(1)
        d_y(1)
        p_y(3)
        l_step(k_pd, True)
        l_step(k_s, True)
        y_recv(2)
        d_x(2)
        e_out(2)
        xd_recv(0)
        yd_recv(1)
        l_step(k_sd, True)

    @pl.when(inner)
    def _():
        out_recv(0)
        p_x(0)
        p_y(0)
        out_recv(1)
        p_x(1)
        l_step(k_p, True)
        x_recv(0)
        d_y(0)
        out_recv(2)
        p_x(2)
        x_recv(1)
        d_y(1)
        l_step(k_s, True)
        out_recv(3)
        p_x(3)
    l_step(k_p, False)
    l_step(k_p, False, 1)

    @pl.when(source)
    def _():
        y_recv(3)
        e_out(3)
        x_recv(2)
        x_recv(3)
        d_y(3)

    @pl.when(inner)
    def _():
        x_recv(2)
        d_y(2)
        y_recv(0)
        quarter(k_pd, 1, s_out.at[4], r_out.at[4], to_o).wait_recv()
        l_step(k_pd, True)
        yd_recv(0)
        yd_recv(1)
        l_step(k_sd, True)
        x_recv(3)
        d_y(3)
    l_step(k_pd, False)
    l_step(k_s, False)

    @pl.when(source)
    def _():
        xd_recv(2)

    @pl.when(inner)
    def _():
        yd_recv(2)
        quarter(k_pd, 2, s_out.at[5], r_out.at[5], to_o).wait_recv()
        quarter(k_pd, 3, s_out.at[6], r_out.at[6], to_o).wait_recv()
    yd_recv(3)
    l_step(k_sd, False)

    zero = jnp.where(row < S, 0.0, 1.0).astype(F32)
    for k in range(S):
        for a in range(2):
            rows = pl.ds(a * B, B)
            hi, lo = split(pn[k, rows, :] * zero if a == 0 else pn[k, rows, :])
            pbh[k, rows, :] = hi
            pbl[k, rows, :] = lo
    c_core = [remote(ut.at[2 - 2 * core + u], cr.at[u], s_c.at[u], r_c.at[u], at(r=r_core)) for u in range(2)]

    def products(t):
        @pl.loop(0, S)
        def _(k):
            value = dot3((gth[t], gtl[t]), (pbh[k], pbl[k]))
            for q in range(4):
                ut[t, q, :, pl.ds(pl.multiple_of(k * B, B), B)] = value[q * 64:(q + 1) * 64]

    for u in range(2):
        products(2 - 2 * core + u)
        c_core[u].start()
    for u in range(2):
        products(2 * core + u)

    halves = [pl.ds(0, 32), pl.ds(32, 32)]
    q_op, q_rm, q_rp = (z + 2) % 4, (z + 1) % 4, (z + 3) % 4

    def unit(q, u, h):
        return ut.at[2 * core + u, q, halves[h], :]

    c_op = [remote(unit(q_op, 0, h), op.at[h], s_zo.at[0, h], r_zo.at[0, h], at(r=r_zp)) for h in range(2)]
    c_om = [remote(unit(q_op, 1, h), om.at[h], s_zo.at[1, h], r_zo.at[1, h], at(r=r_zm)) for h in range(2)]
    c_rm = [[remote(unit(q_rm, u, h), rm.at[u, h], s_zr.at[0, u, h], r_zr.at[0, u, h], at(r=r_zp)) for h in range(2)]
            for u in range(2)]
    c_rp = [[remote(unit(q_rp, u, h), rp.at[u, h], s_zr.at[1, u, h], r_zr.at[1, u, h], at(r=r_zm)) for h in range(2)]
            for u in range(2)]
    c_core[0].wait_recv()
    ut[2 * core, q_op] = ut[2 * core, q_op] + cr[0, q_op]
    for h in range(2):
        c_op[h].start()
    for q in (q_rp, q_rm, z):
        ut[2 * core, q] = ut[2 * core, q] + cr[0, q]
    c_rp[0][0].start()
    c_core[1].wait_recv()
    ut[2 * core + 1, q_op] = ut[2 * core + 1, q_op] + cr[1, q_op]
    for h in range(2):
        c_om[h].start()
    for q in (q_rm, q_rp, z):
        ut[2 * core + 1, q] = ut[2 * core + 1, q] + cr[1, q]
    c_rm[1][0].start()
    for k in (k_pd, k_s, k_sd):
        l_step(k, False, 1)
    for h in range(2):
        c_op[h].wait_recv()
        ut[2 * core, q_rm, halves[h], :] = ut[2 * core, q_rm, halves[h], :] + op[h]
        c_rm[0][h].start()
        c_om[h].wait_recv()
        ut[2 * core + 1, q_rp, halves[h], :] = ut[2 * core + 1, q_rp, halves[h], :] + om[h]
        c_rp[1][h].start()
        if h == 0:
            c_rp[0][1].start()
            c_rm[1][1].start()
    for k in (k_pd, k_p, k_sd, k_s):
        l_step(k, False, 2)

    for u, (j, k) in enumerate(LOW):
        @pl.when(core != CORE_OF[j])
        def _():
            l_wait(u)
    for u in range(6):
        hi, lo = split(lt[u])
        lbh[u] = hi
        lbl[u] = lo

    def low(j, k):
        return lbh[LOW.index((j, k))], lbl[LOW.index((j, k))]

    away = 1 - yh
    c_yh = [remote(unit(z, away, h), yr.at[h], s_yh.at[h], r_yh.at[h], at(r=r_y2)) for h in range(2)]

    def z_sum(h):
        for u in range(2):
            c_rm[u][h].wait_recv()
            c_rp[u][h].wait_recv()
        ut[2 * core + away, z, halves[h], :] = (
            ut[2 * core + away, z, halves[h], :] + (rm[away, h] + rp[away, h]))
        c_yh[h].start()

    z_sum(0)

    @pl.when(col < S)
    def _():
        for k in (3, 2, 1, 0):
            acc = jnp.concatenate([pn[k, pl.ds(0, B), :] * zero, pn[k, pl.ds(B, B), :]], axis=0)
            for j in range(k + 1, S):
                acc = acc - dot3((pbh[j], pbl[j]), low(j, k))
            hi, lo = split(acc)
            pbh[k] = hi
            pbl[k] = lo
            hi, lo = split(acc.T)
            ph[k] = hi
            plo[k] = lo

    z_sum(1)

    dload.wait()

    @pl.when((row < S) & (col < S))
    def _():
        ones = (lax.broadcasted_iota(jnp.int32, (B, B), 0) == lax.broadcasted_iota(jnp.int32, (B, B), 1))
        for m in range(S):
            for k in range(S):
                if m < k:
                    mt[m, k] = jnp.zeros((B, B), F32)
                elif m == k:
                    mt[m, k] = ones.astype(F32)
                else:
                    acc = lt[LOW.index((m, k))]
                    for j in range(k + 1, m):
                        acc = acc + dot3(low(m, j), split(mt[j, k]))
                    mt[m, k] = -acc
        zo[...] = jnp.zeros((B, B), F32)
        for m in range(S):
            part = dot3(split(dv[m]), split(mt[m, col]))
            zo[...] = zo[...] + dot3(split(mt[m, row].T), split(part))

    for h in range(2):
        c_yh[h].wait_recv()
    total = ut[2 * core + yh, z] + jnp.concatenate([rm[yh, h] + rp[yh, h] + yr[h] for h in range(2)], axis=0)
    found = {}
    for k in (3, 2, 1, 0):
        acc = total[:, k * B:(k + 1) * B]
        for j in range(k + 1, S):
            acc = acc + dot3(found[j], low(j, k))
        xt[k] = -acc
        found[k] = split(-acc)
    c_xa = [remote(xt.at[k], xa.at[t_own, q_own, :], s_xa.at[k], r_xa.at[t_own, z], at(r=k)) for k in range(S)]
    c_xb = [remote(xt.at[k], xb.at[core, q_own, :], s_xb.at[k], r_xb.at[core, z], at(r=b_row, c=k)) for k in range(S)]

    def b_self(k):
        return (row == b_row) & (col == k)

    for k in (3, 2, 1, 0):
        @pl.when(jnp.logical_not(b_self(k)))
        def _():
            c_xb[k].start()

        @pl.when(b_self(k))
        def _():
            xb[core, q_own, :] = xt[k]
    for k in range(S):
        @pl.when(row != k)
        def _():
            c_xa[k].start()

        @pl.when(row == k)
        def _():
            xa[t_own, q_own, :] = xt[k]

    c_zc = remote(zp.at[1 - core], zc, s_zc, r_zc, at(r=r_core))
    c_zd = [remote(zp.at[core, :, pl.ds(((quad + d) % 8) * 32, 32), :], zr.at[d - 1], s_zd.at[d - 1], r_zd.at[d - 1],
                   at(r=((quad + d) % 8) * 2 + core)) for d in range(1, 8)]
    c_zf = [remote(zs.at[m], zf.at[pl.ds(quad * 32, 32), :], s_zf.at[m], r_zf.at[quad], at(r=2 * m + core))
            for m in range(2)]

    @pl.when(col < S)
    def _():
        for a in range(2):
            for q in range(4):
                @pl.when(b_other(a, q))
                def _():
                    remote(xt.at[0], xb.at[a, pl.ds(64 * q, 64), :], s_xb.at[0], r_xb.at[a, q], at(r=b_row)).wait_recv()
            hi, lo = split(xb[a])
            xh[pl.ds(a * B, B), :] = hi
            xl[pl.ds(a * B, B), :] = lo
        for l in range(S):
            zp[l % 2, l // 2] = dot3((ph[l], plo[l]), (xh[...], xl[...]))
        c_zc.start()
        c_zc.wait_recv()
        zp[core] = zp[core] + zc[...]
        for copy in c_zd:
            copy.start()
        acc = zp[core, :, pl.ds(quad * 32, 32), :]
        for d in range(7):
            c_zd[d].wait_recv()
            acc = acc + zr[d]
        zs[...] = acc
        for m in range(2):
            @pl.when(quad != m)
            def _():
                c_zf[m].start()

            @pl.when(quad == m)
            def _():
                zf[pl.ds(quad * 32, 32), :] = zs[m]

        @pl.when(row < S)
        def _():
            for q in range(8):
                @pl.when(quad != q)
                def _():
                    remote(zs.at[0], zf.at[pl.ds(q * 32, 32), :], s_zf.at[0], r_zf.at[q], at(r=r_core)).wait_recv()
            zo[...] = zo[...] - zf[...]

    w_row = [pltpu.make_async_copy(xat.at[t], out.at[0, :, t, :], w_sem.at[t]) for t in range(4)]
    w_col = [pltpu.make_async_copy(xb.at[a], out.at[a, :, 0, :], w_sem.at[4 + a]) for a in range(2)]
    w_dia = pltpu.make_async_copy(zo, out.at[0, :, 0, :], w_sem.at[6])
    writes = [((row < S) & (col >= S), w_row[0])] + [(row < S, w_row[t]) for t in range(1, 4)]
    writes += [((col < S) & (row >= S), w_col[0]), (col < S, w_col[1]), ((row < S) & (col < S), w_dia)]

    @pl.when(row < S)
    def _():
        for t in range(4):
            for q in range(4):
                @pl.when(row != (t % 2) * 8 + q * 2 + t // 2)
                def _():
                    remote(xt.at[0], xa.at[t, pl.ds(64 * q, 64), :], s_xa.at[0], r_xa.at[t, q], at(r=r_core)).wait_recv()
            xat[t] = xa[t].T
    for cond, copy in writes:
        @pl.when(cond)
        def _():
            copy.start()

    @pl.when(source)
    def _():
        for ch in range(4):
            quarter(k_p, ch, s_out.at[ch], r_out.at[ch], to_o).wait_send()
        for ch in (1, 2, 3):
            quarter(k_pd, ch, s_out.at[3 + ch], r_out.at[3 + ch], to_o).wait_send()
            quarter(k_p, ch, s_y.at[ch], r_y.at[ch], to_y).wait_send()
        for ch in (0, 2):
            quarter(k_pd, ch, s_x.at[4 + ch // 2], r_x.at[4 + ch // 2], to_x).wait_send()

    @pl.when(inner)
    def _():
        for ch in (0, 2):
            quarter(k_s, ch, s_y.at[4 + ch], r_y.at[4 + ch], to_y).wait_send()
    for ch in range(4):
        quarter(k_p, ch, s_x.at[ch], r_x.at[ch], to_x).wait_send()
    quarter(k_p, 0, s_y.at[0], r_y.at[0], to_y).wait_send()
    for ch in (1, 3):
        quarter(k_s, ch, s_y.at[4 + ch], r_y.at[4 + ch], to_y).wait_send()
    for j, k in LOW:
        @pl.when(core == CORE_OF[j])
        def _():
            for cond, copy in l_routes(LOW.index((j, k)), j):
                @pl.when(cond)
                def _():
                    copy.wait_send()
    for copy in c_core + c_op + c_om + c_rm[0] + c_rm[1] + c_rp[0] + c_rp[1] + c_yh:
        copy.wait_send()

    for k in range(S):
        @pl.when(jnp.logical_not(b_self(k)))
        def _():
            c_xb[k].wait_send()

        @pl.when(row != k)
        def _():
            c_xa[k].wait_send()

    @pl.when(col < S)
    def _():
        c_zc.wait_send()
        for copy in c_zd:
            copy.wait_send()
        for m in range(2):
            @pl.when(quad != m)
            def _():
                c_zf[m].wait_send()
    for cond, copy in writes + keeps:
        @pl.when(cond)
        def _():
            copy.wait()


def body(prior, lfac, tile_mask, dinv):
    def vmem(*shape, kind=F32):
        return pltpu.VMEM(shape, kind)

    dma = pltpu.SemaphoreType.DMA
    wide = S * B
    scratch = [
        vmem(4, 2 * B, B), vmem(4, B, 2 * B, kind=BF16), vmem(4, B, 2 * B, kind=BF16),
        vmem(2, B, B), vmem(4, 2 * B, B), vmem(4, 2 * B, B, kind=BF16), vmem(4, 2 * B, B, kind=BF16),
        vmem(4, B, 2 * B, kind=BF16), vmem(4, B, 2 * B, kind=BF16),
        vmem(6, B, B), vmem(6, B, B, kind=BF16), vmem(6, B, B, kind=BF16),
        vmem(4, 4, 64, wide), vmem(2, 4, 64, wide),
        vmem(2, 32, wide), vmem(2, 32, wide), vmem(2, 2, 32, wide), vmem(2, 2, 32, wide), vmem(2, 32, wide),
        vmem(4, 64, B), vmem(4, B, B), vmem(2, B, B), vmem(4, B, B),
        vmem(2 * B, B, kind=BF16), vmem(2 * B, B, kind=BF16),
        vmem(2, 2, B, B), vmem(2, B, B), vmem(7, 2, 32, B), vmem(2, 32, B), vmem(B, B),
        vmem(4, 4, B, B), vmem(4, B, B), vmem(B, B),
        dma((2, 4)), dma((2,)), dma, dma((2, 4)), dma((7,)),
        dma((7,)), dma((7,)), dma((6,)), dma((6,)), dma((8,)), dma((8,)),
        dma((6, 4)), dma((6,)), dma((2,)), dma((2,)),
        dma((2, 2)), dma((2, 2)), dma((2, 2, 2)), dma((2, 2, 2)), dma((2,)), dma((2,)),
        dma((4,)), dma((4, 4)), dma((4,)), dma((2, 4)),
        dma, dma, dma((7,)), dma((7,)), dma((2,)), dma((8,)),
    ]
    return pl.pallas_call(
        kernel,
        out_shape=jax.ShapeDtypeStruct(prior.shape, F32),
        in_specs=[pl.BlockSpec(memory_space=pl.ANY), pl.BlockSpec(memory_space=pl.ANY),
                  pl.BlockSpec(memory_space=pltpu.SMEM), pl.BlockSpec(memory_space=pl.ANY)],
        out_specs=pl.BlockSpec(memory_space=pl.ANY),
        scratch_shapes=scratch,
        compiler_params=pltpu.CompilerParams(
            collective_id=0, has_side_effects=True, vmem_limit_bytes=56 * 1024 * 1024),
    )(prior, lfac, tile_mask, dinv)


def solution(mesh):
    placed = (P("prow", None, "pcol", None), P("prow", None, "pcol", None), P(), P())
    return jax.shard_map(
        body, mesh=mesh, in_specs=placed, out_specs=P("prow", None, "pcol", None), check_vma=False
    )
```

```python
import jax
import jax.numpy as jnp
from jax import lax
from jax.experimental import pallas as pl
from jax.experimental.pallas import tpu as pltpu
from jax.sharding import PartitionSpec as P

B = 256
S = 4
F32 = jnp.float32
BF16 = jnp.bfloat16
MESH = pl.DeviceIdType.MESH
LOW = [(1, 0), (2, 0), (2, 1), (3, 0), (3, 1), (3, 2)]
CORE_OF = {1: 1, 2: 0, 3: 1}


def split(value):
    hi = value.astype(BF16)
    lo = (value - hi.astype(F32)).astype(BF16)
    return hi, lo


def dot3(a, b, dims=((1,), (0,))):
    def one(left, right):
        return lax.dot_general(left, right, (dims, ((), ())), preferred_element_type=F32)

    return one(a[0], b[0]) + (one(a[0], b[1]) + one(a[1], b[0]))


def kernel(prior, lfac, tile_mask, dinv, out,
           g32, gth, gtl, lt32, pn, pbh, pbl, ph, plo, lt, lbh, lbl, ut, cr, op, om, rm, rp, yr, xt, xa, xb, xat, xh, xl,
           zp, zc, zr, zs, zf, mt, dv, zo, mask, m_sem,
           g_sem, l_sem, d_sem, o_sem, w_sem,
           s_out, r_out, s_x, r_x, s_y, r_y,
           s_l, r_l, s_c, r_c, s_zo, r_zo, s_zr, r_zr, s_yh, r_yh,
           s_xa, r_xa, s_xb, r_xb, s_zc, r_zc, s_zd, r_zd, s_zf, r_zf):
    row = lax.axis_index("prow")
    col = lax.axis_index("pcol")
    yh, z, core = row // 8, (row // 2) % 4, row % 2
    x, yl = col // 2, col % 2
    quad = row // 2

    def at(r=None, c=None):
        return {"prow": row if r is None else r, "pcol": col if c is None else c}

    def remote(src, dst, ssem, rsem, where):
        return pltpu.make_async_remote_copy(
            src_ref=src, dst_ref=dst, send_sem=ssem, recv_sem=rsem, device_id=where, device_id_type=MESH)

    c_x = (x + 1 - 2 * (x % 2)) * 2 + yl
    c_y = x * 2 + 1 - yl
    c_o = (3 - x) * 2 + yl
    r_core = row + 1 - 2 * core
    r_zp = yh * 8 + ((z + 1) % 4) * 2 + core
    r_zm = yh * 8 + ((z + 3) % 4) * 2 + core
    r_y2 = (row + 8) % 16
    t_own = 2 * core + yh
    b_row = col + 8 * yh
    q_own = pl.ds(64 * z, 64)

    loads = []
    for a in range(2):
        for b in range(4):
            loads.append(pltpu.make_async_copy(prior.at[a, :, b, :], g32.at[b, pl.ds(a * B, B), :], g_sem.at[a, b]))
    keeps = []
    for a in range(2):
        for b in range(4):
            stays = row >= 0
            if a == 0:
                stays = stays & (row >= S)
            if b == 0:
                stays = stays & (col >= S)
            keeps.append((stays, pltpu.make_async_copy(
                g32.at[b, pl.ds(a * B, B), :], out.at[a, :, b, :], o_sem.at[a, b])))
    ltile = [pltpu.make_async_copy(lfac.at[a, :, 0, :], lt32.at[a], l_sem.at[a]) for a in range(2)]
    mload = pltpu.make_async_copy(tile_mask, mask, m_sem)
    dload = pltpu.make_async_copy(dinv, dv, d_sem)

    @pl.when(col < S)
    def _():
        mload.start()
        for copy in ltile:
            copy.start()
    for copy in loads:
        copy.start()
    dload.start()

    barrier = pltpu.get_barrier_semaphore()

    def greet(where):
        pl.semaphore_signal(barrier, inc=1, device_id=where, device_id_type=MESH)

    for step in range(1, 16):
        greet(at(r=(row + step) % 16))
    for c in (c_x, c_y, c_o):
        greet(at(c=c))
    greet(at(r=r_y2, c=c_y))

    def b_source(a, q):
        return yh * 8 + q * 2 + a, row % 8

    def b_other(a, q):
        sr, sc = b_source(a, q)
        return jnp.logical_not((sr == row) & (sc == col))

    for a in range(2):
        for q in range(4):
            sr, sc = b_source(a, q)

            @pl.when((col < S) & b_other(a, q))
            def _():
                greet(at(r=sr, c=sc))

    @pl.when(col < S)
    def _():
        mload.wait()
        for a in range(2):
            ltile[a].wait()
            live = mask[row + 16 * a, col] * (row + 16 * a > col).astype(jnp.int32)
            pn[col, pl.ds(a * B, B), :] = lt32[a] * live.astype(F32)

    pl.semaphore_wait(barrier, 19 + 4 - jnp.where((row == b_row) & (col < S), 1, 0))

    near = jnp.where((x == 0) | (x == 3), 0, 1)
    k_p, k_s = 2 * near + yl, 2 * (1 - near) + yl
    k_pd, k_sd = 2 * near + 1 - yl, 2 * (1 - near) + 1 - yl

    def quarter(k, ch, ssem, rsem, where):
        part = pn.at[k, pl.ds(128 * ch, 128), :]
        return remote(part, part, ssem, rsem, where)

    source, inner = x < 2, x >= 2
    always = row >= 0
    to_x, to_y, to_o = at(c=c_x), at(c=c_y), at(c=c_o)

    def out_recv(ch):
        quarter(k_p, ch, s_out.at[ch], r_out.at[ch], to_o).wait_recv()

    def x_recv(ch):
        quarter(k_s, ch, s_x.at[ch], r_x.at[ch], to_x).wait_recv()

    def y_recv(ch):
        quarter(k_pd, ch, s_y.at[ch], r_y.at[ch], to_y).wait_recv()

    def xd_recv(ch):
        quarter(k_sd, ch, s_x.at[4 + ch // 2], r_x.at[4 + ch // 2], to_x).wait_recv()

    def yd_recv(ch):
        quarter(k_sd, ch, s_y.at[4 + ch], r_y.at[4 + ch], to_y).wait_recv()

    def l_copy(u, slot, where):
        return remote(lt.at[u], lt.at[u], s_l.at[u, slot], r_l.at[u], where)

    def l_wait(u):
        l_copy(u, 0, at(r=r_core)).wait_recv()

    def l_routes(u, j):
        routes = [(always, l_copy(u, 0, at(r=r_core))), (yh == 0, l_copy(u, 1, at(r=r_y2, c=c_y)))]
        if j == 1:
            routes.append(((row == 1) | (row == 3), l_copy(u, 2, at(r=r_zp))))
            routes.append((row == 1, l_copy(u, 3, at(r=r_zm))))
        else:
            routes.append(((row == j) | (row == j + 2), l_copy(u, 2, at(r=r_zp))))
            routes.append((row == j, l_copy(u, 3, at(r=r_zm))))
        return routes

    groups = [(yh == 0) & (z < 3), (yh == 0) & (z == 3), yh == 1]

    def l_step(k, first, group=0):
        for j in (2, 3, 1):
            u = (j * (j - 1)) // 2 + k
            here = (core == CORE_OF[j]) & (k < j)

            @pl.when(here & (row == j) if first else here & (row != j) & groups[group])
            def _():
                if first:
                    lt[u] = pn[k, pl.ds(0, B), :]
                else:
                    l_wait(u)
                for cond, copy in l_routes(u, j):
                    @pl.when(cond)
                    def _():
                        copy.start()

    def p_out(ch):
        quarter(k_p, ch, s_out.at[ch], r_out.at[ch], to_o).start()

    def p_x(ch):
        quarter(k_p, ch, s_x.at[ch], r_x.at[ch], to_x).start()

    def p_y(ch):
        quarter(k_p, ch, s_y.at[ch], r_y.at[ch], to_y).start()

    def e_out(ch):
        quarter(k_pd, ch, s_out.at[3 + ch], r_out.at[3 + ch], to_o).start()

    def d_x(ch):
        quarter(k_pd, ch, s_x.at[4 + ch // 2], r_x.at[4 + ch // 2], to_x).start()

    def d_y(ch):
        quarter(k_s, ch, s_y.at[4 + ch], r_y.at[4 + ch], to_y).start()

    @pl.when(source)
    def _():
        for ch in range(3):
            p_out(ch)
            p_y(ch)
        p_x(0)
        p_x(1)
        l_step(k_p, True)

    for a in range(2):
        for b in range(4):
            loads[a * 4 + b].wait()
            cond, copy = keeps[a * 4 + b]

            @pl.when(cond)
            def _():
                copy.start()
    for b in range(4):
        for a in range(2):
            hi, lo = split(g32[b, pl.ds(a * B, B), :].T)
            gth[b, :, pl.ds(a * B, B)] = hi
            gtl[b, :, pl.ds(a * B, B)] = lo

    zero = jnp.where(row < S, 0.0, 1.0).astype(F32)

    def core_copy(k):
        lanes = pl.ds(pl.multiple_of(k * B, B), B)
        return remote(ut.at[pl.ds(2 - 2 * core, 2), :, :, lanes], cr.at[:, :, :, lanes], s_c.at[k], r_c.at[k], at(r=r_core))

    def products(k):
        for a in range(2):
            rows = pl.ds(a * B, B)
            hi, lo = split(pn[k, rows, :] * zero if a == 0 else pn[k, rows, :])
            pbh[k, rows, :] = hi
            pbl[k, rows, :] = lo

        @pl.loop(0, 4)
        def _(step):
            t = lax.rem(2 - 2 * core + step, 4)
            value = dot3((gth[t], gtl[t]), (pbh[k], pbl[k]))
            for q in range(4):
                ut[t, q, :, pl.ds(pl.multiple_of(k * B, B), B)] = value[q * 64:(q + 1) * 64]
        core_copy(k).start()

    @pl.when(source)
    def _():
        products(k_p)
        y_recv(0)
        d_x(0)
        p_x(2)
        p_out(3)
        y_recv(1)
        e_out(1)
        p_x(3)
        x_recv(0)
        x_recv(1)
        d_y(1)
        p_y(3)
        l_step(k_pd, True)
        l_step(k_s, True)
        y_recv(2)
        d_x(2)
        e_out(2)
        xd_recv(0)
        yd_recv(1)
        l_step(k_sd, True)

    @pl.when(inner)
    def _():
        out_recv(0)
        p_x(0)
        p_y(0)
        out_recv(1)
        p_x(1)
        l_step(k_p, True)
        x_recv(0)
        d_y(0)
        out_recv(2)
        p_x(2)
        x_recv(1)
        d_y(1)
        l_step(k_s, True)
        out_recv(3)
        p_x(3)
        products(k_p)
    l_step(k_p, False)
    l_step(k_p, False, 1)

    @pl.when(source)
    def _():
        y_recv(3)
        e_out(3)
        x_recv(2)
        x_recv(3)
        d_y(3)

    @pl.when(inner)
    def _():
        x_recv(2)
        d_y(2)
        y_recv(0)
        quarter(k_pd, 1, s_out.at[4], r_out.at[4], to_o).wait_recv()
        l_step(k_pd, True)
        yd_recv(0)
        yd_recv(1)
        l_step(k_sd, True)
        x_recv(3)
        d_y(3)
    l_step(k_pd, False)
    l_step(k_s, False)
    products(k_s)

    @pl.when(inner)
    def _():
        for ch in (2, 3):
            quarter(k_pd, ch, s_out.at[3 + ch], r_out.at[3 + ch], to_o).wait_recv()
    products(k_pd)
    l_step(k_sd, False)

    @pl.when(source)
    def _():
        xd_recv(2)

    @pl.when(inner)
    def _():
        yd_recv(2)
    yd_recv(3)
    products(k_sd)

    halves = [pl.ds(0, 32), pl.ds(32, 32)]
    q_op, q_rm, q_rp = (z + 2) % 4, (z + 1) % 4, (z + 3) % 4

    def unit(q, u, h):
        return ut.at[2 * core + u, q, halves[h], :]

    c_op = [remote(unit(q_op, 0, h), op.at[h], s_zo.at[0, h], r_zo.at[0, h], at(r=r_zp)) for h in range(2)]
    c_om = [remote(unit(q_op, 1, h), om.at[h], s_zo.at[1, h], r_zo.at[1, h], at(r=r_zm)) for h in range(2)]
    c_rm = [[remote(unit(q_rm, u, h), rm.at[u, h], s_zr.at[0, u, h], r_zr.at[0, u, h], at(r=r_zp)) for h in range(2)]
            for u in range(2)]
    c_rp = [[remote(unit(q_rp, u, h), rp.at[u, h], s_zr.at[1, u, h], r_zr.at[1, u, h], at(r=r_zm)) for h in range(2)]
            for u in range(2)]
    for k in range(S):
        core_copy(k).wait_recv()
    ut[2 * core, q_op] = ut[2 * core, q_op] + cr[0, q_op]
    for h in range(2):
        c_op[h].start()
    for q in (q_rp, q_rm, z):
        ut[2 * core, q] = ut[2 * core, q] + cr[0, q]
    c_rp[0][0].start()
    ut[2 * core + 1, q_op] = ut[2 * core + 1, q_op] + cr[1, q_op]
    for h in range(2):
        c_om[h].start()
    for q in (q_rm, q_rp, z):
        ut[2 * core + 1, q] = ut[2 * core + 1, q] + cr[1, q]
    c_rm[1][0].start()
    for k in (k_pd, k_s, k_sd):
        l_step(k, False, 1)
    for h in range(2):
        c_op[h].wait_recv()
        ut[2 * core, q_rm, halves[h], :] = ut[2 * core, q_rm, halves[h], :] + op[h]
        c_rm[0][h].start()
        c_om[h].wait_recv()
        ut[2 * core + 1, q_rp, halves[h], :] = ut[2 * core + 1, q_rp, halves[h], :] + om[h]
        c_rp[1][h].start()
        if h == 0:
            c_rp[0][1].start()
            c_rm[1][1].start()
    for k in (k_pd, k_p, k_sd, k_s):
        l_step(k, False, 2)

    for u, (j, k) in enumerate(LOW):
        @pl.when(core != CORE_OF[j])
        def _():
            l_wait(u)
    for u in range(6):
        hi, lo = split(lt[u])
        lbh[u] = hi
        lbl[u] = lo

    def low(j, k):
        return lbh[LOW.index((j, k))], lbl[LOW.index((j, k))]

    away = 1 - yh
    c_yh = [remote(unit(z, away, h), yr.at[h], s_yh.at[h], r_yh.at[h], at(r=r_y2)) for h in range(2)]

    def z_sum(h):
        for u in range(2):
            c_rm[u][h].wait_recv()
            c_rp[u][h].wait_recv()
        ut[2 * core + away, z, halves[h], :] = (
            ut[2 * core + away, z, halves[h], :] + (rm[away, h] + rp[away, h]))
        c_yh[h].start()

    z_sum(0)

    @pl.when(col < S)
    def _():
        for k in (3, 2, 1, 0):
            acc = jnp.concatenate([pn[k, pl.ds(0, B), :] * zero, pn[k, pl.ds(B, B), :]], axis=0)
            for j in range(k + 1, S):
                acc = acc - dot3((pbh[j], pbl[j]), low(j, k))
            hi, lo = split(acc)
            pbh[k] = hi
            pbl[k] = lo
            hi, lo = split(acc.T)
            ph[k] = hi
            plo[k] = lo

    z_sum(1)

    dload.wait()

    @pl.when((row < S) & (col < S))
    def _():
        ones = (lax.broadcasted_iota(jnp.int32, (B, B), 0) == lax.broadcasted_iota(jnp.int32, (B, B), 1))
        for m in range(S):
            for k in range(S):
                if m < k:
                    mt[m, k] = jnp.zeros((B, B), F32)
                elif m == k:
                    mt[m, k] = ones.astype(F32)
                else:
                    acc = lt[LOW.index((m, k))]
                    for j in range(k + 1, m):
                        acc = acc + dot3(low(m, j), split(mt[j, k]))
                    mt[m, k] = -acc
        zo[...] = jnp.zeros((B, B), F32)
        for m in range(S):
            part = dot3(split(dv[m]), split(mt[m, col]))
            zo[...] = zo[...] + dot3(split(mt[m, row].T), split(part))

    for h in range(2):
        c_yh[h].wait_recv()
    total = ut[2 * core + yh, z] + jnp.concatenate([rm[yh, h] + rp[yh, h] + yr[h] for h in range(2)], axis=0)
    found = {}
    for k in (3, 2, 1, 0):
        acc = total[:, k * B:(k + 1) * B]
        for j in range(k + 1, S):
            acc = acc + dot3(found[j], low(j, k))
        xt[k] = -acc
        found[k] = split(-acc)
    c_xa = [remote(xt.at[k], xa.at[t_own, q_own, :], s_xa.at[k], r_xa.at[t_own, z], at(r=k)) for k in range(S)]
    c_xb = [remote(xt.at[k], xb.at[core, q_own, :], s_xb.at[k], r_xb.at[core, z], at(r=b_row, c=k)) for k in range(S)]

    def b_self(k):
        return (row == b_row) & (col == k)

    for k in (3, 2, 1, 0):
        @pl.when(jnp.logical_not(b_self(k)))
        def _():
            c_xb[k].start()

        @pl.when(b_self(k))
        def _():
            xb[core, q_own, :] = xt[k]
    for k in range(S):
        @pl.when(row != k)
        def _():
            c_xa[k].start()

        @pl.when(row == k)
        def _():
            xa[t_own, q_own, :] = xt[k]

    c_zc = remote(zp.at[1 - core], zc, s_zc, r_zc, at(r=r_core))
    c_zd = [remote(zp.at[core, :, pl.ds(((quad + d) % 8) * 32, 32), :], zr.at[d - 1], s_zd.at[d - 1], r_zd.at[d - 1],
                   at(r=((quad + d) % 8) * 2 + core)) for d in range(1, 8)]
    c_zf = [remote(zs.at[m], zf.at[pl.ds(quad * 32, 32), :], s_zf.at[m], r_zf.at[quad], at(r=2 * m + core))
            for m in range(2)]

    w_row = [pltpu.make_async_copy(xat.at[t], out.at[0, :, t, :], w_sem.at[t]) for t in range(4)]
    w_col = [pltpu.make_async_copy(xb.at[a], out.at[a, :, 0, :], w_sem.at[4 + a]) for a in range(2)]
    w_dia = pltpu.make_async_copy(zo, out.at[0, :, 0, :], w_sem.at[6])
    rows_new = [((row < S) & (col >= S), w_row[0])] + [(row < S, w_row[t]) for t in range(1, 4)]
    cols_new = [((col < S) & (row >= S), w_col[0]), (col < S, w_col[1])]
    writes = rows_new + cols_new + [((row < S) & (col < S), w_dia)]

    def diagonal(side):
        @pl.loop(0, 2)
        def _(m):
            zp[side, m] = dot3((ph[2 * m + side], plo[2 * m + side]), (xh[...], xl[...]))

    @pl.when(col < S)
    def _():
        for a in range(2):
            for q in range(4):
                @pl.when(b_other(a, q))
                def _():
                    remote(xt.at[0], xb.at[a, pl.ds(64 * q, 64), :], s_xb.at[0], r_xb.at[a, q], at(r=b_row)).wait_recv()
            hi, lo = split(xb[a])
            xh[pl.ds(a * B, B), :] = hi
            xl[pl.ds(a * B, B), :] = lo
        diagonal(1 - core)
        c_zc.start()
        diagonal(core)
        for cond, copy in cols_new:
            @pl.when(cond)
            def _():
                copy.start()
        c_zc.wait_recv()
        zp[core] = zp[core] + zc[...]
        for copy in c_zd:
            copy.start()
        acc = zp[core, :, pl.ds(quad * 32, 32), :]
        for d in range(7):
            c_zd[d].wait_recv()
            acc = acc + zr[d]
        zs[...] = acc
        for m in range(2):
            @pl.when(quad != m)
            def _():
                c_zf[m].start()

            @pl.when(quad == m)
            def _():
                zf[pl.ds(quad * 32, 32), :] = zs[m]

    @pl.when(row < S)
    def _():
        for t in range(4):
            for q in range(4):
                @pl.when(row != (t % 2) * 8 + q * 2 + t // 2)
                def _():
                    remote(xt.at[0], xa.at[t, pl.ds(64 * q, 64), :], s_xa.at[0], r_xa.at[t, q], at(r=r_core)).wait_recv()
            xat[t] = xa[t].T
        for cond, copy in rows_new:
            @pl.when(cond)
            def _():
                copy.start()

    @pl.when((row < S) & (col < S))
    def _():
        for q in range(8):
            @pl.when(quad != q)
            def _():
                remote(zs.at[0], zf.at[pl.ds(q * 32, 32), :], s_zf.at[0], r_zf.at[q], at(r=r_core)).wait_recv()
        zo[...] = zo[...] - zf[...]
        w_dia.start()

    @pl.when(source)
    def _():
        for ch in range(4):
            quarter(k_p, ch, s_out.at[ch], r_out.at[ch], to_o).wait_send()
        for ch in (1, 2, 3):
            quarter(k_pd, ch, s_out.at[3 + ch], r_out.at[3 + ch], to_o).wait_send()
            quarter(k_p, ch, s_y.at[ch], r_y.at[ch], to_y).wait_send()
        for ch in (0, 2):
            quarter(k_pd, ch, s_x.at[4 + ch // 2], r_x.at[4 + ch // 2], to_x).wait_send()

    @pl.when(inner)
    def _():
        for ch in (0, 2):
            quarter(k_s, ch, s_y.at[4 + ch], r_y.at[4 + ch], to_y).wait_send()
    for ch in range(4):
        quarter(k_p, ch, s_x.at[ch], r_x.at[ch], to_x).wait_send()
    quarter(k_p, 0, s_y.at[0], r_y.at[0], to_y).wait_send()
    for ch in (1, 3):
        quarter(k_s, ch, s_y.at[4 + ch], r_y.at[4 + ch], to_y).wait_send()
    for j, k in LOW:
        @pl.when(core == CORE_OF[j])
        def _():
            for cond, copy in l_routes(LOW.index((j, k)), j):
                @pl.when(cond)
                def _():
                    copy.wait_send()
    for copy in [core_copy(k) for k in range(S)] + c_op + c_om + c_rm[0] + c_rm[1] + c_rp[0] + c_rp[1] + c_yh:
        copy.wait_send()

    for k in range(S):
        @pl.when(jnp.logical_not(b_self(k)))
        def _():
            c_xb[k].wait_send()

        @pl.when(row != k)
        def _():
            c_xa[k].wait_send()

    @pl.when(col < S)
    def _():
        c_zc.wait_send()
        for copy in c_zd:
            copy.wait_send()
        for m in range(2):
            @pl.when(quad != m)
            def _():
                c_zf[m].wait_send()
    for cond, copy in writes + keeps:
        @pl.when(cond)
        def _():
            copy.wait()


def body(prior, lfac, tile_mask, dinv):
    def vmem(*shape, kind=F32):
        return pltpu.VMEM(shape, kind)

    dma = pltpu.SemaphoreType.DMA
    wide = S * B
    scratch = [
        vmem(4, 2 * B, B), vmem(4, B, 2 * B, kind=BF16), vmem(4, B, 2 * B, kind=BF16),
        vmem(2, B, B), vmem(4, 2 * B, B), vmem(4, 2 * B, B, kind=BF16), vmem(4, 2 * B, B, kind=BF16),
        vmem(4, B, 2 * B, kind=BF16), vmem(4, B, 2 * B, kind=BF16),
        vmem(6, B, B), vmem(6, B, B, kind=BF16), vmem(6, B, B, kind=BF16),
        vmem(4, 4, 64, wide), vmem(2, 4, 64, wide),
        vmem(2, 32, wide), vmem(2, 32, wide), vmem(2, 2, 32, wide), vmem(2, 2, 32, wide), vmem(2, 32, wide),
        vmem(4, 64, B), vmem(4, B, B), vmem(2, B, B), vmem(4, B, B),
        vmem(2 * B, B, kind=BF16), vmem(2 * B, B, kind=BF16),
        vmem(2, 2, B, B), vmem(2, B, B), vmem(7, 2, 32, B), vmem(2, 32, B), vmem(B, B),
        vmem(4, 4, B, B), vmem(4, B, B), vmem(B, B), pltpu.SMEM((32, 32), jnp.int32), dma,
        dma((2, 4)), dma((2,)), dma, dma((2, 4)), dma((7,)),
        dma((7,)), dma((7,)), dma((6,)), dma((6,)), dma((8,)), dma((8,)),
        dma((6, 4)), dma((6,)), dma((4,)), dma((4,)),
        dma((2, 2)), dma((2, 2)), dma((2, 2, 2)), dma((2, 2, 2)), dma((2,)), dma((2,)),
        dma((4,)), dma((4, 4)), dma((4,)), dma((2, 4)),
        dma, dma, dma((7,)), dma((7,)), dma((2,)), dma((8,)),
    ]
    return pl.pallas_call(
        kernel,
        out_shape=jax.ShapeDtypeStruct(prior.shape, F32),
        in_specs=[pl.BlockSpec(memory_space=pl.ANY), pl.BlockSpec(memory_space=pl.ANY),
                  pl.BlockSpec(memory_space=pl.ANY), pl.BlockSpec(memory_space=pl.ANY)],
        out_specs=pl.BlockSpec(memory_space=pl.ANY),
        scratch_shapes=scratch,
        compiler_params=pltpu.CompilerParams(
            collective_id=0, has_side_effects=True, vmem_limit_bytes=56 * 1024 * 1024),
    )(prior, lfac, tile_mask, dinv)


def solution(mesh):
    placed = (P("prow", None, "pcol", None), P("prow", None, "pcol", None), P(), P())
    return jax.shard_map(
        body, mesh=mesh, in_specs=placed, out_specs=P("prow", None, "pcol", None), check_vma=False
    )
```

```python
import jax
import jax.numpy as jnp
from jax import lax
from jax.experimental import pallas as pl
from jax.experimental.pallas import tpu as pltpu
from jax.sharding import PartitionSpec as P

B = 256
S = 4
F32 = jnp.float32
BF16 = jnp.bfloat16
MESH = pl.DeviceIdType.MESH
LOW = [(1, 0), (2, 0), (2, 1), (3, 0), (3, 1), (3, 2)]
CORE_OF = {1: 1, 2: 0, 3: 1}


def split(value):
    hi = value.astype(BF16)
    lo = (value - hi.astype(F32)).astype(BF16)
    return hi, lo


def dot3(a, b, dims=((1,), (0,))):
    def one(left, right):
        return lax.dot_general(left, right, (dims, ((), ())), preferred_element_type=F32)

    return one(a[0], b[0]) + (one(a[0], b[1]) + one(a[1], b[0]))


def kernel(prior, lfac, tile_mask, dinv, out,
           g32, gth, gtl, lt32, pn, pbh, pbl, ph, plo, lt, lbh, lbl, ut, cr, op, om, rm, rp, yr,
           yq, op1, om1, rm1, rp1, sums, xt, xa, xb, xat, xh, xl,
           zp, zc, zr, zs, zf, mt, dv, zo, mask, m_sem,
           g_sem, l_sem, d_sem, o_sem, w_sem,
           s_out, r_out, s_x, r_x, s_y, r_y,
           s_l, r_l, s_c, r_c, s_zo, r_zo, s_zr, r_zr, s_yh, r_yh, s_yq, r_yq, s_eo, r_eo, s_er, r_er,
           s_xa, r_xa, s_xb, r_xb, s_zc, r_zc, s_zd, r_zd, s_zf, r_zf):
    row = lax.axis_index("prow")
    col = lax.axis_index("pcol")
    yh, z, core = row // 8, (row // 2) % 4, row % 2
    x, yl = col // 2, col % 2
    quad = row // 2

    def at(r=None, c=None):
        return {"prow": row if r is None else r, "pcol": col if c is None else c}

    def remote(src, dst, ssem, rsem, where):
        return pltpu.make_async_remote_copy(
            src_ref=src, dst_ref=dst, send_sem=ssem, recv_sem=rsem, device_id=where, device_id_type=MESH)

    c_x = (x + 1 - 2 * (x % 2)) * 2 + yl
    c_y = x * 2 + 1 - yl
    c_o = (3 - x) * 2 + yl
    r_core = row + 1 - 2 * core
    r_zp = yh * 8 + ((z + 1) % 4) * 2 + core
    r_zm = yh * 8 + ((z + 3) % 4) * 2 + core
    r_y2 = (row + 8) % 16
    t_own = 2 * core + yh
    b_row = col + 8 * yh
    q_own = pl.ds(64 * z, 64)

    loads = []
    for a in range(2):
        for b in range(4):
            loads.append(pltpu.make_async_copy(prior.at[a, :, b, :], g32.at[b, pl.ds(a * B, B), :], g_sem.at[a, b]))
    keeps = []
    for a in range(2):
        for b in range(4):
            stays = row >= 0
            if a == 0:
                stays = stays & (row >= S)
            if b == 0:
                stays = stays & (col >= S)
            keeps.append((stays, pltpu.make_async_copy(
                g32.at[b, pl.ds(a * B, B), :], out.at[a, :, b, :], o_sem.at[a, b])))
    ltile = [pltpu.make_async_copy(lfac.at[a, :, 0, :], lt32.at[a], l_sem.at[a]) for a in range(2)]
    mload = pltpu.make_async_copy(tile_mask, mask, m_sem)
    dload = pltpu.make_async_copy(dinv, dv, d_sem)

    @pl.when(col < S)
    def _():
        mload.start()
        for copy in ltile:
            copy.start()
    for copy in loads:
        copy.start()
    dload.start()

    barrier = pltpu.get_barrier_semaphore()

    def greet(where):
        pl.semaphore_signal(barrier, inc=1, device_id=where, device_id_type=MESH)

    for step in range(1, 16):
        greet(at(r=(row + step) % 16))
    for c in (c_x, c_y, c_o):
        greet(at(c=c))
    greet(at(r=r_y2, c=c_y))

    def b_source(a, q):
        return yh * 8 + q * 2 + a, row % 8

    def b_other(a, q):
        sr, sc = b_source(a, q)
        return jnp.logical_not((sr == row) & (sc == col))

    for a in range(2):
        for q in range(4):
            sr, sc = b_source(a, q)

            @pl.when((col < S) & b_other(a, q))
            def _():
                greet(at(r=sr, c=sc))

    @pl.when(col < S)
    def _():
        mload.wait()
        for a in range(2):
            ltile[a].wait()
            live = mask[row + 16 * a, col] * (row + 16 * a > col).astype(jnp.int32)
            pn[col, pl.ds(a * B, B), :] = lt32[a] * live.astype(F32)

    pl.semaphore_wait(barrier, 19 + 4 - jnp.where((row == b_row) & (col < S), 1, 0))

    near = jnp.where((x == 0) | (x == 3), 0, 1)
    k_p, k_s = 2 * near + yl, 2 * (1 - near) + yl
    k_pd, k_sd = 2 * near + 1 - yl, 2 * (1 - near) + 1 - yl

    def quarter(k, ch, ssem, rsem, where):
        part = pn.at[k, pl.ds(128 * ch, 128), :]
        return remote(part, part, ssem, rsem, where)

    source, inner = x < 2, x >= 2
    always = row >= 0
    to_x, to_y, to_o = at(c=c_x), at(c=c_y), at(c=c_o)

    def out_recv(ch):
        quarter(k_p, ch, s_out.at[ch], r_out.at[ch], to_o).wait_recv()

    def x_recv(ch):
        quarter(k_s, ch, s_x.at[ch], r_x.at[ch], to_x).wait_recv()

    def y_recv(ch):
        quarter(k_pd, ch, s_y.at[ch], r_y.at[ch], to_y).wait_recv()

    def xd_recv(ch):
        quarter(k_sd, ch, s_x.at[4 + ch // 2], r_x.at[4 + ch // 2], to_x).wait_recv()

    def yd_recv(ch):
        quarter(k_sd, ch, s_y.at[4 + ch], r_y.at[4 + ch], to_y).wait_recv()

    def l_copy(u, slot, where):
        return remote(lt.at[u], lt.at[u], s_l.at[u, slot], r_l.at[u], where)

    def l_wait(u):
        l_copy(u, 0, at(r=r_core)).wait_recv()

    place = row % 8

    def l_routes(u, j):
        ahead, behind = {1: ((1, 3), (1,)), 2: ((2,), (2, 0)), 3: ((3, 5), (3,))}[j]
        plus = (place == ahead[0]) | (place == ahead[-1])
        minus = (place == behind[0]) | (place == behind[-1])
        return [(always, l_copy(u, 0, at(r=r_core))), (row == j, l_copy(u, 1, at(r=r_y2, c=c_y))),
                (plus, l_copy(u, 2, at(r=r_zp))), (minus, l_copy(u, 3, at(r=r_zm)))]

    def l_step(k, mine, rows=(2, 3, 1)):
        for j in rows:
            u = (j * (j - 1)) // 2 + k
            here = (core == CORE_OF[j]) & (k < j)

            @pl.when(here & (row == j) if mine is None else here & (row != j) & mine)
            def _():
                if mine is None:
                    lt[u] = pn[k, pl.ds(0, B), :]
                else:
                    l_wait(u)
                for cond, copy in l_routes(u, j):
                    @pl.when(cond)
                    def _():
                        copy.start()

    l_order = [jnp.where(yh == 0, a, b) for a, b in ((k_p, k_pd), (k_pd, k_p), (k_s, k_sd), (k_sd, k_s))]
    early, later, last = z == 1, (z == 0) | (z == 2), z == 3

    def p_out(ch):
        quarter(k_p, ch, s_out.at[ch], r_out.at[ch], to_o).start()

    def p_x(ch):
        quarter(k_p, ch, s_x.at[ch], r_x.at[ch], to_x).start()

    def p_y(ch):
        quarter(k_p, ch, s_y.at[ch], r_y.at[ch], to_y).start()

    def e_out(ch):
        quarter(k_pd, ch, s_out.at[3 + ch], r_out.at[3 + ch], to_o).start()

    def d_x(ch):
        quarter(k_pd, ch, s_x.at[4 + ch // 2], r_x.at[4 + ch // 2], to_x).start()

    def d_y(ch):
        quarter(k_s, ch, s_y.at[4 + ch], r_y.at[4 + ch], to_y).start()

    @pl.when(source)
    def _():
        for ch in range(3):
            p_out(ch)
            p_y(ch)
        p_x(0)
        p_x(1)
        l_step(k_p, None)

    for a in range(2):
        for b in range(4):
            loads[a * 4 + b].wait()
            cond, copy = keeps[a * 4 + b]

            @pl.when(cond)
            def _():
                copy.start()
    for b in range(4):
        for a in range(2):
            hi, lo = split(g32[b, pl.ds(a * B, B), :].T)
            gth[b, :, pl.ds(a * B, B)] = hi
            gtl[b, :, pl.ds(a * B, B)] = lo

    zero = jnp.where(row < S, 0.0, 1.0).astype(F32)

    def core_copy(k):
        lanes = pl.ds(pl.multiple_of(k * B, B), B)
        return remote(ut.at[pl.ds(2 - 2 * core, 2), :, :, lanes], cr.at[:, :, :, lanes], s_c.at[k], r_c.at[k], at(r=r_core))

    def products(k):
        for a in range(2):
            rows = pl.ds(a * B, B)
            hi, lo = split(pn[k, rows, :] * zero if a == 0 else pn[k, rows, :])
            pbh[k, rows, :] = hi
            pbl[k, rows, :] = lo

        @pl.loop(0, 4)
        def _(step):
            t = lax.rem(2 - 2 * core + step, 4)
            value = dot3((gth[t], gtl[t]), (pbh[k], pbl[k]))
            for q in range(4):
                ut[t, q, :, pl.ds(pl.multiple_of(k * B, B), B)] = value[q * 64:(q + 1) * 64]
        core_copy(k).start()

    @pl.when(source)
    def _():
        products(k_p)
        y_recv(0)
        d_x(0)
        p_x(2)
        p_out(3)
        y_recv(1)
        e_out(1)
        p_x(3)
        x_recv(0)
        x_recv(1)
        d_y(1)
        p_y(3)
        l_step(k_pd, None)
        l_step(k_s, None)
        y_recv(2)
        d_x(2)
        e_out(2)
        xd_recv(0)
        yd_recv(1)
        l_step(k_sd, None)

    @pl.when(inner)
    def _():
        out_recv(0)
        p_x(0)
        p_y(0)
        out_recv(1)
        p_x(1)
        l_step(k_p, None)
        x_recv(0)
        d_y(0)
        out_recv(2)
        p_x(2)
        x_recv(1)
        d_y(1)
        l_step(k_s, None)
        out_recv(3)
        p_x(3)
        products(k_p)
    l_step(l_order[0], early, (2, 3))

    @pl.when(source)
    def _():
        y_recv(3)
        e_out(3)
        x_recv(2)
        x_recv(3)
        d_y(3)

    @pl.when(inner)
    def _():
        x_recv(2)
        d_y(2)
        y_recv(0)
        quarter(k_pd, 1, s_out.at[4], r_out.at[4], to_o).wait_recv()
        l_step(k_pd, None)
        yd_recv(0)
        yd_recv(1)
        l_step(k_sd, None)
        x_recv(3)
        d_y(3)
    l_step(l_order[1], early, (2, 3))
    l_step(l_order[2], early, (2, 3))
    l_step(l_order[0], later, (2, 3))
    products(k_s)

    @pl.when(inner)
    def _():
        for ch in (2, 3):
            quarter(k_pd, ch, s_out.at[3 + ch], r_out.at[3 + ch], to_o).wait_recv()
    products(k_pd)
    l_step(l_order[3], early, (2, 3))
    l_step(l_order[1], later, (2, 3))
    l_step(0, row == 9, (1,))

    @pl.when(source)
    def _():
        xd_recv(2)

    @pl.when(inner)
    def _():
        yd_recv(2)
    yd_recv(3)
    products(k_sd)

    top, end = pl.ds(0, 32), pl.ds(32, 32)
    low16, high16 = pl.ds(32, 16), pl.ds(48, 16)
    q_op, q_rm, q_rp = (z + 2) % 4, (z + 1) % 4, (z + 3) % 4
    away = 1 - yh
    t_away = 2 * core + away

    def unit(q, u):
        return ut.at[2 * core + u, q, top, :]

    c_op = remote(unit(q_op, 0), op, s_zo.at[0], r_zo.at[0], at(r=r_zp))
    c_om = remote(unit(q_op, 1), om, s_zo.at[1], r_zo.at[1], at(r=r_zm))
    c_rm = [remote(unit(q_rm, u), rm.at[u], s_zr.at[0, u], r_zr.at[0, u], at(r=r_zp)) for u in range(2)]
    c_rp = [remote(unit(q_rp, u), rp.at[u], s_zr.at[1, u], r_zr.at[1, u], at(r=r_zm)) for u in range(2)]
    c_yh = remote(unit(z, away), yr, s_yh, r_yh, at(r=r_y2))

    def y_copy(q):
        return remote(ut.at[t_away, q, end, :], yq.at[q], s_yq.at[q], r_yq.at[q], at(r=r_y2))

    def y_add(q):
        y_copy(q).wait_recv()
        ut[t_own, q, end, :] = ut[t_own, q, end, :] + yq[q]

    e_op = remote(ut.at[t_own, q_op, low16, :], op1, s_eo.at[0], r_eo.at[0], at(r=r_zp))
    e_om = remote(ut.at[t_own, q_op, high16, :], om1, s_eo.at[1], r_eo.at[1], at(r=r_zm))
    e_rm = [remote(ut.at[t_own, q_rm, part, :], rm1.at[n], s_er.at[0, n], r_er.at[0, n], at(r=r_zp))
            for n, part in enumerate((low16, high16))]
    e_rp = [remote(ut.at[t_own, q_rp, part, :], rp1.at[n], s_er.at[1, n], r_er.at[1, n], at(r=r_zm))
            for n, part in enumerate((low16, high16))]

    def core_add(q):
        for u in range(2):
            ut[2 * core + u, q] = ut[2 * core + u, q] + cr[u, q]

    for k in range(S):
        core_copy(k).wait_recv()
    core_add(q_op)
    c_op.start()
    c_om.start()
    y_copy(q_op).start()
    core_add(q_rm)
    c_rm[1].start()
    y_copy(q_rm).start()
    core_add(q_rp)
    c_rp[0].start()
    y_copy(q_rp).start()
    core_add(z)
    y_copy(z).start()
    l_step(l_order[2], later, (2, 3))
    c_op.wait_recv()
    ut[2 * core, q_rm, top, :] = ut[2 * core, q_rm, top, :] + op[...]
    c_rm[0].start()
    c_om.wait_recv()
    ut[2 * core + 1, q_rp, top, :] = ut[2 * core + 1, q_rp, top, :] + om[...]
    c_rp[1].start()
    y_add(q_op)
    e_op.start()
    e_om.start()
    y_add(q_rm)
    e_rm[1].start()
    y_add(q_rp)
    e_rp[0].start()
    l_step(l_order[3], later, (2, 3))
    l_step(0, place == 3, (1,))
    e_op.wait_recv()
    ut[t_own, q_rm, low16, :] = ut[t_own, q_rm, low16, :] + op1[...]
    e_rm[0].start()
    e_om.wait_recv()
    ut[t_own, q_rp, high16, :] = ut[t_own, q_rp, high16, :] + om1[...]
    e_rp[1].start()
    for u in range(2):
        c_rm[u].wait_recv()
        c_rp[u].wait_recv()
    ut[t_away, z, top, :] = ut[t_away, z, top, :] + (rm[away] + rp[away])
    c_yh.start()
    for n in range(4):
        l_step(l_order[n], last, (2, 3))
    l_step(0, (row != 9) & (place != 3), (1,))

    y_add(z)
    for n in range(2):
        e_rm[n].wait_recv()
        e_rp[n].wait_recv()
    sums[pl.ds(32, 32), :] = ut[t_own, z, end, :] + jnp.concatenate([rm1[n] + rp1[n] for n in range(2)], axis=0)
    c_yh.wait_recv()
    sums[pl.ds(0, 32), :] = ut[t_own, z, top, :] + (rm[yh] + rp[yh] + yr[...])

    for u, (j, k) in enumerate(LOW):
        @pl.when(core != CORE_OF[j])
        def _():
            l_wait(u)

    def low(j, k):
        return lbh[LOW.index((j, k))], lbl[LOW.index((j, k))]

    for m, k in [(1, 0), (2, 1), (3, 2), (2, 0), (3, 1), (3, 0)]:
        u = LOW.index((m, k))
        acc = lt[u]
        for j in range(k + 1, m):
            acc = acc + dot3(split(lt[LOW.index((m, j))]), low(j, k))
        mt[m, k] = -acc
        hi, lo = split(-acc)
        lbh[u] = hi
        lbl[u] = lo

    parts = [split(sums[:, pl.ds(k * B, B)]) for k in range(S)]
    for k in range(S):
        acc = sums[:, pl.ds(k * B, B)]
        for j in range(k + 1, S):
            acc = acc + dot3(parts[j], low(j, k))
        xt[k] = -acc
    c_xa = [remote(xt.at[k], xa.at[t_own, q_own, :], s_xa.at[k], r_xa.at[t_own, z], at(r=k)) for k in range(S)]
    c_xb = [remote(xt.at[k], xb.at[core, q_own, :], s_xb.at[k], r_xb.at[core, z], at(r=b_row, c=k)) for k in range(S)]

    def b_self(k):
        return (row == b_row) & (col == k)

    for k in (3, 2, 1, 0):
        @pl.when(jnp.logical_not(b_self(k)))
        def _():
            c_xb[k].start()

        @pl.when(b_self(k))
        def _():
            xb[core, q_own, :] = xt[k]
    for k in range(S):
        @pl.when(row != k)
        def _():
            c_xa[k].start()

        @pl.when(row == k)
        def _():
            xa[t_own, q_own, :] = xt[k]

    @pl.when(col < S)
    def _():
        for k in range(S):
            acc = jnp.concatenate([pn[k, pl.ds(0, B), :] * zero, pn[k, pl.ds(B, B), :]], axis=0)
            for j in range(k + 1, S):
                acc = acc + dot3((pbh[j], pbl[j]), low(j, k))
            hi, lo = split(acc.T)
            ph[k] = hi
            plo[k] = lo

    dload.wait()

    @pl.when((row < S) & (col < S))
    def _():
        ones = (lax.broadcasted_iota(jnp.int32, (B, B), 0) == lax.broadcasted_iota(jnp.int32, (B, B), 1))
        for m in range(S):
            mt[m, m] = ones.astype(F32)
            for k in range(m + 1, S):
                mt[m, k] = jnp.zeros((B, B), F32)
        zo[...] = jnp.zeros((B, B), F32)
        for m in range(S):
            part = dot3(split(dv[m]), split(mt[m, col]))
            zo[...] = zo[...] + dot3(split(mt[m, row].T), split(part))

    c_zc = remote(zp.at[1 - core], zc, s_zc, r_zc, at(r=r_core))
    c_zd = [remote(zp.at[core, :, pl.ds(((quad + d) % 8) * 32, 32), :], zr.at[d - 1], s_zd.at[d - 1], r_zd.at[d - 1],
                   at(r=((quad + d) % 8) * 2 + core)) for d in range(1, 8)]
    c_zf = [remote(zs.at[m], zf.at[pl.ds(quad * 32, 32), :], s_zf.at[m], r_zf.at[quad], at(r=2 * m + core))
            for m in range(2)]

    w_row = [pltpu.make_async_copy(xat.at[t], out.at[0, :, t, :], w_sem.at[t]) for t in range(4)]
    w_col = [pltpu.make_async_copy(xb.at[a], out.at[a, :, 0, :], w_sem.at[4 + a]) for a in range(2)]
    w_dia = pltpu.make_async_copy(zo, out.at[0, :, 0, :], w_sem.at[6])
    rows_new = [((row < S) & (col >= S), w_row[0])] + [(row < S, w_row[t]) for t in range(1, 4)]
    cols_new = [((col < S) & (row >= S), w_col[0]), (col < S, w_col[1])]
    writes = rows_new + cols_new + [((row < S) & (col < S), w_dia)]

    def diagonal(side):
        @pl.loop(0, 2)
        def _(m):
            zp[side, m] = dot3((ph[2 * m + side], plo[2 * m + side]), (xh[...], xl[...]))

    @pl.when(col < S)
    def _():
        for a in range(2):
            for q in range(4):
                @pl.when(b_other(a, q))
                def _():
                    remote(xt.at[0], xb.at[a, pl.ds(64 * q, 64), :], s_xb.at[0], r_xb.at[a, q], at(r=b_row)).wait_recv()
            hi, lo = split(xb[a])
            xh[pl.ds(a * B, B), :] = hi
            xl[pl.ds(a * B, B), :] = lo
        diagonal(1 - core)
        c_zc.start()
        diagonal(core)
        for cond, copy in cols_new:
            @pl.when(cond)
            def _():
                copy.start()
        c_zc.wait_recv()
        zp[core] = zp[core] + zc[...]
        for copy in c_zd:
            copy.start()
        acc = zp[core, :, pl.ds(quad * 32, 32), :]
        for d in range(7):
            c_zd[d].wait_recv()
            acc = acc + zr[d]
        zs[...] = acc
        for m in range(2):
            @pl.when(quad != m)
            def _():
                c_zf[m].start()

            @pl.when(quad == m)
            def _():
                zf[pl.ds(quad * 32, 32), :] = zs[m]

    @pl.when(row < S)
    def _():
        for t in range(4):
            for q in range(4):
                @pl.when(row != (t % 2) * 8 + q * 2 + t // 2)
                def _():
                    remote(xt.at[0], xa.at[t, pl.ds(64 * q, 64), :], s_xa.at[0], r_xa.at[t, q], at(r=r_core)).wait_recv()
            xat[t] = xa[t].T
        for cond, copy in rows_new:
            @pl.when(cond)
            def _():
                copy.start()

    @pl.when((row < S) & (col < S))
    def _():
        for q in range(8):
            @pl.when(quad != q)
            def _():
                remote(zs.at[0], zf.at[pl.ds(q * 32, 32), :], s_zf.at[0], r_zf.at[q], at(r=r_core)).wait_recv()
        zo[...] = zo[...] - zf[...]
        w_dia.start()

    @pl.when(source)
    def _():
        for ch in range(4):
            quarter(k_p, ch, s_out.at[ch], r_out.at[ch], to_o).wait_send()
        for ch in (1, 2, 3):
            quarter(k_pd, ch, s_out.at[3 + ch], r_out.at[3 + ch], to_o).wait_send()
            quarter(k_p, ch, s_y.at[ch], r_y.at[ch], to_y).wait_send()
        for ch in (0, 2):
            quarter(k_pd, ch, s_x.at[4 + ch // 2], r_x.at[4 + ch // 2], to_x).wait_send()

    @pl.when(inner)
    def _():
        for ch in (0, 2):
            quarter(k_s, ch, s_y.at[4 + ch], r_y.at[4 + ch], to_y).wait_send()
    for ch in range(4):
        quarter(k_p, ch, s_x.at[ch], r_x.at[ch], to_x).wait_send()
    quarter(k_p, 0, s_y.at[0], r_y.at[0], to_y).wait_send()
    for ch in (1, 3):
        quarter(k_s, ch, s_y.at[4 + ch], r_y.at[4 + ch], to_y).wait_send()
    for j, k in LOW:
        @pl.when(core == CORE_OF[j])
        def _():
            for cond, copy in l_routes(LOW.index((j, k)), j):
                @pl.when(cond)
                def _():
                    copy.wait_send()
    for copy in [core_copy(k) for k in range(S)] + [y_copy(k) for k in range(4)] + [c_op, c_om, c_yh, e_op, e_om]:
        copy.wait_send()
    for copy in c_rm + c_rp + e_rm + e_rp:
        copy.wait_send()

    for k in range(S):
        @pl.when(jnp.logical_not(b_self(k)))
        def _():
            c_xb[k].wait_send()

        @pl.when(row != k)
        def _():
            c_xa[k].wait_send()

    @pl.when(col < S)
    def _():
        c_zc.wait_send()
        for copy in c_zd:
            copy.wait_send()
        for m in range(2):
            @pl.when(quad != m)
            def _():
                c_zf[m].wait_send()
    for cond, copy in writes + keeps:
        @pl.when(cond)
        def _():
            copy.wait()


def body(prior, lfac, tile_mask, dinv):
    def vmem(*shape, kind=F32):
        return pltpu.VMEM(shape, kind)

    dma = pltpu.SemaphoreType.DMA
    wide = S * B
    scratch = [
        vmem(4, 2 * B, B), vmem(4, B, 2 * B, kind=BF16), vmem(4, B, 2 * B, kind=BF16),
        vmem(2, B, B), vmem(4, 2 * B, B), vmem(4, 2 * B, B, kind=BF16), vmem(4, 2 * B, B, kind=BF16),
        vmem(4, B, 2 * B, kind=BF16), vmem(4, B, 2 * B, kind=BF16),
        vmem(6, B, B), vmem(6, B, B, kind=BF16), vmem(6, B, B, kind=BF16),
        vmem(4, 4, 64, wide), vmem(2, 4, 64, wide),
        vmem(32, wide), vmem(32, wide), vmem(2, 32, wide), vmem(2, 32, wide), vmem(32, wide),
        vmem(4, 32, wide), vmem(16, wide), vmem(16, wide), vmem(2, 16, wide), vmem(2, 16, wide), vmem(64, wide),
        vmem(4, 64, B), vmem(4, B, B), vmem(2, B, B), vmem(4, B, B),
        vmem(2 * B, B, kind=BF16), vmem(2 * B, B, kind=BF16),
        vmem(2, 2, B, B), vmem(2, B, B), vmem(7, 2, 32, B), vmem(2, 32, B), vmem(B, B),
        vmem(4, 4, B, B), vmem(4, B, B), vmem(B, B), pltpu.SMEM((32, 32), jnp.int32), dma,
        dma((2, 4)), dma((2,)), dma, dma((2, 4)), dma((7,)),
        dma((7,)), dma((7,)), dma((6,)), dma((6,)), dma((8,)), dma((8,)),
        dma((6, 4)), dma((6,)), dma((4,)), dma((4,)),
        dma((2,)), dma((2,)), dma((2, 2)), dma((2, 2)), dma, dma,
        dma((4,)), dma((4,)), dma((2,)), dma((2,)), dma((2, 2)), dma((2, 2)),
        dma((4,)), dma((4, 4)), dma((4,)), dma((2, 4)),
        dma, dma, dma((7,)), dma((7,)), dma((2,)), dma((8,)),
    ]
    return pl.pallas_call(
        kernel,
        out_shape=jax.ShapeDtypeStruct(prior.shape, F32),
        in_specs=[pl.BlockSpec(memory_space=pl.ANY), pl.BlockSpec(memory_space=pl.ANY),
                  pl.BlockSpec(memory_space=pl.ANY), pl.BlockSpec(memory_space=pl.ANY)],
        out_specs=pl.BlockSpec(memory_space=pl.ANY),
        scratch_shapes=scratch,
        compiler_params=pltpu.CompilerParams(
            collective_id=0, has_side_effects=True, vmem_limit_bytes=56 * 1024 * 1024),
    )(prior, lfac, tile_mask, dinv)


def solution(mesh):
    placed = (P("prow", None, "pcol", None), P("prow", None, "pcol", None), P(), P())
    return jax.shard_map(
        body, mesh=mesh, in_specs=placed, out_specs=P("prow", None, "pcol", None), check_vma=False
    )
```

```python
import jax
import jax.numpy as jnp
from jax import lax
from jax.experimental import pallas as pl
from jax.experimental.pallas import tpu as pltpu
from jax.sharding import PartitionSpec as P

B = 256
S = 4
F32 = jnp.float32
BF16 = jnp.bfloat16
MESH = pl.DeviceIdType.MESH
LOW = [(1, 0), (2, 0), (2, 1), (3, 0), (3, 1), (3, 2)]
LATE = 32
TOP = 64 - LATE
HALF = LATE // 2
CORE_OF = {1: 1, 2: 0, 3: 1}


def split(value):
    hi = value.astype(BF16)
    lo = (value - hi.astype(F32)).astype(BF16)
    return hi, lo


def dot3(a, b, dims=((1,), (0,))):
    def one(left, right):
        return lax.dot_general(left, right, (dims, ((), ())), preferred_element_type=F32)

    return one(a[0], b[0]) + (one(a[0], b[1]) + one(a[1], b[0]))


def kernel(prior, lfac, tile_mask, dinv, out,
           g32, gth, gtl, lt32, pn, pbh, pbl, ph, plo, lt, lbh, lbl, ut, cr, op, om, rm, rp, yr,
           yq, op1, om1, rm1, rp1, sums, xt, xa, xb, xat, xh, xl,
           zp, zc, zr, zs, zf, mt, dv, zo, mask, m_sem,
           g_sem, l_sem, d_sem, o_sem, w_sem,
           s_out, r_out, s_x, r_x, s_y, r_y,
           s_l, r_l, s_c, r_c, s_zo, r_zo, s_zr, r_zr, s_yh, r_yh, s_yq, r_yq, s_eo, r_eo, s_er, r_er,
           s_xa, r_xa, s_xb, r_xb, s_zc, r_zc, s_zd, r_zd, s_zf, r_zf):
    row = lax.axis_index("prow")
    col = lax.axis_index("pcol")
    yh, z, core = row // 8, (row // 2) % 4, row % 2
    x, yl = col // 2, col % 2
    quad = row // 2

    def at(r=None, c=None):
        return {"prow": row if r is None else r, "pcol": col if c is None else c}

    def remote(src, dst, ssem, rsem, where):
        return pltpu.make_async_remote_copy(
            src_ref=src, dst_ref=dst, send_sem=ssem, recv_sem=rsem, device_id=where, device_id_type=MESH)

    c_x = (x + 1 - 2 * (x % 2)) * 2 + yl
    c_y = x * 2 + 1 - yl
    c_o = (3 - x) * 2 + yl
    r_core = row + 1 - 2 * core
    r_zp = yh * 8 + ((z + 1) % 4) * 2 + core
    r_zm = yh * 8 + ((z + 3) % 4) * 2 + core
    r_y2 = (row + 8) % 16
    t_own = 2 * core + yh
    b_row = col + 8 * yh
    q_own = pl.ds(64 * z, 64)

    loads = []
    for a in range(2):
        for b in range(4):
            loads.append(pltpu.make_async_copy(prior.at[a, :, b, :], g32.at[b, pl.ds(a * B, B), :], g_sem.at[a, b]))
    keeps = []
    for a in range(2):
        for b in range(4):
            stays = row >= 0
            if a == 0:
                stays = stays & (row >= S)
            if b == 0:
                stays = stays & (col >= S)
            keeps.append((stays, pltpu.make_async_copy(
                g32.at[b, pl.ds(a * B, B), :], out.at[a, :, b, :], o_sem.at[a, b])))
    ltile = [pltpu.make_async_copy(lfac.at[a, :, 0, :], lt32.at[a], l_sem.at[a]) for a in range(2)]
    mload = pltpu.make_async_copy(tile_mask, mask, m_sem)
    dload = pltpu.make_async_copy(dinv, dv, d_sem)

    @pl.when(col < S)
    def _():
        mload.start()
        for copy in ltile:
            copy.start()
    for copy in loads:
        copy.start()
    dload.start()

    barrier = pltpu.get_barrier_semaphore()

    def greet(where):
        pl.semaphore_signal(barrier, inc=1, device_id=where, device_id_type=MESH)

    for step in range(1, 16):
        greet(at(r=(row + step) % 16))
    for c in (c_x, c_y, c_o):
        greet(at(c=c))
    greet(at(r=r_y2, c=c_y))

    def b_source(a, q):
        return yh * 8 + q * 2 + a, row % 8

    def b_other(a, q):
        sr, sc = b_source(a, q)
        return jnp.logical_not((sr == row) & (sc == col))

    for a in range(2):
        for q in range(4):
            sr, sc = b_source(a, q)

            @pl.when((col < S) & b_other(a, q))
            def _():
                greet(at(r=sr, c=sc))

    @pl.when(col < S)
    def _():
        mload.wait()
        for a in range(2):
            ltile[a].wait()
            live = mask[row + 16 * a, col] * (row + 16 * a > col).astype(jnp.int32)
            pn[col, pl.ds(a * B, B), :] = lt32[a] * live.astype(F32)

    pl.semaphore_wait(barrier, 19 + 4 - jnp.where((row == b_row) & (col < S), 1, 0))

    near = jnp.where((x == 0) | (x == 3), 0, 1)
    k_p, k_s = 2 * near + yl, 2 * (1 - near) + yl
    k_pd, k_sd = 2 * near + 1 - yl, 2 * (1 - near) + 1 - yl

    def quarter(k, ch, ssem, rsem, where):
        part = pn.at[k, pl.ds(128 * ch, 128), :]
        return remote(part, part, ssem, rsem, where)

    source, inner = x < 2, x >= 2
    always = row >= 0
    to_x, to_y, to_o = at(c=c_x), at(c=c_y), at(c=c_o)

    def out_recv(ch):
        quarter(k_p, ch, s_out.at[ch], r_out.at[ch], to_o).wait_recv()

    def x_recv(ch):
        quarter(k_s, ch, s_x.at[ch], r_x.at[ch], to_x).wait_recv()

    def y_recv(ch):
        quarter(k_pd, ch, s_y.at[ch], r_y.at[ch], to_y).wait_recv()

    def xd_recv(ch):
        quarter(k_sd, ch, s_x.at[4 + ch // 2], r_x.at[4 + ch // 2], to_x).wait_recv()

    def yd_recv(ch):
        quarter(k_sd, ch, s_y.at[4 + ch], r_y.at[4 + ch], to_y).wait_recv()

    def l_copy(u, slot, where):
        return remote(lt.at[u], lt.at[u], s_l.at[u, slot], r_l.at[u], where)

    def l_wait(u):
        l_copy(u, 0, at(r=r_core)).wait_recv()

    place = row % 8

    def l_routes(u, j):
        ahead, behind = {1: ((1, 3), (1,)), 2: ((2,), (2, 0)), 3: ((3, 5), (3,))}[j]
        plus = (place == ahead[0]) | (place == ahead[-1])
        minus = (place == behind[0]) | (place == behind[-1])
        return [(always, l_copy(u, 0, at(r=r_core))), (row == j, l_copy(u, 1, at(r=r_y2, c=c_y))),
                (plus, l_copy(u, 2, at(r=r_zp))), (minus, l_copy(u, 3, at(r=r_zm)))]

    def l_step(k, mine, rows=(2, 3, 1)):
        for j in rows:
            u = (j * (j - 1)) // 2 + k
            here = (core == CORE_OF[j]) & (k < j)

            @pl.when(here & (row == j) if mine is None else here & (row != j) & mine)
            def _():
                if mine is None:
                    lt[u] = pn[k, pl.ds(0, B), :]
                else:
                    l_wait(u)
                for cond, copy in l_routes(u, j):
                    @pl.when(cond)
                    def _():
                        copy.start()

    l_order = [jnp.where(yh == 0, a, b) for a, b in ((k_p, k_pd), (k_pd, k_p), (k_s, k_sd), (k_sd, k_s))]
    early, later, last = z == 1, (z == 0) | (z == 2), z == 3

    def p_out(ch):
        quarter(k_p, ch, s_out.at[ch], r_out.at[ch], to_o).start()

    def p_x(ch):
        quarter(k_p, ch, s_x.at[ch], r_x.at[ch], to_x).start()

    def p_y(ch):
        quarter(k_p, ch, s_y.at[ch], r_y.at[ch], to_y).start()

    def e_out(ch):
        quarter(k_pd, ch, s_out.at[3 + ch], r_out.at[3 + ch], to_o).start()

    def d_x(ch):
        quarter(k_pd, ch, s_x.at[4 + ch // 2], r_x.at[4 + ch // 2], to_x).start()

    def d_y(ch):
        quarter(k_s, ch, s_y.at[4 + ch], r_y.at[4 + ch], to_y).start()

    @pl.when(source)
    def _():
        for ch in range(3):
            p_out(ch)
            p_y(ch)
        p_x(0)
        p_x(1)
        l_step(k_p, None)

    for a in range(2):
        for b in range(4):
            loads[a * 4 + b].wait()
            cond, copy = keeps[a * 4 + b]

            @pl.when(cond)
            def _():
                copy.start()
    for b in range(4):
        for a in range(2):
            hi, lo = split(g32[b, pl.ds(a * B, B), :].T)
            gth[b, :, pl.ds(a * B, B)] = hi
            gtl[b, :, pl.ds(a * B, B)] = lo

    zero = jnp.where(row < S, 0.0, 1.0).astype(F32)

    def core_copy(k):
        lanes = pl.ds(pl.multiple_of(k * B, B), B)
        return remote(ut.at[pl.ds(2 - 2 * core, 2), :, :, lanes], cr.at[:, :, :, lanes], s_c.at[k], r_c.at[k], at(r=r_core))

    def products(k):
        for a in range(2):
            rows = pl.ds(a * B, B)
            hi, lo = split(pn[k, rows, :] * zero if a == 0 else pn[k, rows, :])
            pbh[k, rows, :] = hi
            pbl[k, rows, :] = lo

        @pl.loop(0, 4)
        def _(step):
            t = lax.rem(2 - 2 * core + step, 4)
            value = dot3((gth[t], gtl[t]), (pbh[k], pbl[k]))
            for q in range(4):
                ut[t, q, :, pl.ds(pl.multiple_of(k * B, B), B)] = value[q * 64:(q + 1) * 64]
        core_copy(k).start()

    @pl.when(source)
    def _():
        products(k_p)
        y_recv(0)
        d_x(0)
        p_x(2)
        p_out(3)
        y_recv(1)
        e_out(1)
        p_x(3)
        x_recv(0)
        x_recv(1)
        d_y(1)
        p_y(3)
        l_step(k_pd, None)
        l_step(k_s, None)
        y_recv(2)
        d_x(2)
        e_out(2)
        xd_recv(0)
        yd_recv(1)
        l_step(k_sd, None)

    @pl.when(inner)
    def _():
        out_recv(0)
        p_x(0)
        p_y(0)
        out_recv(1)
        p_x(1)
        l_step(k_p, None)
        x_recv(0)
        d_y(0)
        out_recv(2)
        p_x(2)
        x_recv(1)
        d_y(1)
        l_step(k_s, None)
        out_recv(3)
        p_x(3)
        products(k_p)
    l_step(l_order[0], early, (2, 3))

    @pl.when(source)
    def _():
        y_recv(3)
        e_out(3)
        x_recv(2)
        x_recv(3)
        d_y(3)

    @pl.when(inner)
    def _():
        x_recv(2)
        d_y(2)
        y_recv(0)
        quarter(k_pd, 1, s_out.at[4], r_out.at[4], to_o).wait_recv()
        l_step(k_pd, None)
        yd_recv(0)
        yd_recv(1)
        l_step(k_sd, None)
        x_recv(3)
        d_y(3)
    l_step(l_order[1], early, (2, 3))
    l_step(l_order[2], early, (2, 3))
    l_step(l_order[0], later, (2, 3))
    products(k_s)

    @pl.when(inner)
    def _():
        for ch in (2, 3):
            quarter(k_pd, ch, s_out.at[3 + ch], r_out.at[3 + ch], to_o).wait_recv()
    products(k_pd)
    l_step(l_order[3], early, (2, 3))
    l_step(l_order[1], later, (2, 3))
    l_step(0, row == 9, (1,))

    @pl.when(source)
    def _():
        xd_recv(2)

    @pl.when(inner)
    def _():
        yd_recv(2)
    yd_recv(3)
    products(k_sd)

    top, end = pl.ds(0, TOP), pl.ds(TOP, LATE)
    low_half, high_half = pl.ds(TOP, HALF), pl.ds(TOP + HALF, HALF)
    q_op, q_rm, q_rp = (z + 2) % 4, (z + 1) % 4, (z + 3) % 4
    away = 1 - yh
    t_away = 2 * core + away

    def unit(q, u):
        return ut.at[2 * core + u, q, top, :]

    c_op = remote(unit(q_op, 0), op, s_zo.at[0], r_zo.at[0], at(r=r_zp))
    c_om = remote(unit(q_op, 1), om, s_zo.at[1], r_zo.at[1], at(r=r_zm))
    c_rm = [remote(unit(q_rm, u), rm.at[u], s_zr.at[0, u], r_zr.at[0, u], at(r=r_zp)) for u in range(2)]
    c_rp = [remote(unit(q_rp, u), rp.at[u], s_zr.at[1, u], r_zr.at[1, u], at(r=r_zm)) for u in range(2)]
    c_yh = remote(unit(z, away), yr, s_yh, r_yh, at(r=r_y2))

    def y_copy(q):
        return remote(ut.at[t_away, q, end, :], yq.at[q], s_yq.at[q], r_yq.at[q], at(r=r_y2))

    def y_add(q):
        y_copy(q).wait_recv()
        ut[t_own, q, end, :] = ut[t_own, q, end, :] + yq[q]

    e_op = remote(ut.at[t_own, q_op, low_half, :], op1, s_eo.at[0], r_eo.at[0], at(r=r_zp))
    e_om = remote(ut.at[t_own, q_op, high_half, :], om1, s_eo.at[1], r_eo.at[1], at(r=r_zm))
    e_rm = [remote(ut.at[t_own, q_rm, part, :], rm1.at[n], s_er.at[0, n], r_er.at[0, n], at(r=r_zp))
            for n, part in enumerate((low_half, high_half))]
    e_rp = [remote(ut.at[t_own, q_rp, part, :], rp1.at[n], s_er.at[1, n], r_er.at[1, n], at(r=r_zm))
            for n, part in enumerate((low_half, high_half))]

    def core_add(q):
        for u in range(2):
            ut[2 * core + u, q] = ut[2 * core + u, q] + cr[u, q]

    for k in range(S):
        core_copy(k).wait_recv()
    core_add(q_op)
    c_op.start()
    c_om.start()
    y_copy(q_op).start()
    core_add(q_rm)
    c_rm[1].start()
    y_copy(q_rm).start()
    core_add(q_rp)
    c_rp[0].start()
    y_copy(q_rp).start()
    core_add(z)
    y_copy(z).start()
    l_step(l_order[2], later, (2, 3))
    c_op.wait_recv()
    ut[2 * core, q_rm, top, :] = ut[2 * core, q_rm, top, :] + op[...]
    c_rm[0].start()
    c_om.wait_recv()
    ut[2 * core + 1, q_rp, top, :] = ut[2 * core + 1, q_rp, top, :] + om[...]
    c_rp[1].start()
    y_add(q_op)
    e_op.start()
    e_om.start()
    y_add(q_rm)
    e_rm[1].start()
    y_add(q_rp)
    e_rp[0].start()
    l_step(l_order[3], later, (2, 3))
    l_step(0, place == 3, (1,))
    e_op.wait_recv()
    ut[t_own, q_rm, low_half, :] = ut[t_own, q_rm, low_half, :] + op1[...]
    e_rm[0].start()
    e_om.wait_recv()
    ut[t_own, q_rp, high_half, :] = ut[t_own, q_rp, high_half, :] + om1[...]
    e_rp[1].start()
    for u in range(2):
        c_rm[u].wait_recv()
        c_rp[u].wait_recv()
    ut[t_away, z, top, :] = ut[t_away, z, top, :] + (rm[away] + rp[away])
    c_yh.start()
    for n in range(4):
        l_step(l_order[n], last, (2, 3))
    l_step(0, (row != 9) & (place != 3), (1,))

    y_add(z)
    for n in range(2):
        e_rm[n].wait_recv()
        e_rp[n].wait_recv()
    sums[end, :] = ut[t_own, z, end, :] + jnp.concatenate([rm1[n] + rp1[n] for n in range(2)], axis=0)
    c_yh.wait_recv()
    sums[top, :] = ut[t_own, z, top, :] + (rm[yh] + rp[yh] + yr[...])

    for u, (j, k) in enumerate(LOW):
        @pl.when(core != CORE_OF[j])
        def _():
            l_wait(u)

    def low(j, k):
        return lbh[LOW.index((j, k))], lbl[LOW.index((j, k))]

    for m, k in [(1, 0), (2, 1), (3, 2), (2, 0), (3, 1), (3, 0)]:
        u = LOW.index((m, k))
        acc = lt[u]
        for j in range(k + 1, m):
            acc = acc + dot3(split(lt[LOW.index((m, j))]), low(j, k))
        mt[m, k] = -acc
        hi, lo = split(-acc)
        lbh[u] = hi
        lbl[u] = lo

    parts = [split(sums[:, pl.ds(k * B, B)]) for k in range(S)]
    c_xa = [remote(xt.at[k], xa.at[t_own, q_own, :], s_xa.at[k], r_xa.at[t_own, z], at(r=k)) for k in range(S)]
    c_xb = [remote(xt.at[k], xb.at[core, q_own, :], s_xb.at[k], r_xb.at[core, z], at(r=b_row, c=k)) for k in range(S)]

    def b_self(k):
        return (row == b_row) & (col == k)

    for k in (3, 2, 1, 0):
        acc = sums[:, pl.ds(k * B, B)]
        for j in range(k + 1, S):
            acc = acc + dot3(parts[j], low(j, k))
        xt[k] = -acc

        @pl.when(jnp.logical_not(b_self(k)))
        def _():
            c_xb[k].start()

        @pl.when(b_self(k))
        def _():
            xb[core, q_own, :] = xt[k]
    for k in range(S):
        @pl.when(row != k)
        def _():
            c_xa[k].start()

        @pl.when(row == k)
        def _():
            xa[t_own, q_own, :] = xt[k]

    @pl.when(col < S)
    def _():
        for k in range(S):
            acc = jnp.concatenate([pn[k, pl.ds(0, B), :] * zero, pn[k, pl.ds(B, B), :]], axis=0)
            for j in range(k + 1, S):
                acc = acc + dot3((pbh[j], pbl[j]), low(j, k))
            hi, lo = split(acc.T)
            ph[k] = hi
            plo[k] = lo

    dload.wait()

    @pl.when((row < S) & (col < S))
    def _():
        ones = (lax.broadcasted_iota(jnp.int32, (B, B), 0) == lax.broadcasted_iota(jnp.int32, (B, B), 1))
        for m in range(S):
            mt[m, m] = ones.astype(F32)
            for k in range(m + 1, S):
                mt[m, k] = jnp.zeros((B, B), F32)
        zo[...] = jnp.zeros((B, B), F32)
        for m in range(S):
            part = dot3(split(dv[m]), split(mt[m, col]))
            zo[...] = zo[...] + dot3(split(mt[m, row].T), split(part))

    c_zc = [remote(zp.at[1 - core, m], zc.at[m], s_zc.at[m], r_zc.at[m], at(r=r_core)) for m in range(2)]
    c_zd = [[remote(zp.at[core, m, pl.ds(((quad + d) % 8) * 32, 32), :], zr.at[d - 1, m], s_zd.at[d - 1, m],
                    r_zd.at[d - 1, m], at(r=((quad + d) % 8) * 2 + core)) for d in range(1, 8)] for m in range(2)]
    c_zf = [remote(zs.at[m], zf.at[pl.ds(quad * 32, 32), :], s_zf.at[m], r_zf.at[quad], at(r=2 * m + core))
            for m in range(2)]

    w_row = [pltpu.make_async_copy(xat.at[t], out.at[0, :, t, :], w_sem.at[t]) for t in range(4)]
    w_col = [pltpu.make_async_copy(xb.at[a], out.at[a, :, 0, :], w_sem.at[4 + a]) for a in range(2)]
    w_dia = pltpu.make_async_copy(zo, out.at[0, :, 0, :], w_sem.at[6])
    rows_new = [((row < S) & (col >= S), w_row[0])] + [(row < S, w_row[t]) for t in range(1, 4)]
    cols_new = [((col < S) & (row >= S), w_col[0]), (col < S, w_col[1])]
    writes = rows_new + cols_new + [((row < S) & (col < S), w_dia)]

    def diagonal(side, m):
        zp[side, m] = dot3((ph[2 * m + side], plo[2 * m + side]), (xh[...], xl[...]))

    @pl.when(col < S)
    def _():
        for a in range(2):
            for q in range(4):
                @pl.when(b_other(a, q))
                def _():
                    remote(xt.at[0], xb.at[a, pl.ds(64 * q, 64), :], s_xb.at[0], r_xb.at[a, q], at(r=b_row)).wait_recv()
            hi, lo = split(xb[a])
            xh[pl.ds(a * B, B), :] = hi
            xl[pl.ds(a * B, B), :] = lo
        for m in range(2):
            diagonal(1 - core, m)
            c_zc[m].start()
        for m in range(2):
            diagonal(core, m)
            c_zc[m].wait_recv()
            zp[core, m] = zp[core, m] + zc[m]
            for copy in c_zd[m]:
                copy.start()
        for cond, copy in cols_new:
            @pl.when(cond)
            def _():
                copy.start()
        for m in range(2):
            acc = zp[core, m, pl.ds(quad * 32, 32), :]
            for d in range(7):
                c_zd[m][d].wait_recv()
                acc = acc + zr[d, m]
            zs[m] = acc

            @pl.when(quad != m)
            def _():
                c_zf[m].start()

            @pl.when(quad == m)
            def _():
                zf[pl.ds(quad * 32, 32), :] = zs[m]

    @pl.when(row < S)
    def _():
        for t in range(4):
            for q in range(4):
                @pl.when(row != (t % 2) * 8 + q * 2 + t // 2)
                def _():
                    remote(xt.at[0], xa.at[t, pl.ds(64 * q, 64), :], s_xa.at[0], r_xa.at[t, q], at(r=r_core)).wait_recv()
            xat[t] = xa[t].T
        for cond, copy in rows_new:
            @pl.when(cond)
            def _():
                copy.start()

    @pl.when((row < S) & (col < S))
    def _():
        for q in range(8):
            @pl.when(quad != q)
            def _():
                remote(zs.at[0], zf.at[pl.ds(q * 32, 32), :], s_zf.at[0], r_zf.at[q], at(r=r_core)).wait_recv()
        zo[...] = zo[...] - zf[...]
        w_dia.start()

    @pl.when(source)
    def _():
        for ch in range(4):
            quarter(k_p, ch, s_out.at[ch], r_out.at[ch], to_o).wait_send()
        for ch in (1, 2, 3):
            quarter(k_pd, ch, s_out.at[3 + ch], r_out.at[3 + ch], to_o).wait_send()
            quarter(k_p, ch, s_y.at[ch], r_y.at[ch], to_y).wait_send()
        for ch in (0, 2):
            quarter(k_pd, ch, s_x.at[4 + ch // 2], r_x.at[4 + ch // 2], to_x).wait_send()

    @pl.when(inner)
    def _():
        for ch in (0, 2):
            quarter(k_s, ch, s_y.at[4 + ch], r_y.at[4 + ch], to_y).wait_send()
    for ch in range(4):
        quarter(k_p, ch, s_x.at[ch], r_x.at[ch], to_x).wait_send()
    quarter(k_p, 0, s_y.at[0], r_y.at[0], to_y).wait_send()
    for ch in (1, 3):
        quarter(k_s, ch, s_y.at[4 + ch], r_y.at[4 + ch], to_y).wait_send()
    for j, k in LOW:
        @pl.when(core == CORE_OF[j])
        def _():
            for cond, copy in l_routes(LOW.index((j, k)), j):
                @pl.when(cond)
                def _():
                    copy.wait_send()
    for copy in [core_copy(k) for k in range(S)] + [y_copy(k) for k in range(4)] + [c_op, c_om, c_yh, e_op, e_om]:
        copy.wait_send()
    for copy in c_rm + c_rp + e_rm + e_rp:
        copy.wait_send()

    for k in range(S):
        @pl.when(jnp.logical_not(b_self(k)))
        def _():
            c_xb[k].wait_send()

        @pl.when(row != k)
        def _():
            c_xa[k].wait_send()

    @pl.when(col < S)
    def _():
        for copy in c_zc + c_zd[0] + c_zd[1]:
            copy.wait_send()
        for m in range(2):
            @pl.when(quad != m)
            def _():
                c_zf[m].wait_send()
    for cond, copy in writes + keeps:
        @pl.when(cond)
        def _():
            copy.wait()


def body(prior, lfac, tile_mask, dinv):
    def vmem(*shape, kind=F32):
        return pltpu.VMEM(shape, kind)

    dma = pltpu.SemaphoreType.DMA
    wide = S * B
    scratch = [
        vmem(4, 2 * B, B), vmem(4, B, 2 * B, kind=BF16), vmem(4, B, 2 * B, kind=BF16),
        vmem(2, B, B), vmem(4, 2 * B, B), vmem(4, 2 * B, B, kind=BF16), vmem(4, 2 * B, B, kind=BF16),
        vmem(4, B, 2 * B, kind=BF16), vmem(4, B, 2 * B, kind=BF16),
        vmem(6, B, B), vmem(6, B, B, kind=BF16), vmem(6, B, B, kind=BF16),
        vmem(4, 4, 64, wide), vmem(2, 4, 64, wide),
        vmem(TOP, wide), vmem(TOP, wide), vmem(2, TOP, wide), vmem(2, TOP, wide), vmem(TOP, wide),
        vmem(4, LATE, wide), vmem(HALF, wide), vmem(HALF, wide), vmem(2, HALF, wide), vmem(2, HALF, wide),
        vmem(64, wide),
        vmem(4, 64, B), vmem(4, B, B), vmem(2, B, B), vmem(4, B, B),
        vmem(2 * B, B, kind=BF16), vmem(2 * B, B, kind=BF16),
        vmem(2, 2, B, B), vmem(2, B, B), vmem(7, 2, 32, B), vmem(2, 32, B), vmem(B, B),
        vmem(4, 4, B, B), vmem(4, B, B), vmem(B, B), pltpu.SMEM((32, 32), jnp.int32), dma,
        dma((2, 4)), dma((2,)), dma, dma((2, 4)), dma((7,)),
        dma((7,)), dma((7,)), dma((6,)), dma((6,)), dma((8,)), dma((8,)),
        dma((6, 4)), dma((6,)), dma((4,)), dma((4,)),
        dma((2,)), dma((2,)), dma((2, 2)), dma((2, 2)), dma, dma,
        dma((4,)), dma((4,)), dma((2,)), dma((2,)), dma((2, 2)), dma((2, 2)),
        dma((4,)), dma((4, 4)), dma((4,)), dma((2, 4)),
        dma((2,)), dma((2,)), dma((7, 2)), dma((7, 2)), dma((2,)), dma((8,)),
    ]
    return pl.pallas_call(
        kernel,
        out_shape=jax.ShapeDtypeStruct(prior.shape, F32),
        in_specs=[pl.BlockSpec(memory_space=pl.ANY), pl.BlockSpec(memory_space=pl.ANY),
                  pl.BlockSpec(memory_space=pl.ANY), pl.BlockSpec(memory_space=pl.ANY)],
        out_specs=pl.BlockSpec(memory_space=pl.ANY),
        scratch_shapes=scratch,
        compiler_params=pltpu.CompilerParams(
            collective_id=0, has_side_effects=True, vmem_limit_bytes=56 * 1024 * 1024),
    )(prior, lfac, tile_mask, dinv)


def solution(mesh):
    placed = (P("prow", None, "pcol", None), P("prow", None, "pcol", None), P(), P())
    return jax.shard_map(
        body, mesh=mesh, in_specs=placed, out_specs=P("prow", None, "pcol", None), check_vma=False
    )
```

```python
import jax
import jax.numpy as jnp
from jax import lax
from jax.experimental import pallas as pl
from jax.experimental.pallas import tpu as pltpu
from jax.sharding import PartitionSpec as P

B = 256
S = 4
F32 = jnp.float32
BF16 = jnp.bfloat16
MESH = pl.DeviceIdType.MESH
LOW = [(1, 0), (2, 0), (2, 1), (3, 0), (3, 1), (3, 2)]
LATE = 32
TOP = 64 - LATE
HALF = LATE // 2
CORE_OF = {1: 1, 2: 0, 3: 1}


def split(value):
    hi = value.astype(BF16)
    lo = (value - hi.astype(F32)).astype(BF16)
    return hi, lo


def dot3(a, b, dims=((1,), (0,))):
    def one(left, right):
        return lax.dot_general(left, right, (dims, ((), ())), preferred_element_type=F32)

    return one(a[0], b[0]) + (one(a[0], b[1]) + one(a[1], b[0]))


def kernel(prior, lfac, tile_mask, dinv, out,
           g32, gth, gtl, lt32, pn, pbh, pbl, ph, plo, lt, lbh, lbl, ut, cr, op, om, rm, rp, yr,
           yq, op1, om1, rm1, rp1, sums, xt, xa, xb, xat, xh, xl,
           zp, zc, zr, zs, zf, mt, dv, zo, mask, m_sem,
           g_sem, l_sem, d_sem, o_sem, w_sem,
           s_out, r_out, s_x, r_x, s_y, r_y,
           s_l, r_l, s_c, r_c, s_zo, r_zo, s_zr, r_zr, s_yh, r_yh, s_yq, r_yq, s_eo, r_eo, s_er, r_er,
           s_xa, r_xa, s_xb, r_xb, s_zc, r_zc, s_zd, r_zd, s_zf, r_zf):
    row = lax.axis_index("prow")
    col = lax.axis_index("pcol")
    yh, z, core = row // 8, (row // 2) % 4, row % 2
    x, yl = col // 2, col % 2
    quad = row // 2

    def at(r=None, c=None):
        return {"prow": row if r is None else r, "pcol": col if c is None else c}

    def remote(src, dst, ssem, rsem, where):
        return pltpu.make_async_remote_copy(
            src_ref=src, dst_ref=dst, send_sem=ssem, recv_sem=rsem, device_id=where, device_id_type=MESH)

    c_x = (x + 1 - 2 * (x % 2)) * 2 + yl
    c_y = x * 2 + 1 - yl
    c_o = (3 - x) * 2 + yl
    r_core = row + 1 - 2 * core
    r_zp = yh * 8 + ((z + 1) % 4) * 2 + core
    r_zm = yh * 8 + ((z + 3) % 4) * 2 + core
    r_y2 = (row + 8) % 16
    t_own = 2 * core + yh
    b_row = col + 8 * yh
    q_own = pl.ds(64 * z, 64)

    loads = []
    for a in range(2):
        for b in range(4):
            loads.append(pltpu.make_async_copy(prior.at[a, :, b, :], g32.at[b, pl.ds(a * B, B), :], g_sem.at[a, b]))
    keeps = []
    for a in range(2):
        for b in range(4):
            stays = row >= 0
            if a == 0:
                stays = stays & (row >= S)
            if b == 0:
                stays = stays & (col >= S)
            keeps.append((stays, pltpu.make_async_copy(
                g32.at[b, pl.ds(a * B, B), :], out.at[a, :, b, :], o_sem.at[a, b])))
    ltile = [pltpu.make_async_copy(lfac.at[a, :, 0, :], lt32.at[a], l_sem.at[a]) for a in range(2)]
    mload = pltpu.make_async_copy(tile_mask, mask, m_sem)
    dload = pltpu.make_async_copy(dinv, dv, d_sem)

    @pl.when(col < S)
    def _():
        mload.start()
        for copy in ltile:
            copy.start()
    for copy in loads:
        copy.start()
    dload.start()

    barrier = pltpu.get_barrier_semaphore()

    def greet(where):
        pl.semaphore_signal(barrier, inc=1, device_id=where, device_id_type=MESH)

    for step in range(1, 16):
        greet(at(r=(row + step) % 16))
    for c in (c_x, c_y, c_o):
        greet(at(c=c))
    greet(at(r=r_y2, c=c_y))

    def b_source(a, q):
        return yh * 8 + q * 2 + a, row % 8

    def b_other(a, q):
        sr, sc = b_source(a, q)
        return jnp.logical_not((sr == row) & (sc == col))

    for a in range(2):
        for q in range(4):
            sr, sc = b_source(a, q)

            @pl.when((col < S) & b_other(a, q))
            def _():
                greet(at(r=sr, c=sc))

    @pl.when(col < S)
    def _():
        mload.wait()
        for a in range(2):
            ltile[a].wait()
            live = mask[row + 16 * a, col] * (row + 16 * a > col).astype(jnp.int32)
            pn[col, pl.ds(a * B, B), :] = lt32[a] * live.astype(F32)

    pl.semaphore_wait(barrier, 19 + 4 - jnp.where((row == b_row) & (col < S), 1, 0))

    near = jnp.where((x == 0) | (x == 3), 0, 1)
    k_p, k_s = 2 * near + yl, 2 * (1 - near) + yl
    k_pd, k_sd = 2 * near + 1 - yl, 2 * (1 - near) + 1 - yl

    def quarter(k, ch, ssem, rsem, where):
        part = pn.at[k, pl.ds(128 * ch, 128), :]
        return remote(part, part, ssem, rsem, where)

    source, inner = x < 2, x >= 2
    always = row >= 0
    to_x, to_y, to_o = at(c=c_x), at(c=c_y), at(c=c_o)

    def out_recv(ch):
        quarter(k_p, ch, s_out.at[ch], r_out.at[ch], to_o).wait_recv()

    def x_recv(ch):
        quarter(k_s, ch, s_x.at[ch], r_x.at[ch], to_x).wait_recv()

    def y_recv(ch):
        quarter(k_pd, ch, s_y.at[ch], r_y.at[ch], to_y).wait_recv()

    def xd_recv(ch):
        quarter(k_sd, ch, s_x.at[4 + ch // 2], r_x.at[4 + ch // 2], to_x).wait_recv()

    def yd_recv(ch):
        quarter(k_sd, ch, s_y.at[4 + ch], r_y.at[4 + ch], to_y).wait_recv()

    def l_copy(u, slot, where):
        return remote(lt.at[u], lt.at[u], s_l.at[u, slot], r_l.at[u], where)

    def l_wait(u):
        l_copy(u, 0, at(r=r_core)).wait_recv()

    place = row % 8

    def l_routes(u, j):
        ahead, behind = {1: ((1, 3), (1,)), 2: ((2,), (2, 0)), 3: ((3, 5), (3,))}[j]
        plus = (place == ahead[0]) | (place == ahead[-1])
        minus = (place == behind[0]) | (place == behind[-1])
        return [(always, l_copy(u, 0, at(r=r_core))), (row == j, l_copy(u, 1, at(r=r_y2, c=c_y))),
                (plus, l_copy(u, 2, at(r=r_zp))), (minus, l_copy(u, 3, at(r=r_zm)))]

    def l_step(k, mine, rows=(2, 3, 1)):
        for j in rows:
            u = (j * (j - 1)) // 2 + k
            here = (core == CORE_OF[j]) & (k < j)

            @pl.when(here & (row == j) if mine is None else here & (row != j) & mine)
            def _():
                if mine is None:
                    lt[u] = pn[k, pl.ds(0, B), :]
                else:
                    l_wait(u)
                for cond, copy in l_routes(u, j):
                    @pl.when(cond)
                    def _():
                        copy.start()

    l_order = [jnp.where(yh == 0, a, b) for a, b in ((k_p, k_pd), (k_pd, k_p), (k_s, k_sd), (k_sd, k_s))]
    early, later, last = z == 1, (z == 0) | (z == 2), z == 3

    def p_out(ch):
        quarter(k_p, ch, s_out.at[ch], r_out.at[ch], to_o).start()

    def p_x(ch):
        quarter(k_p, ch, s_x.at[ch], r_x.at[ch], to_x).start()

    def p_y(ch):
        quarter(k_p, ch, s_y.at[ch], r_y.at[ch], to_y).start()

    def e_out(ch):
        quarter(k_pd, ch, s_out.at[3 + ch], r_out.at[3 + ch], to_o).start()

    def d_x(ch):
        quarter(k_pd, ch, s_x.at[4 + ch // 2], r_x.at[4 + ch // 2], to_x).start()

    def d_y(ch):
        quarter(k_s, ch, s_y.at[4 + ch], r_y.at[4 + ch], to_y).start()

    @pl.when(source)
    def _():
        for ch in range(3):
            p_out(ch)
            p_y(ch)
        p_x(0)
        p_x(1)
        l_step(k_p, None)

    for a in range(2):
        for b in range(4):
            loads[a * 4 + b].wait()
            cond, copy = keeps[a * 4 + b]

            @pl.when(cond)
            def _():
                copy.start()
    for b in range(4):
        for a in range(2):
            hi, lo = split(g32[b, pl.ds(a * B, B), :].T)
            gth[b, :, pl.ds(a * B, B)] = hi
            gtl[b, :, pl.ds(a * B, B)] = lo

    zero = jnp.where(row < S, 0.0, 1.0).astype(F32)

    def core_copy(k):
        lanes = pl.ds(pl.multiple_of(k * B, B), B)
        return remote(ut.at[pl.ds(2 - 2 * core, 2), :, :, lanes], cr.at[:, :, :, lanes], s_c.at[k], r_c.at[k], at(r=r_core))

    def products(k):
        for a in range(2):
            rows = pl.ds(a * B, B)
            hi, lo = split(pn[k, rows, :] * zero if a == 0 else pn[k, rows, :])
            pbh[k, rows, :] = hi
            pbl[k, rows, :] = lo

        @pl.loop(0, 4)
        def _(step):
            t = lax.rem(2 - 2 * core + step, 4)
            value = dot3((gth[t], gtl[t]), (pbh[k], pbl[k]))
            for q in range(4):
                ut[t, q, :, pl.ds(pl.multiple_of(k * B, B), B)] = value[q * 64:(q + 1) * 64]
        core_copy(k).start()

    @pl.when(source)
    def _():
        products(k_p)
        y_recv(0)
        d_x(0)
        p_x(2)
        p_out(3)
        y_recv(1)
        e_out(1)
        p_x(3)
        x_recv(0)
        x_recv(1)
        d_y(1)
        p_y(3)
        l_step(k_pd, None)
        l_step(k_s, None)
        y_recv(2)
        d_x(2)
        e_out(2)
        xd_recv(0)
        yd_recv(1)
        l_step(k_sd, None)

    @pl.when(inner)
    def _():
        out_recv(0)
        p_x(0)
        p_y(0)
        out_recv(1)
        p_x(1)
        l_step(k_p, None)
        x_recv(0)
        d_y(0)
        out_recv(2)
        p_x(2)
        x_recv(1)
        d_y(1)
        l_step(k_s, None)
        out_recv(3)
        p_x(3)
        products(k_p)
    l_step(l_order[0], early, (2, 3))

    @pl.when(source)
    def _():
        y_recv(3)
        e_out(3)
        x_recv(2)
        x_recv(3)
        d_y(3)

    @pl.when(inner)
    def _():
        x_recv(2)
        d_y(2)
        y_recv(0)
        quarter(k_pd, 1, s_out.at[4], r_out.at[4], to_o).wait_recv()
        l_step(k_pd, None)
        yd_recv(0)
        yd_recv(1)
        l_step(k_sd, None)
        x_recv(3)
        d_y(3)
    products(k_s)
    l_step(l_order[1], early, (2, 3))
    l_step(l_order[2], early, (2, 3))
    l_step(l_order[0], later, (2, 3))

    @pl.when(inner)
    def _():
        for ch in (2, 3):
            quarter(k_pd, ch, s_out.at[3 + ch], r_out.at[3 + ch], to_o).wait_recv()
    products(k_pd)
    l_step(l_order[3], early, (2, 3))
    l_step(l_order[1], later, (2, 3))
    l_step(0, row == 9, (1,))

    @pl.when(source)
    def _():
        xd_recv(2)

    @pl.when(inner)
    def _():
        yd_recv(2)
    yd_recv(3)
    products(k_sd)

    top, end = pl.ds(0, TOP), pl.ds(TOP, LATE)
    low_half, high_half = pl.ds(TOP, HALF), pl.ds(TOP + HALF, HALF)
    q_op, q_rm, q_rp = (z + 2) % 4, (z + 1) % 4, (z + 3) % 4
    away = 1 - yh
    t_away = 2 * core + away

    def unit(q, u):
        return ut.at[2 * core + u, q, top, :]

    c_op = remote(unit(q_op, 0), op, s_zo.at[0], r_zo.at[0], at(r=r_zp))
    c_om = remote(unit(q_op, 1), om, s_zo.at[1], r_zo.at[1], at(r=r_zm))
    c_rm = [remote(unit(q_rm, u), rm.at[u], s_zr.at[0, u], r_zr.at[0, u], at(r=r_zp)) for u in range(2)]
    c_rp = [remote(unit(q_rp, u), rp.at[u], s_zr.at[1, u], r_zr.at[1, u], at(r=r_zm)) for u in range(2)]
    c_yh = remote(unit(z, away), yr, s_yh, r_yh, at(r=r_y2))

    def y_copy(q):
        return remote(ut.at[t_away, q, end, :], yq.at[q], s_yq.at[q], r_yq.at[q], at(r=r_y2))

    def y_add(q):
        y_copy(q).wait_recv()
        ut[t_own, q, end, :] = ut[t_own, q, end, :] + yq[q]

    e_op = remote(ut.at[t_own, q_op, low_half, :], op1, s_eo.at[0], r_eo.at[0], at(r=r_zp))
    e_om = remote(ut.at[t_own, q_op, high_half, :], om1, s_eo.at[1], r_eo.at[1], at(r=r_zm))
    e_rm = [remote(ut.at[t_own, q_rm, part, :], rm1.at[n], s_er.at[0, n], r_er.at[0, n], at(r=r_zp))
            for n, part in enumerate((low_half, high_half))]
    e_rp = [remote(ut.at[t_own, q_rp, part, :], rp1.at[n], s_er.at[1, n], r_er.at[1, n], at(r=r_zm))
            for n, part in enumerate((low_half, high_half))]

    def core_add(q):
        for u in range(2):
            ut[2 * core + u, q] = ut[2 * core + u, q] + cr[u, q]

    for k in range(S):
        core_copy(k).wait_recv()
    core_add(q_op)
    y_copy(q_op).start()
    c_op.start()
    c_om.start()
    core_add(q_rm)
    c_rm[1].start()
    y_copy(q_rm).start()
    core_add(q_rp)
    c_rp[0].start()
    y_copy(q_rp).start()
    core_add(z)
    y_copy(z).start()
    l_step(l_order[2], later, (2, 3))
    c_op.wait_recv()
    ut[2 * core, q_rm, top, :] = ut[2 * core, q_rm, top, :] + op[...]
    c_rm[0].start()
    c_om.wait_recv()
    ut[2 * core + 1, q_rp, top, :] = ut[2 * core + 1, q_rp, top, :] + om[...]
    c_rp[1].start()
    y_add(q_op)
    e_op.start()
    e_om.start()
    y_add(q_rm)
    e_rm[1].start()
    y_add(q_rp)
    e_rp[0].start()
    l_step(l_order[3], later, (2, 3))
    l_step(0, place == 3, (1,))
    e_op.wait_recv()
    ut[t_own, q_rm, low_half, :] = ut[t_own, q_rm, low_half, :] + op1[...]
    e_rm[0].start()
    e_om.wait_recv()
    ut[t_own, q_rp, high_half, :] = ut[t_own, q_rp, high_half, :] + om1[...]
    e_rp[1].start()
    for u in range(2):
        c_rm[u].wait_recv()
        c_rp[u].wait_recv()
    ut[t_away, z, top, :] = ut[t_away, z, top, :] + (rm[away] + rp[away])
    c_yh.start()
    for n in range(4):
        l_step(l_order[n], last, (2, 3))
    l_step(0, (row != 9) & (place != 3), (1,))

    y_add(z)
    for n in range(2):
        e_rm[n].wait_recv()
        e_rp[n].wait_recv()
    sums[end, :] = ut[t_own, z, end, :] + jnp.concatenate([rm1[n] + rp1[n] for n in range(2)], axis=0)
    c_yh.wait_recv()
    sums[top, :] = ut[t_own, z, top, :] + (rm[yh] + rp[yh] + yr[...])

    for u, (j, k) in enumerate(LOW):
        @pl.when(core != CORE_OF[j])
        def _():
            l_wait(u)

    def low(j, k):
        return lbh[LOW.index((j, k))], lbl[LOW.index((j, k))]

    for m, k in [(1, 0), (2, 1), (3, 2), (2, 0), (3, 1), (3, 0)]:
        u = LOW.index((m, k))
        acc = lt[u]
        for j in range(k + 1, m):
            acc = acc + dot3(split(lt[LOW.index((m, j))]), low(j, k))
        mt[m, k] = -acc
        hi, lo = split(-acc)
        lbh[u] = hi
        lbl[u] = lo

    parts = [split(sums[:, pl.ds(k * B, B)]) for k in range(S)]
    c_xa = [remote(xt.at[k], xa.at[t_own, q_own, :], s_xa.at[k], r_xa.at[t_own, z], at(r=k)) for k in range(S)]
    c_xb = [remote(xt.at[k], xb.at[core, q_own, :], s_xb.at[k], r_xb.at[core, z], at(r=b_row, c=k)) for k in range(S)]

    def b_self(k):
        return (row == b_row) & (col == k)

    for k in (3, 2, 1, 0):
        acc = sums[:, pl.ds(k * B, B)]
        for j in range(k + 1, S):
            acc = acc + dot3(parts[j], low(j, k))
        xt[k] = -acc

        @pl.when(jnp.logical_not(b_self(k)))
        def _():
            c_xb[k].start()

        @pl.when(b_self(k))
        def _():
            xb[core, q_own, :] = xt[k]
    for k in range(S):
        @pl.when(row != k)
        def _():
            c_xa[k].start()

        @pl.when(row == k)
        def _():
            xa[t_own, q_own, :] = xt[k]

    @pl.when(col < S)
    def _():
        for k in range(S):
            acc = jnp.concatenate([pn[k, pl.ds(0, B), :] * zero, pn[k, pl.ds(B, B), :]], axis=0)
            for j in range(k + 1, S):
                acc = acc + dot3((pbh[j], pbl[j]), low(j, k))
            hi, lo = split(acc.T)
            ph[k] = hi
            plo[k] = lo

    dload.wait()

    @pl.when((row < S) & (col < S))
    def _():
        ones = (lax.broadcasted_iota(jnp.int32, (B, B), 0) == lax.broadcasted_iota(jnp.int32, (B, B), 1))
        for m in range(S):
            mt[m, m] = ones.astype(F32)
            for k in range(m + 1, S):
                mt[m, k] = jnp.zeros((B, B), F32)
        zo[...] = jnp.zeros((B, B), F32)
        for m in range(S):
            part = dot3(split(dv[m]), split(mt[m, col]))
            zo[...] = zo[...] + dot3(split(mt[m, row].T), split(part))

    c_zc = [remote(zp.at[1 - core, m], zc.at[m], s_zc.at[m], r_zc.at[m], at(r=r_core)) for m in range(2)]
    c_zd = [[remote(zp.at[core, m, pl.ds(((quad + d) % 8) * 32, 32), :], zr.at[d - 1, m], s_zd.at[d - 1, m],
                    r_zd.at[d - 1, m], at(r=((quad + d) % 8) * 2 + core)) for d in range(1, 8)] for m in range(2)]
    c_zf = [remote(zs.at[m], zf.at[pl.ds(quad * 32, 32), :], s_zf.at[m], r_zf.at[quad], at(r=2 * m + core))
            for m in range(2)]

    w_row = [pltpu.make_async_copy(xat.at[t], out.at[0, :, t, :], w_sem.at[t]) for t in range(4)]
    w_col = [pltpu.make_async_copy(xb.at[a], out.at[a, :, 0, :], w_sem.at[4 + a]) for a in range(2)]
    w_dia = pltpu.make_async_copy(zo, out.at[0, :, 0, :], w_sem.at[6])
    rows_new = [((row < S) & (col >= S), w_row[0])] + [(row < S, w_row[t]) for t in range(1, 4)]
    cols_new = [((col < S) & (row >= S), w_col[0]), (col < S, w_col[1])]
    writes = rows_new + cols_new + [((row < S) & (col < S), w_dia)]

    def diagonal(side, m):
        zp[side, m] = dot3((ph[2 * m + side], plo[2 * m + side]), (xh[...], xl[...]))

    @pl.when(col < S)
    def _():
        for a in range(2):
            for q in range(4):
                @pl.when(b_other(a, q))
                def _():
                    remote(xt.at[0], xb.at[a, pl.ds(64 * q, 64), :], s_xb.at[0], r_xb.at[a, q], at(r=b_row)).wait_recv()
            hi, lo = split(xb[a])
            xh[pl.ds(a * B, B), :] = hi
            xl[pl.ds(a * B, B), :] = lo
        for m in range(2):
            diagonal(1 - core, m)
            c_zc[m].start()
        for m in range(2):
            diagonal(core, m)
            c_zc[m].wait_recv()
            zp[core, m] = zp[core, m] + zc[m]
            for copy in c_zd[m]:
                copy.start()
        for cond, copy in cols_new:
            @pl.when(cond)
            def _():
                copy.start()
        for m in range(2):
            acc = zp[core, m, pl.ds(quad * 32, 32), :]
            for d in range(7):
                c_zd[m][d].wait_recv()
                acc = acc + zr[d, m]
            zs[m] = acc

            @pl.when(quad != m)
            def _():
                c_zf[m].start()

            @pl.when(quad == m)
            def _():
                zf[pl.ds(quad * 32, 32), :] = zs[m]

    @pl.when(row < S)
    def _():
        for t in range(4):
            for q in range(4):
                @pl.when(row != (t % 2) * 8 + q * 2 + t // 2)
                def _():
                    remote(xt.at[0], xa.at[t, pl.ds(64 * q, 64), :], s_xa.at[0], r_xa.at[t, q], at(r=r_core)).wait_recv()
            xat[t] = xa[t].T
        for cond, copy in rows_new:
            @pl.when(cond)
            def _():
                copy.start()

    @pl.when((row < S) & (col < S))
    def _():
        for q in range(8):
            @pl.when(quad != q)
            def _():
                remote(zs.at[0], zf.at[pl.ds(q * 32, 32), :], s_zf.at[0], r_zf.at[q], at(r=r_core)).wait_recv()
        zo[...] = zo[...] - zf[...]
        w_dia.start()

    @pl.when(source)
    def _():
        for ch in range(4):
            quarter(k_p, ch, s_out.at[ch], r_out.at[ch], to_o).wait_send()
        for ch in (1, 2, 3):
            quarter(k_pd, ch, s_out.at[3 + ch], r_out.at[3 + ch], to_o).wait_send()
            quarter(k_p, ch, s_y.at[ch], r_y.at[ch], to_y).wait_send()
        for ch in (0, 2):
            quarter(k_pd, ch, s_x.at[4 + ch // 2], r_x.at[4 + ch // 2], to_x).wait_send()

    @pl.when(inner)
    def _():
        for ch in (0, 2):
            quarter(k_s, ch, s_y.at[4 + ch], r_y.at[4 + ch], to_y).wait_send()
    for ch in range(4):
        quarter(k_p, ch, s_x.at[ch], r_x.at[ch], to_x).wait_send()
    quarter(k_p, 0, s_y.at[0], r_y.at[0], to_y).wait_send()
    for ch in (1, 3):
        quarter(k_s, ch, s_y.at[4 + ch], r_y.at[4 + ch], to_y).wait_send()
    for j, k in LOW:
        @pl.when(core == CORE_OF[j])
        def _():
            for cond, copy in l_routes(LOW.index((j, k)), j):
                @pl.when(cond)
                def _():
                    copy.wait_send()
    for copy in [core_copy(k) for k in range(S)] + [y_copy(k) for k in range(4)] + [c_op, c_om, c_yh, e_op, e_om]:
        copy.wait_send()
    for copy in c_rm + c_rp + e_rm + e_rp:
        copy.wait_send()

    for k in range(S):
        @pl.when(jnp.logical_not(b_self(k)))
        def _():
            c_xb[k].wait_send()

        @pl.when(row != k)
        def _():
            c_xa[k].wait_send()

    @pl.when(col < S)
    def _():
        for copy in c_zc + c_zd[0] + c_zd[1]:
            copy.wait_send()
        for m in range(2):
            @pl.when(quad != m)
            def _():
                c_zf[m].wait_send()
    for cond, copy in writes + keeps:
        @pl.when(cond)
        def _():
            copy.wait()


def body(prior, lfac, tile_mask, dinv):
    def vmem(*shape, kind=F32):
        return pltpu.VMEM(shape, kind)

    dma = pltpu.SemaphoreType.DMA
    wide = S * B
    scratch = [
        vmem(4, 2 * B, B), vmem(4, B, 2 * B, kind=BF16), vmem(4, B, 2 * B, kind=BF16),
        vmem(2, B, B), vmem(4, 2 * B, B), vmem(4, 2 * B, B, kind=BF16), vmem(4, 2 * B, B, kind=BF16),
        vmem(4, B, 2 * B, kind=BF16), vmem(4, B, 2 * B, kind=BF16),
        vmem(6, B, B), vmem(6, B, B, kind=BF16), vmem(6, B, B, kind=BF16),
        vmem(4, 4, 64, wide), vmem(2, 4, 64, wide),
        vmem(TOP, wide), vmem(TOP, wide), vmem(2, TOP, wide), vmem(2, TOP, wide), vmem(TOP, wide),
        vmem(4, LATE, wide), vmem(HALF, wide), vmem(HALF, wide), vmem(2, HALF, wide), vmem(2, HALF, wide),
        vmem(64, wide),
        vmem(4, 64, B), vmem(4, B, B), vmem(2, B, B), vmem(4, B, B),
        vmem(2 * B, B, kind=BF16), vmem(2 * B, B, kind=BF16),
        vmem(2, 2, B, B), vmem(2, B, B), vmem(7, 2, 32, B), vmem(2, 32, B), vmem(B, B),
        vmem(4, 4, B, B), vmem(4, B, B), vmem(B, B), pltpu.SMEM((32, 32), jnp.int32), dma,
        dma((2, 4)), dma((2,)), dma, dma((2, 4)), dma((7,)),
        dma((7,)), dma((7,)), dma((6,)), dma((6,)), dma((8,)), dma((8,)),
        dma((6, 4)), dma((6,)), dma((4,)), dma((4,)),
        dma((2,)), dma((2,)), dma((2, 2)), dma((2, 2)), dma, dma,
        dma((4,)), dma((4,)), dma((2,)), dma((2,)), dma((2, 2)), dma((2, 2)),
        dma((4,)), dma((4, 4)), dma((4,)), dma((2, 4)),
        dma((2,)), dma((2,)), dma((7, 2)), dma((7, 2)), dma((2,)), dma((8,)),
    ]
    return pl.pallas_call(
        kernel,
        out_shape=jax.ShapeDtypeStruct(prior.shape, F32),
        in_specs=[pl.BlockSpec(memory_space=pl.ANY), pl.BlockSpec(memory_space=pl.ANY),
                  pl.BlockSpec(memory_space=pl.ANY), pl.BlockSpec(memory_space=pl.ANY)],
        out_specs=pl.BlockSpec(memory_space=pl.ANY),
        scratch_shapes=scratch,
        compiler_params=pltpu.CompilerParams(
            collective_id=0, has_side_effects=True, vmem_limit_bytes=56 * 1024 * 1024),
    )(prior, lfac, tile_mask, dinv)


def solution(mesh):
    placed = (P("prow", None, "pcol", None), P("prow", None, "pcol", None), P(), P())
    return jax.shard_map(
        body, mesh=mesh, in_specs=placed, out_specs=P("prow", None, "pcol", None), check_vma=False
    )
```

```python
import jax
import jax.numpy as jnp
from jax import lax
from jax.experimental import pallas as pl
from jax.experimental.pallas import tpu as pltpu
from jax.sharding import PartitionSpec as P

B = 256
S = 4
F32 = jnp.float32
BF16 = jnp.bfloat16
MESH = pl.DeviceIdType.MESH
LOW = [(1, 0), (2, 0), (2, 1), (3, 0), (3, 1), (3, 2)]
LATE = 32
TOP = 64 - LATE
HALF = LATE // 2
CORE_OF = {1: 1, 2: 0, 3: 1}


def split(value):
    hi = value.astype(BF16)
    lo = (value - hi.astype(F32)).astype(BF16)
    return hi, lo


def dot3(a, b, dims=((1,), (0,))):
    def one(left, right):
        return lax.dot_general(left, right, (dims, ((), ())), preferred_element_type=F32)

    return one(a[0], b[0]) + (one(a[0], b[1]) + one(a[1], b[0]))


def kernel(prior, lfac, tile_mask, dinv, out,
           g32, gth, gtl, lt32, pn, pbh, pbl, ph, plo, lt, lbh, lbl, ut, cr, op, om, rm, rp, yr,
           yq, op1, om1, rm1, rp1, sums, xt, xa, xb, xat, xh, xl,
           zp, zc, zr, zs, zf, mt, dv, zo, mask, m_sem,
           g_sem, l_sem, d_sem, o_sem, w_sem,
           s_out, r_out, s_x, r_x, s_y, r_y,
           s_l, r_l, s_c, r_c, s_zo, r_zo, s_zr, r_zr, s_yh, r_yh, s_yq, r_yq, s_eo, r_eo, s_er, r_er,
           s_xa, r_xa, s_xb, r_xb, s_zc, r_zc, s_zd, r_zd, s_zf, r_zf):
    row = lax.axis_index("prow")
    col = lax.axis_index("pcol")
    yh, z, core = row // 8, (row // 2) % 4, row % 2
    x, yl = col // 2, col % 2
    quad = row // 2

    def at(r=None, c=None):
        return {"prow": row if r is None else r, "pcol": col if c is None else c}

    def remote(src, dst, ssem, rsem, where):
        return pltpu.make_async_remote_copy(
            src_ref=src, dst_ref=dst, send_sem=ssem, recv_sem=rsem, device_id=where, device_id_type=MESH)

    c_x = (x + 1 - 2 * (x % 2)) * 2 + yl
    c_y = x * 2 + 1 - yl
    c_o = (3 - x) * 2 + yl
    r_core = row + 1 - 2 * core
    r_zp = yh * 8 + ((z + 1) % 4) * 2 + core
    r_zm = yh * 8 + ((z + 3) % 4) * 2 + core
    r_y2 = (row + 8) % 16
    t_own = 2 * core + yh
    b_row = col + 8 * yh
    q_own = pl.ds(64 * z, 64)

    loads = []
    for a in range(2):
        for b in range(4):
            loads.append(pltpu.make_async_copy(prior.at[a, :, b, :], g32.at[b, pl.ds(a * B, B), :], g_sem.at[a, b]))
    keeps = []
    for a in range(2):
        for b in range(4):
            stays = row >= 0
            if a == 0:
                stays = stays & (row >= S)
            if b == 0:
                stays = stays & (col >= S)
            keeps.append((stays, pltpu.make_async_copy(
                g32.at[b, pl.ds(a * B, B), :], out.at[a, :, b, :], o_sem.at[a, b])))
    ltile = [pltpu.make_async_copy(lfac.at[a, :, 0, :], lt32.at[a], l_sem.at[a]) for a in range(2)]
    mload = pltpu.make_async_copy(tile_mask, mask, m_sem)
    dload = pltpu.make_async_copy(dinv, dv, d_sem)

    @pl.when(col < S)
    def _():
        mload.start()
        for copy in ltile:
            copy.start()
    for copy in loads:
        copy.start()
    dload.start()

    barrier = pltpu.get_barrier_semaphore()

    def greet(where):
        pl.semaphore_signal(barrier, inc=1, device_id=where, device_id_type=MESH)

    for step in range(1, 16):
        greet(at(r=(row + step) % 16))
    for c in (c_x, c_y, c_o):
        greet(at(c=c))
    greet(at(r=r_y2, c=c_y))

    def b_source(a, q):
        return yh * 8 + q * 2 + a, row % 8

    def b_other(a, q):
        sr, sc = b_source(a, q)
        return jnp.logical_not((sr == row) & (sc == col))

    for a in range(2):
        for q in range(4):
            sr, sc = b_source(a, q)

            @pl.when((col < S) & b_other(a, q))
            def _():
                greet(at(r=sr, c=sc))

    @pl.when(col < S)
    def _():
        mload.wait()
        for a in range(2):
            ltile[a].wait()
            live = mask[row + 16 * a, col] * (row + 16 * a > col).astype(jnp.int32)
            pn[col, pl.ds(a * B, B), :] = lt32[a] * live.astype(F32)

    pl.semaphore_wait(barrier, 19 + 4 - jnp.where((row == b_row) & (col < S), 1, 0))

    near = jnp.where((x == 0) | (x == 3), 0, 1)
    k_p, k_s = 2 * near + yl, 2 * (1 - near) + yl
    k_pd, k_sd = 2 * near + 1 - yl, 2 * (1 - near) + 1 - yl

    def quarter(k, ch, ssem, rsem, where):
        part = pn.at[k, pl.ds(128 * ch, 128), :]
        return remote(part, part, ssem, rsem, where)

    source, inner = x < 2, x >= 2
    always = row >= 0
    to_x, to_y, to_o = at(c=c_x), at(c=c_y), at(c=c_o)

    def out_recv(ch):
        quarter(k_p, ch, s_out.at[ch], r_out.at[ch], to_o).wait_recv()

    def x_recv(ch):
        quarter(k_s, ch, s_x.at[ch], r_x.at[ch], to_x).wait_recv()

    def y_recv(ch):
        quarter(k_pd, ch, s_y.at[ch], r_y.at[ch], to_y).wait_recv()

    def xd_recv(ch):
        quarter(k_sd, ch, s_x.at[4 + ch // 2], r_x.at[4 + ch // 2], to_x).wait_recv()

    def yd_recv(ch):
        quarter(k_sd, ch, s_y.at[4 + ch], r_y.at[4 + ch], to_y).wait_recv()

    def l_copy(u, slot, where):
        return remote(lt.at[u], lt.at[u], s_l.at[u, slot], r_l.at[u], where)

    def l_wait(u):
        l_copy(u, 0, at(r=r_core)).wait_recv()

    place = row % 8

    def l_routes(u, j):
        ahead, behind = {1: ((1, 3), (1,)), 2: ((2,), (2, 0)), 3: ((3, 5), (3,))}[j]
        plus = (place == ahead[0]) | (place == ahead[-1])
        minus = (place == behind[0]) | (place == behind[-1])
        return [(always, l_copy(u, 0, at(r=r_core))), (row == j, l_copy(u, 1, at(r=r_y2, c=c_y))),
                (plus, l_copy(u, 2, at(r=r_zp))), (minus, l_copy(u, 3, at(r=r_zm)))]

    def l_step(k, mine, rows=(2, 3, 1)):
        for j in rows:
            u = (j * (j - 1)) // 2 + k
            here = (core == CORE_OF[j]) & (k < j)

            @pl.when(here & (row == j) if mine is None else here & (row != j) & mine)
            def _():
                if mine is None:
                    lt[u] = pn[k, pl.ds(0, B), :]
                else:
                    l_wait(u)
                for cond, copy in l_routes(u, j):
                    @pl.when(cond)
                    def _():
                        copy.start()

    l_order = [jnp.where(yh == 0, a, b) for a, b in ((k_p, k_pd), (k_pd, k_p), (k_s, k_sd), (k_sd, k_s))]
    early, later, last = z == 1, (z == 0) | (z == 2), z == 3

    def p_out(ch):
        quarter(k_p, ch, s_out.at[ch], r_out.at[ch], to_o).start()

    def p_x(ch):
        quarter(k_p, ch, s_x.at[ch], r_x.at[ch], to_x).start()

    def p_y(ch):
        quarter(k_p, ch, s_y.at[ch], r_y.at[ch], to_y).start()

    def e_out(ch):
        quarter(k_pd, ch, s_out.at[3 + ch], r_out.at[3 + ch], to_o).start()

    def d_x(ch):
        quarter(k_pd, ch, s_x.at[4 + ch // 2], r_x.at[4 + ch // 2], to_x).start()

    def d_y(ch):
        quarter(k_s, ch, s_y.at[4 + ch], r_y.at[4 + ch], to_y).start()

    @pl.when(source)
    def _():
        for ch in range(3):
            p_out(ch)
            p_y(ch)
        p_x(0)
        p_x(1)
        l_step(k_p, None)

    for a in range(2):
        for b in range(4):
            loads[a * 4 + b].wait()
            cond, copy = keeps[a * 4 + b]

            @pl.when(cond)
            def _():
                copy.start()
    for b in range(4):
        for a in range(2):
            hi, lo = split(g32[b, pl.ds(a * B, B), :].T)
            gth[b, :, pl.ds(a * B, B)] = hi
            gtl[b, :, pl.ds(a * B, B)] = lo

    zero = jnp.where(row < S, 0.0, 1.0).astype(F32)

    def core_copy(k):
        lanes = pl.ds(pl.multiple_of(k * B, B), B)
        return remote(ut.at[pl.ds(2 - 2 * core, 2), :, :, lanes], cr.at[:, :, :, lanes], s_c.at[k], r_c.at[k], at(r=r_core))

    def products(k):
        for a in range(2):
            rows = pl.ds(a * B, B)
            hi, lo = split(pn[k, rows, :] * zero if a == 0 else pn[k, rows, :])
            pbh[k, rows, :] = hi
            pbl[k, rows, :] = lo

        @pl.loop(0, 4)
        def _(step):
            t = lax.rem(2 - 2 * core + step, 4)
            value = dot3((gth[t], gtl[t]), (pbh[k], pbl[k]))
            for q in range(4):
                ut[t, q, :, pl.ds(pl.multiple_of(k * B, B), B)] = value[q * 64:(q + 1) * 64]
        core_copy(k).start()

    @pl.when(source)
    def _():
        products(k_p)
        y_recv(0)
        d_x(0)
        p_x(2)
        p_out(3)
        y_recv(1)
        e_out(1)
        p_x(3)
        x_recv(0)
        x_recv(1)
        d_y(1)
        p_y(3)
        l_step(k_pd, None)
        l_step(k_s, None)
        y_recv(2)
        d_x(2)
        e_out(2)
        xd_recv(0)
        yd_recv(1)
        l_step(k_sd, None)

    @pl.when(inner)
    def _():
        out_recv(0)
        p_x(0)
        p_y(0)
        out_recv(1)
        p_x(1)
        l_step(k_p, None)
        x_recv(0)
        d_y(0)
        out_recv(2)
        p_x(2)
        x_recv(1)
        d_y(1)
        l_step(k_s, None)
        out_recv(3)
        p_x(3)
        products(k_p)
    l_step(l_order[0], early, (2, 3))

    @pl.when(source)
    def _():
        y_recv(3)
        e_out(3)
        x_recv(2)
        x_recv(3)
        d_y(3)

    @pl.when(inner)
    def _():
        x_recv(2)
        d_y(2)
        y_recv(0)
        quarter(k_pd, 1, s_out.at[4], r_out.at[4], to_o).wait_recv()
        l_step(k_pd, None)
        yd_recv(0)
        yd_recv(1)
        l_step(k_sd, None)
        x_recv(3)
        d_y(3)
    products(k_s)
    l_step(l_order[1], early, (2, 3))
    l_step(l_order[2], early, (2, 3))
    l_step(l_order[0], later, (2, 3))

    @pl.when(inner)
    def _():
        for ch in (2, 3):
            quarter(k_pd, ch, s_out.at[3 + ch], r_out.at[3 + ch], to_o).wait_recv()
    products(k_pd)

    @pl.when(source)
    def _():
        xd_recv(2)

    @pl.when(inner)
    def _():
        yd_recv(2)
    yd_recv(3)
    products(k_sd)
    l_step(l_order[3], early, (2, 3))
    l_step(l_order[1], later, (2, 3))
    l_step(0, row == 9, (1,))

    top, end = pl.ds(0, TOP), pl.ds(TOP, LATE)
    low_half, high_half = pl.ds(TOP, HALF), pl.ds(TOP + HALF, HALF)
    q_op, q_rm, q_rp = (z + 2) % 4, (z + 1) % 4, (z + 3) % 4
    away = 1 - yh
    t_away = 2 * core + away

    def unit(q, u):
        return ut.at[2 * core + u, q, top, :]

    c_op = remote(unit(q_op, 0), op, s_zo.at[0], r_zo.at[0], at(r=r_zp))
    c_om = remote(unit(q_op, 1), om, s_zo.at[1], r_zo.at[1], at(r=r_zm))
    c_rm = [remote(unit(q_rm, u), rm.at[u], s_zr.at[0, u], r_zr.at[0, u], at(r=r_zp)) for u in range(2)]
    c_rp = [remote(unit(q_rp, u), rp.at[u], s_zr.at[1, u], r_zr.at[1, u], at(r=r_zm)) for u in range(2)]
    c_yh = remote(unit(z, away), yr, s_yh, r_yh, at(r=r_y2))

    def y_copy(q):
        return remote(ut.at[t_away, q, end, :], yq.at[q], s_yq.at[q], r_yq.at[q], at(r=r_y2))

    def y_add(q):
        y_copy(q).wait_recv()
        ut[t_own, q, end, :] = ut[t_own, q, end, :] + yq[q]

    e_op = remote(ut.at[t_own, q_op, low_half, :], op1, s_eo.at[0], r_eo.at[0], at(r=r_zp))
    e_om = remote(ut.at[t_own, q_op, high_half, :], om1, s_eo.at[1], r_eo.at[1], at(r=r_zm))
    e_rm = [remote(ut.at[t_own, q_rm, part, :], rm1.at[n], s_er.at[0, n], r_er.at[0, n], at(r=r_zp))
            for n, part in enumerate((low_half, high_half))]
    e_rp = [remote(ut.at[t_own, q_rp, part, :], rp1.at[n], s_er.at[1, n], r_er.at[1, n], at(r=r_zm))
            for n, part in enumerate((low_half, high_half))]

    def core_add(q):
        for u in range(2):
            ut[2 * core + u, q] = ut[2 * core + u, q] + cr[u, q]

    for k in range(S):
        core_copy(k).wait_recv()
    core_add(q_op)
    y_copy(q_op).start()
    c_op.start()
    c_om.start()
    core_add(q_rm)
    c_rm[1].start()
    y_copy(q_rm).start()
    core_add(q_rp)
    c_rp[0].start()
    y_copy(q_rp).start()
    core_add(z)
    y_copy(z).start()
    l_step(l_order[2], later, (2, 3))
    c_op.wait_recv()
    ut[2 * core, q_rm, top, :] = ut[2 * core, q_rm, top, :] + op[...]
    c_rm[0].start()
    c_om.wait_recv()
    ut[2 * core + 1, q_rp, top, :] = ut[2 * core + 1, q_rp, top, :] + om[...]
    c_rp[1].start()
    y_add(q_op)
    e_op.start()
    e_om.start()
    y_add(q_rm)
    e_rm[1].start()
    y_add(q_rp)
    e_rp[0].start()
    l_step(l_order[3], later, (2, 3))
    l_step(0, place == 3, (1,))
    e_op.wait_recv()
    ut[t_own, q_rm, low_half, :] = ut[t_own, q_rm, low_half, :] + op1[...]
    e_rm[0].start()
    e_om.wait_recv()
    ut[t_own, q_rp, high_half, :] = ut[t_own, q_rp, high_half, :] + om1[...]
    e_rp[1].start()
    for u in range(2):
        c_rm[u].wait_recv()
        c_rp[u].wait_recv()
    ut[t_away, z, top, :] = ut[t_away, z, top, :] + (rm[away] + rp[away])
    c_yh.start()
    for n in range(4):
        l_step(l_order[n], last, (2, 3))
    l_step(0, (row != 9) & (place != 3), (1,))

    y_add(z)
    for n in range(2):
        e_rm[n].wait_recv()
        e_rp[n].wait_recv()
    sums[end, :] = ut[t_own, z, end, :] + jnp.concatenate([rm1[n] + rp1[n] for n in range(2)], axis=0)
    c_yh.wait_recv()
    sums[top, :] = ut[t_own, z, top, :] + (rm[yh] + rp[yh] + yr[...])

    for u, (j, k) in enumerate(LOW):
        @pl.when(core != CORE_OF[j])
        def _():
            l_wait(u)

    def low(j, k):
        return lbh[LOW.index((j, k))], lbl[LOW.index((j, k))]

    for m, k in [(1, 0), (2, 1), (3, 2), (2, 0), (3, 1), (3, 0)]:
        u = LOW.index((m, k))
        acc = lt[u]
        for j in range(k + 1, m):
            acc = acc + dot3(split(lt[LOW.index((m, j))]), low(j, k))
        mt[m, k] = -acc
        hi, lo = split(-acc)
        lbh[u] = hi
        lbl[u] = lo

    parts = [split(sums[:, pl.ds(k * B, B)]) for k in range(S)]
    c_xa = [remote(xt.at[k], xa.at[t_own, q_own, :], s_xa.at[k], r_xa.at[t_own, z], at(r=k)) for k in range(S)]
    c_xb = [remote(xt.at[k], xb.at[core, q_own, :], s_xb.at[k], r_xb.at[core, z], at(r=b_row, c=k)) for k in range(S)]

    def b_self(k):
        return (row == b_row) & (col == k)

    for k in (3, 2, 1, 0):
        acc = sums[:, pl.ds(k * B, B)]
        for j in range(k + 1, S):
            acc = acc + dot3(parts[j], low(j, k))
        xt[k] = -acc

        @pl.when(jnp.logical_not(b_self(k)))
        def _():
            c_xb[k].start()

        @pl.when(b_self(k))
        def _():
            xb[core, q_own, :] = xt[k]
    for k in range(S):
        @pl.when(row != k)
        def _():
            c_xa[k].start()

        @pl.when(row == k)
        def _():
            xa[t_own, q_own, :] = xt[k]

    @pl.when(col < S)
    def _():
        for k in range(S):
            acc = jnp.concatenate([pn[k, pl.ds(0, B), :] * zero, pn[k, pl.ds(B, B), :]], axis=0)
            for j in range(k + 1, S):
                acc = acc + dot3((pbh[j], pbl[j]), low(j, k))
            hi, lo = split(acc.T)
            ph[k] = hi
            plo[k] = lo

    dload.wait()

    @pl.when((row < S) & (col < S))
    def _():
        ones = (lax.broadcasted_iota(jnp.int32, (B, B), 0) == lax.broadcasted_iota(jnp.int32, (B, B), 1))
        for m in range(S):
            mt[m, m] = ones.astype(F32)
            for k in range(m + 1, S):
                mt[m, k] = jnp.zeros((B, B), F32)
        zo[...] = jnp.zeros((B, B), F32)
        for m in range(S):
            part = dot3(split(dv[m]), split(mt[m, col]))
            zo[...] = zo[...] + dot3(split(mt[m, row].T), split(part))

    c_zc = [remote(zp.at[1 - core, m], zc.at[m], s_zc.at[m], r_zc.at[m], at(r=r_core)) for m in range(2)]
    c_zd = [[remote(zp.at[core, m, pl.ds(((quad + d) % 8) * 32, 32), :], zr.at[d - 1, m], s_zd.at[d - 1, m],
                    r_zd.at[d - 1, m], at(r=((quad + d) % 8) * 2 + core)) for d in range(1, 8)] for m in range(2)]
    c_zf = [remote(zs.at[m], zf.at[pl.ds(quad * 32, 32), :], s_zf.at[m], r_zf.at[quad], at(r=2 * m + core))
            for m in range(2)]

    w_row = [pltpu.make_async_copy(xat.at[t], out.at[0, :, t, :], w_sem.at[t]) for t in range(4)]
    w_col = [pltpu.make_async_copy(xb.at[a], out.at[a, :, 0, :], w_sem.at[4 + a]) for a in range(2)]
    w_dia = pltpu.make_async_copy(zo, out.at[0, :, 0, :], w_sem.at[6])
    rows_new = [((row < S) & (col >= S), w_row[0])] + [(row < S, w_row[t]) for t in range(1, 4)]
    cols_new = [((col < S) & (row >= S), w_col[0]), (col < S, w_col[1])]
    writes = rows_new + cols_new + [((row < S) & (col < S), w_dia)]

    def diagonal(side, m):
        zp[side, m] = dot3((ph[2 * m + side], plo[2 * m + side]), (xh[...], xl[...]))

    @pl.when(col < S)
    def _():
        for a in range(2):
            for q in range(4):
                @pl.when(b_other(a, q))
                def _():
                    remote(xt.at[0], xb.at[a, pl.ds(64 * q, 64), :], s_xb.at[0], r_xb.at[a, q], at(r=b_row)).wait_recv()
            hi, lo = split(xb[a])
            xh[pl.ds(a * B, B), :] = hi
            xl[pl.ds(a * B, B), :] = lo
        for m in range(2):
            diagonal(1 - core, m)
            c_zc[m].start()
        for m in range(2):
            diagonal(core, m)
            c_zc[m].wait_recv()
            zp[core, m] = zp[core, m] + zc[m]
            for copy in c_zd[m]:
                copy.start()
        for cond, copy in cols_new:
            @pl.when(cond)
            def _():
                copy.start()
        for m in range(2):
            acc = zp[core, m, pl.ds(quad * 32, 32), :]
            for d in range(7):
                c_zd[m][d].wait_recv()
                acc = acc + zr[d, m]
            zs[m] = acc

            @pl.when(quad != m)
            def _():
                c_zf[m].start()

            @pl.when(quad == m)
            def _():
                zf[pl.ds(quad * 32, 32), :] = zs[m]

    @pl.when(row < S)
    def _():
        for t in range(4):
            for q in range(4):
                @pl.when(row != (t % 2) * 8 + q * 2 + t // 2)
                def _():
                    remote(xt.at[0], xa.at[t, pl.ds(64 * q, 64), :], s_xa.at[0], r_xa.at[t, q], at(r=r_core)).wait_recv()
            xat[t] = xa[t].T
        for cond, copy in rows_new:
            @pl.when(cond)
            def _():
                copy.start()

    @pl.when((row < S) & (col < S))
    def _():
        for q in range(8):
            @pl.when(quad != q)
            def _():
                remote(zs.at[0], zf.at[pl.ds(q * 32, 32), :], s_zf.at[0], r_zf.at[q], at(r=r_core)).wait_recv()
        zo[...] = zo[...] - zf[...]
        w_dia.start()

    @pl.when(source)
    def _():
        for ch in range(4):
            quarter(k_p, ch, s_out.at[ch], r_out.at[ch], to_o).wait_send()
        for ch in (1, 2, 3):
            quarter(k_pd, ch, s_out.at[3 + ch], r_out.at[3 + ch], to_o).wait_send()
            quarter(k_p, ch, s_y.at[ch], r_y.at[ch], to_y).wait_send()
        for ch in (0, 2):
            quarter(k_pd, ch, s_x.at[4 + ch // 2], r_x.at[4 + ch // 2], to_x).wait_send()

    @pl.when(inner)
    def _():
        for ch in (0, 2):
            quarter(k_s, ch, s_y.at[4 + ch], r_y.at[4 + ch], to_y).wait_send()
    for ch in range(4):
        quarter(k_p, ch, s_x.at[ch], r_x.at[ch], to_x).wait_send()
    quarter(k_p, 0, s_y.at[0], r_y.at[0], to_y).wait_send()
    for ch in (1, 3):
        quarter(k_s, ch, s_y.at[4 + ch], r_y.at[4 + ch], to_y).wait_send()
    for j, k in LOW:
        @pl.when(core == CORE_OF[j])
        def _():
            for cond, copy in l_routes(LOW.index((j, k)), j):
                @pl.when(cond)
                def _():
                    copy.wait_send()
    for copy in [core_copy(k) for k in range(S)] + [y_copy(k) for k in range(4)] + [c_op, c_om, c_yh, e_op, e_om]:
        copy.wait_send()
    for copy in c_rm + c_rp + e_rm + e_rp:
        copy.wait_send()

    for k in range(S):
        @pl.when(jnp.logical_not(b_self(k)))
        def _():
            c_xb[k].wait_send()

        @pl.when(row != k)
        def _():
            c_xa[k].wait_send()

    @pl.when(col < S)
    def _():
        for copy in c_zc + c_zd[0] + c_zd[1]:
            copy.wait_send()
        for m in range(2):
            @pl.when(quad != m)
            def _():
                c_zf[m].wait_send()
    for cond, copy in writes + keeps:
        @pl.when(cond)
        def _():
            copy.wait()


def body(prior, lfac, tile_mask, dinv):
    def vmem(*shape, kind=F32):
        return pltpu.VMEM(shape, kind)

    dma = pltpu.SemaphoreType.DMA
    wide = S * B
    scratch = [
        vmem(4, 2 * B, B), vmem(4, B, 2 * B, kind=BF16), vmem(4, B, 2 * B, kind=BF16),
        vmem(2, B, B), vmem(4, 2 * B, B), vmem(4, 2 * B, B, kind=BF16), vmem(4, 2 * B, B, kind=BF16),
        vmem(4, B, 2 * B, kind=BF16), vmem(4, B, 2 * B, kind=BF16),
        vmem(6, B, B), vmem(6, B, B, kind=BF16), vmem(6, B, B, kind=BF16),
        vmem(4, 4, 64, wide), vmem(2, 4, 64, wide),
        vmem(TOP, wide), vmem(TOP, wide), vmem(2, TOP, wide), vmem(2, TOP, wide), vmem(TOP, wide),
        vmem(4, LATE, wide), vmem(HALF, wide), vmem(HALF, wide), vmem(2, HALF, wide), vmem(2, HALF, wide),
        vmem(64, wide),
        vmem(4, 64, B), vmem(4, B, B), vmem(2, B, B), vmem(4, B, B),
        vmem(2 * B, B, kind=BF16), vmem(2 * B, B, kind=BF16),
        vmem(2, 2, B, B), vmem(2, B, B), vmem(7, 2, 32, B), vmem(2, 32, B), vmem(B, B),
        vmem(4, 4, B, B), vmem(4, B, B), vmem(B, B), pltpu.SMEM((32, 32), jnp.int32), dma,
        dma((2, 4)), dma((2,)), dma, dma((2, 4)), dma((7,)),
        dma((7,)), dma((7,)), dma((6,)), dma((6,)), dma((8,)), dma((8,)),
        dma((6, 4)), dma((6,)), dma((4,)), dma((4,)),
        dma((2,)), dma((2,)), dma((2, 2)), dma((2, 2)), dma, dma,
        dma((4,)), dma((4,)), dma((2,)), dma((2,)), dma((2, 2)), dma((2, 2)),
        dma((4,)), dma((4, 4)), dma((4,)), dma((2, 4)),
        dma((2,)), dma((2,)), dma((7, 2)), dma((7, 2)), dma((2,)), dma((8,)),
    ]
    return pl.pallas_call(
        kernel,
        out_shape=jax.ShapeDtypeStruct(prior.shape, F32),
        in_specs=[pl.BlockSpec(memory_space=pl.ANY), pl.BlockSpec(memory_space=pl.ANY),
                  pl.BlockSpec(memory_space=pl.ANY), pl.BlockSpec(memory_space=pl.ANY)],
        out_specs=pl.BlockSpec(memory_space=pl.ANY),
        scratch_shapes=scratch,
        compiler_params=pltpu.CompilerParams(
            collective_id=0, has_side_effects=True, vmem_limit_bytes=56 * 1024 * 1024),
    )(prior, lfac, tile_mask, dinv)


def solution(mesh):
    placed = (P("prow", None, "pcol", None), P("prow", None, "pcol", None), P(), P())
    return jax.shard_map(
        body, mesh=mesh, in_specs=placed, out_specs=P("prow", None, "pcol", None), check_vma=False
    )
```
